32 devices in a mesh: dp: 8 (over z, core), tensor: 4 (over y, x).
Axes of the slice: x: 2, y: 2, z: 4, core: 2. Of those that a mesh axis runs over, the one named last changes fastest.
Arguments:
- inputs: bfloat16 [16384, 2048], P(('dp', 'tensor')), may hold values from -6 to 6
- input_projection_weight: float32 [2048, 8, 512], P('dp', 'tensor'), may hold values from -0.125 to 0.125
- input_first_moment: float32 [2048, 8, 512], P('dp', 'tensor'), may hold values from -320 to 320
- input_second_moment: float32 [2048, 8, 512], P('dp', 'tensor'), may hold values from 1064.96 to 16384
- out_weight: float32 [2048, 2048], P('tensor', 'dp'), may hold values from -0.375 to 0.375
- out_mean: float32 [2048, 2048], P('tensor', 'dp'), may hold values from -320 to 320
- out_square: float32 [2048, 2048], P('tensor', 'dp'), may hold values from 1064.96 to 16384
- swiglu_weight: float32 [2048, 2, 6144], P('dp', None, 'tensor'), may hold values from -0.125 to 0.125
- swiglu_mean: float32 [2048, 2, 6144], P('dp', None, 'tensor'), may hold values from -320 to 320
- swiglu_square: float32 [2048, 2, 6144], P('dp', None, 'tensor'), may hold values from 1064.96 to 16384
- down_weight: float32 [6144, 2048], P('tensor', 'dp'), may hold values from -0.078125 to 0.078125
- down_mean: float32 [6144, 2048], P('tensor', 'dp'), may hold values from -448 to 448
- down_square: float32 [6144, 2048], P('tensor', 'dp'), may hold values from 2457.6 to 39321.6
- norm_gains: float32 [2, 2048], replicated, may hold values from 0.5 to 1.5
- norm_mean: float32 [2, 2048], replicated, may hold values from -512 to 512
- norm_square: float32 [2, 2048], replicated, may hold values from 3276.8 to 52428.8
- qknorm_gains: float32 [2, 128], replicated, may hold values from 0.5 to 1.5
- qknorm_mean: float32 [2, 128], replicated, may hold values from -896 to 896
- qknorm_square: float32 [2, 128], replicated, may hold values from 9699.328 to 157286.4
- cotangent: bfloat16 [16384, 2048], P(('dp', 'tensor')), may hold values from -8 to 8
Outputs:
- outputs: bfloat16 [16384, 2048], P(('dp', 'tensor'))
- input_grad: bfloat16 [16384, 2048], P(('dp', 'tensor'))
- in_grad: float32 [2048, 8, 512], P('dp', 'tensor')
- in_new: float32 [2048, 8, 512], P('dp', 'tensor')
- in_second: float32 [2048, 8, 512], P('dp', 'tensor')
- out_grad: float32 [2048, 2048], P('tensor', 'dp')
- out_new: float32 [2048, 2048], P('tensor', 'dp')
- out_second: float32 [2048, 2048], P('tensor', 'dp')
- swiglu_grad: float32 [2048, 2, 6144], P('dp', None, 'tensor')
- swiglu_new: float32 [2048, 2, 6144], P('dp', None, 'tensor')
- swiglu_second: float32 [2048, 2, 6144], P('dp', None, 'tensor')
- down_grad: float32 [6144, 2048], P('tensor', 'dp')
- down_new: float32 [6144, 2048], P('tensor', 'dp')
- down_second: float32 [6144, 2048], P('tensor', 'dp')
- norm_grad: float32 [2, 2048], replicated
- norm_new: float32 [2, 2048], replicated
- norm_second: float32 [2, 2048], replicated
- qknorm_grad: float32 [2, 128], replicated
- qknorm_new: float32 [2, 128], replicated
- qknorm_second: float32 [2, 128], replicated
The draws below stay inside these ranges and needn't reach their ends.
All inputs are finite; a program needn't handle non-finite values.
Results may differ from the reference program's by a relative error of at most 0.015.
Values may be sent and summed in bfloat16 or wider, within the bound.
No kernel may reach another device: no remote copies, remote signals or barrier semaphores. Data moves between devices by JAX's collectives and lax.ppermute only.
A program may use at most 320 MiB of HBM per device.

```python
import math
import jax
import jax.numpy as jnp
from jax import lax

MODEL_WIDTH = 2048
HQ = 16
KEY_HEADS = 8
HEAD_WIDTH = 128
FF = 6144
QUERY_PER_KEY = 2
SEQUENCE_TOKENS = 2048
TOKEN_COUNT = 16384


def draw_cotangent(key, part):
    row_share = jnp.arange(TOKEN_COUNT, dtype=jnp.int32).astype(jnp.float32) / TOKEN_COUNT
    base_draw = jnp.clip(jax.random.normal(key, (TOKEN_COUNT, MODEL_WIDTH), jnp.float32), -5.0, 5.0)
    ramp_scale = 0.5 + row_share
    return (base_draw * ramp_scale[:, None]).astype(jnp.bfloat16)


def shard_levels(own_key, shape, cuts, low, high):
    factor_of = 1.0
    for dim, blocks in cuts:
        draws = jax.random.uniform(jax.random.fold_in(jax.random.fold_in(own_key, 6), dim), (blocks,), jnp.float32, low / len(cuts), high / len(cuts))
        factor_of = factor_of * jnp.repeat(jnp.exp(draws), shape[dim] // blocks).reshape((-1,) + (1,) * (len(shape) - 1 - dim))
    return factor_of


def scatter_about(rng, dims, spread, bound, pieces=(), kind=jnp.bfloat16):
    array = spread * jax.random.normal(rng, dims, jnp.float32)
    if pieces:
        array = array * shard_levels(rng, dims, pieces, -0.22, 0.18)
    return jnp.clip(array, -bound, bound).astype(kind)


def setup_inputs(seed: int = 0) -> dict:
    key_of = jax.random.split(jax.random.key(seed), 21)
    inputs = scatter_about(key_of[0], (TOKEN_COUNT, MODEL_WIDTH), 1.0, 6.0, ((0, 32),))
    input_projection_weight = scatter_about(key_of[1], (MODEL_WIDTH, KEY_HEADS, (QUERY_PER_KEY + 2) * HEAD_WIDTH), MODEL_WIDTH ** -0.5, 0.125, ((0, 8), (1, 4)), jnp.float32)
    input_first_moment = scatter_about(key_of[2], (MODEL_WIDTH, KEY_HEADS, (QUERY_PER_KEY + 2) * HEAD_WIDTH), (0.4 * TOKEN_COUNT ** 0.5), 320.0, ((0, 8), (1, 4)), jnp.float32)
    input_second_moment = jnp.clip(jnp.exp(math.log(16384.0) - 2.73336805 * jax.random.uniform(key_of[3], (MODEL_WIDTH, KEY_HEADS, (QUERY_PER_KEY + 2) * HEAD_WIDTH), jnp.float32) ** shard_levels(key_of[3], (MODEL_WIDTH, KEY_HEADS, (QUERY_PER_KEY + 2) * HEAD_WIDTH), ((0, 8), (1, 4)), -0.2, 0.2)), 1064.96, 16384.0)
    out_weight = scatter_about(key_of[4], (HQ * HEAD_WIDTH, MODEL_WIDTH), (HQ * HEAD_WIDTH // 8) ** -0.5, 0.375, ((0, 4), (1, 8)), jnp.float32)
    out_mean = scatter_about(key_of[5], (HQ * HEAD_WIDTH, MODEL_WIDTH), (0.4 * TOKEN_COUNT ** 0.5), 320.0, ((0, 4), (1, 8)), jnp.float32)
    out_square = jnp.clip(jnp.exp(math.log(16384.0) - 2.73336805 * jax.random.uniform(key_of[6], (HQ * HEAD_WIDTH, MODEL_WIDTH), jnp.float32) ** shard_levels(key_of[6], (HQ * HEAD_WIDTH, MODEL_WIDTH), ((0, 4), (1, 8)), -0.2, 0.2)), 1064.96, 16384.0)
    swiglu_weight = scatter_about(key_of[7], (MODEL_WIDTH, 2, FF), MODEL_WIDTH ** -0.5, 0.125, ((0, 8), (2, 4)), jnp.float32)
    swiglu_mean = scatter_about(key_of[8], (MODEL_WIDTH, 2, FF), (0.4 * TOKEN_COUNT ** 0.5), 320.0, ((0, 8), (2, 4)), jnp.float32)
    swiglu_square = jnp.clip(jnp.exp(math.log(16384.0) - 2.73336805 * jax.random.uniform(key_of[9], (MODEL_WIDTH, 2, FF), jnp.float32) ** shard_levels(key_of[9], (MODEL_WIDTH, 2, FF), ((0, 8), (2, 4)), -0.2, 0.2)), 1064.96, 16384.0)
    down_weight = scatter_about(key_of[10], (FF, MODEL_WIDTH), FF ** -0.5, 0.078125, ((0, 4), (1, 8)), jnp.float32)
    down_mean = scatter_about(key_of[11], (FF, MODEL_WIDTH), (0.6 * TOKEN_COUNT ** 0.5), 448.0, ((0, 4), (1, 8)), jnp.float32)
    down_square = jnp.clip(jnp.exp(math.log(39321.6) - 2.7725887 * jax.random.uniform(key_of[12], (FF, MODEL_WIDTH), jnp.float32) ** shard_levels(key_of[12], (FF, MODEL_WIDTH), ((0, 4), (1, 8)), -0.2, 0.2)), 2457.6, 39321.6)
    norm_gains = jnp.clip(1.0 + 0.1 * jax.random.normal(key_of[13], (2, MODEL_WIDTH), jnp.float32), 0.5, 1.5)
    norm_mean = scatter_about(key_of[14], (2, MODEL_WIDTH), (0.7 * TOKEN_COUNT ** 0.5), 512.0, (), jnp.float32)
    norm_square = jnp.clip(jnp.exp(jax.random.uniform(key_of[15], (2, MODEL_WIDTH), jnp.float32, math.log(3276.8), math.log(52428.8))), 3276.8, 52428.8)
    qknorm_gains = jnp.clip(1.0 + 0.1 * jax.random.normal(key_of[16], (2, HEAD_WIDTH), jnp.float32), 0.5, 1.5)
    qknorm_mean = scatter_about(key_of[17], (2, HEAD_WIDTH), (0.3 * (TOKEN_COUNT * HQ) ** 0.5), 896.0, (), jnp.float32)
    qknorm_square = jnp.clip(jnp.exp(jax.random.uniform(key_of[18], (2, HEAD_WIDTH), jnp.float32, math.log(9699.328), math.log(157286.4))), 9699.328, 157286.4)
    cotangent = draw_cotangent(jax.random.fold_in(key_of[20], 71), 0)
    return dict(inputs=inputs, input_projection_weight=input_projection_weight, input_first_moment=input_first_moment, input_second_moment=input_second_moment, out_weight=out_weight, out_mean=out_mean, out_square=out_square, swiglu_weight=swiglu_weight, swiglu_mean=swiglu_mean, swiglu_square=swiglu_square, down_weight=down_weight, down_mean=down_mean, down_square=down_square, norm_gains=norm_gains, norm_mean=norm_mean, norm_square=norm_square, qknorm_gains=qknorm_gains, qknorm_mean=qknorm_mean, qknorm_square=qknorm_square, cotangent=cotangent)


@jax.custom_vjp
def lowered_forward(v):
    return lax.optimization_barrier(v.astype(jnp.bfloat16)).astype(jnp.float32)

@jax.custom_vjp
def lowered_backward(v):
    return v

def low_keep(v):
    return (lowered_forward(v), None)

def low_pass(kept, grad):
    return (grad,)

def back_keep(v):
    return (v, None)

def back_low(kept, grad):
    return (lowered_forward(grad),)
lowered_forward.defvjp(low_keep, low_pass)
lowered_backward.defvjp(back_keep, back_low)
norm_eps = 1e-06
rope_base = 1000000.0
beta_one = 0.5
beta_two = 0.55
step_count = 5.0
adam_eps = 1e-08
decay_rate = 0.1
gain_rate = 0.3
masked_score = -1e+30

def matrix_product(left, right):
    return jnp.dot(left, right, precision=lax.Precision.HIGHEST, preferred_element_type=jnp.float32)

def rms_gain(values, gain_row):
    return values * lax.rsqrt(lax.optimization_barrier(jnp.mean(values * values, axis=-1, keepdims=True)) + norm_eps) * gain_row

def rotary_tables(row_total, length, width):
    positions = (jnp.arange(row_total, dtype=jnp.int32) % length).astype(jnp.float32)
    frequency = rope_base ** (-2.0 * jnp.arange(width // 2, dtype=jnp.int32).astype(jnp.float32) / width)
    angles = positions[:, None] * frequency[None, :]
    return (jnp.cos(angles), jnp.sin(angles))

def rotate(values, cos_table, sin_table):
    half_width = values.shape[-1] // 2
    table_shape = (cos_table.shape[0],) + (1,) * (values.ndim - 2) + (half_width,)
    cos_rows = cos_table.reshape(table_shape)
    sin_rows = sin_table.reshape(table_shape)
    first_half = values[..., :half_width]
    second_half = values[..., half_width:]
    return jnp.concatenate([first_half * cos_rows - second_half * sin_rows, second_half * cos_rows + first_half * sin_rows], axis=-1)

def layer_forward(inputs, input_projection_weight, out_weight, swiglu_weight, down_weight, norm_gains, qknorm_gains):
    cos_table, sin_table = rotary_tables(SEQUENCE_TOKENS, SEQUENCE_TOKENS, HEAD_WIDTH)
    normalized_rows = lowered_forward(rms_gain(inputs, norm_gains[0]))
    mixed_precision = lowered_backward(matrix_product(normalized_rows, lowered_forward(input_projection_weight).reshape(MODEL_WIDTH, KEY_HEADS * (QUERY_PER_KEY + 2) * HEAD_WIDTH)))
    mixed_precision = mixed_precision.reshape(SEQUENCE_TOKENS, KEY_HEADS, QUERY_PER_KEY + 2, HEAD_WIDTH)
    query_rows = lowered_forward(rotate(rms_gain(mixed_precision[:, :, :QUERY_PER_KEY], qknorm_gains[0]), cos_table, sin_table))
    key_rows = lowered_forward(rotate(rms_gain(mixed_precision[:, :, QUERY_PER_KEY], qknorm_gains[1]), cos_table, sin_table))
    value_rows = lowered_forward(mixed_precision[:, :, QUERY_PER_KEY + 1])
    score_scale = HEAD_WIDTH ** (-0.5)
    block_rows = min(512, SEQUENCE_TOKENS)
    key_pos = jnp.arange(SEQUENCE_TOKENS, dtype=jnp.int32)

    def attend_block(block_start):
        query_block = lax.dynamic_slice_in_dim(query_rows, block_start, block_rows, 0)
        scores = jnp.einsum('qhgd,khd->hgqk', query_block, key_rows, precision=lax.Precision.HIGHEST)
        scores = lowered_backward(scores * score_scale)
        query_pos = block_start + jnp.arange(block_rows, dtype=jnp.int32)
        scores = jnp.where(key_pos[None, :] <= query_pos[:, None], scores, masked_score)
        attention = lowered_forward(jax.nn.softmax(scores, axis=-1))
        return jnp.einsum('hgqk,khd->qhgd', attention, value_rows, precision=lax.Precision.HIGHEST)
    block_starts = jnp.arange(SEQUENCE_TOKENS // block_rows, dtype=jnp.int32) * block_rows
    context = lax.map(jax.checkpoint(attend_block), block_starts).reshape(SEQUENCE_TOKENS, HQ * HEAD_WIDTH)
    context = lowered_forward(lowered_backward(context))
    attended = lowered_backward(matrix_product(context, lowered_forward(out_weight)))
    hidden = inputs + attended
    normed_two = lowered_forward(rms_gain(hidden, norm_gains[1]))
    gate_up = lowered_backward(matrix_product(normed_two, lowered_forward(swiglu_weight).reshape(MODEL_WIDTH, 2 * FF)))
    activated = lowered_forward(jax.nn.silu(gate_up[:, :FF]) * gate_up[:, FF:])
    return hidden + lowered_backward(matrix_product(activated, lowered_forward(down_weight)))

def adamw(weight, gradient, mean_old, square_old, rate):
    mean_new = beta_one * mean_old + (1.0 - beta_one) * gradient
    square_new = beta_two * square_old + (1.0 - beta_two) * gradient * gradient
    mean_hat = mean_new / (1.0 - beta_one ** step_count)
    square_hat = square_new / (1.0 - beta_two ** step_count)
    weight_new = weight - rate * (mean_hat / (jnp.sqrt(square_hat) + adam_eps) + decay_rate * weight)
    return (weight_new, square_new)

def reference(inputs, input_projection_weight, input_first_moment, input_second_moment, out_weight, out_mean, out_square, swiglu_weight, swiglu_mean, swiglu_square, down_weight, down_mean, down_square, norm_gains, norm_mean, norm_square, qknorm_gains, qknorm_mean, qknorm_square, cotangent):
    params = (input_projection_weight, out_weight, swiglu_weight, down_weight, norm_gains, qknorm_gains)
    seq_total = TOKEN_COUNT // SEQUENCE_TOKENS
    rows_in = inputs.astype(jnp.float32).reshape(seq_total, SEQUENCE_TOKENS, MODEL_WIDTH)
    rows_cot = cotangent.astype(jnp.float32).reshape(seq_total, SEQUENCE_TOKENS, MODEL_WIDTH)

    def per_sequence(totals, sequence_pair):
        input_rows, cot_rows = sequence_pair
        output_rows, pullback = jax.vjp(layer_forward, input_rows, *params)
        gradients = pullback(cot_rows)
        summed = tuple((total_part + new_part for total_part, new_part in zip(totals, gradients[1:])))
        return (summed, (output_rows.astype(jnp.bfloat16), gradients[0].astype(jnp.bfloat16)))
    zero_grads = tuple((jnp.zeros(param_one.shape, jnp.float32) for param_one in params))
    grad_sums, (outputs, input_grad) = lax.scan(per_sequence, zero_grads, (rows_in, rows_cot))
    in_grad, out_grad, swiglu_grad, down_grad, norm_grad, qknorm_grad = grad_sums
    in_new, in_second = adamw(input_projection_weight, in_grad, input_first_moment, input_second_moment, MODEL_WIDTH ** (-0.5))
    out_new, out_second = adamw(out_weight, out_grad, out_mean, out_square, (HQ * HEAD_WIDTH / 8.0) ** (-0.5))
    swiglu_new, swiglu_second = adamw(swiglu_weight, swiglu_grad, swiglu_mean, swiglu_square, MODEL_WIDTH ** (-0.5))
    down_new, down_second = adamw(down_weight, down_grad, down_mean, down_square, FF ** (-0.5))
    norm_new, norm_second = adamw(norm_gains, norm_grad, norm_mean, norm_square, gain_rate)
    qknorm_new, qknorm_second = adamw(qknorm_gains, qknorm_grad, qknorm_mean, qknorm_square, gain_rate)
    return (outputs.reshape(TOKEN_COUNT, MODEL_WIDTH), input_grad.reshape(TOKEN_COUNT, MODEL_WIDTH), in_grad, in_new, in_second, out_grad, out_new, out_second, swiglu_grad, swiglu_new, swiglu_second, down_grad, down_new, down_second, norm_grad, norm_new, norm_second, qknorm_grad, qknorm_new, qknorm_second)
```

```python
import jax
import jax.numpy as jnp
from jax import lax
from jax.experimental import pallas as pl
from jax.experimental.pallas import tpu as pltpu
from jax.sharding import PartitionSpec as P

MODEL_WIDTH = 2048
HQ = 16
HEAD_WIDTH = 128
FF = 6144
QUERY_PER_KEY = 2
SEQUENCE_TOKENS = 2048


norm_eps = 1e-06
rope_base = 1000000.0
beta_one = 0.5
beta_two = 0.55
step_count = 5.0
adam_eps = 1e-08
decay_rate = 0.1
gain_rate = 0.3
masked_score = -1e30
log2_e = 1.4426950408889634


def rms_gain(values, gain_row):
    return (
        values * lax.rsqrt(jnp.mean(values * values, axis=-1, keepdims=True) + norm_eps) * gain_row
    )


def rotary_tables(row_total, length, width):
    positions = (jnp.arange(row_total, dtype=jnp.int32) % length).astype(jnp.float32)
    frequency = rope_base ** (
        -2.0 * jnp.arange(width // 2, dtype=jnp.int32).astype(jnp.float32) / width
    )
    angles = positions[:, None] * frequency[None, :]
    return (jnp.cos(angles), jnp.sin(angles))


def rotate(values, cos_table, sin_table):
    half_width = values.shape[-1] // 2
    table_shape = (cos_table.shape[0],) + (1,) * (values.ndim - 2) + (half_width,)
    cos_rows = cos_table.reshape(table_shape)
    sin_rows = sin_table.reshape(table_shape)
    first_half = values[..., :half_width]
    second_half = values[..., half_width:]
    return jnp.concatenate(
        [
            first_half * cos_rows - second_half * sin_rows,
            second_half * cos_rows + first_half * sin_rows,
        ],
        axis=-1,
    )


def contract_rows(left, right):
    return lax.dot_general(
        left, right, (((0,), (0,)), ((), ())), preferred_element_type=jnp.float32
    )


def contract_cols(left, right):
    return lax.dot_general(
        left, right, (((1,), (1,)), ((), ())), preferred_element_type=jnp.float32
    )


def product(left, right):
    return jnp.dot(left, right, preferred_element_type=jnp.float32)


def adamw(weight, gradient, mean_old, square_old, rate):
    mean_new = beta_one * mean_old + (1.0 - beta_one) * gradient
    square_new = beta_two * square_old + (1.0 - beta_two) * gradient * gradient
    mean_hat = mean_new / (1.0 - beta_one**step_count)
    square_hat = square_new / (1.0 - beta_two**step_count)
    weight_new = weight - rate * (
        mean_hat / (jnp.sqrt(square_hat) + adam_eps) + decay_rate * weight
    )
    return (weight_new, square_new)


def ring_place(index, size):
    return jnp.where(index < size // 2, index, size // 2 + size - 1 - index)


def ring_pairs(size):
    half = size // 2
    order = list(range(half)) + list(range(size - 1, half - 1, -1))
    ahead = [(order[r], order[(r + 1) % size]) for r in range(size)]
    return ahead, [(b, a) for a, b in ahead]


def ring_offsets(size):
    offsets = [0]
    for step in range(1, size // 2):
        offsets += [step, -step]
    return offsets + [size // 2]


def ring_gather(rows, size):
    ahead, back = ring_pairs(size)
    half = rows.shape[0] // 2
    slots = [rows]
    from_left = from_right = rows
    for _ in range(1, size // 2):
        from_left, from_right = (
            lax.ppermute(from_left, "tensor", ahead),
            lax.ppermute(from_right, "tensor", back),
        )
        slots += [from_right, from_left]
    low = lax.ppermute(from_left[:half], "tensor", ahead)
    high = lax.ppermute(from_right[half:], "tensor", back)
    return slots + [jnp.concatenate([low, high], axis=0)]


def ring_scatter(parts, size):
    ahead, back = ring_pairs(size)
    far = parts[-1]
    half = far.shape[0] // 2
    going_ahead = lax.ppermute(far[:half], "tensor", ahead)
    going_back = lax.ppermute(far[half:], "tensor", back)
    for step in range(size // 2 - 1, 0, -1):
        to_right, to_left = parts[2 * step - 1], parts[2 * step]
        if step == size // 2 - 1:
            to_right = jnp.concatenate(
                [(to_right[:half] + going_ahead.astype(jnp.float32)), to_right[half:]], axis=0
            )
            to_left = jnp.concatenate(
                [to_left[:half], to_left[half:] + going_back.astype(jnp.float32)], axis=0
            )
        else:
            to_right = to_right + going_ahead.astype(jnp.float32)
            to_left = to_left + going_back.astype(jnp.float32)
        going_ahead = lax.ppermute(to_right.astype(jnp.bfloat16), "tensor", ahead)
        going_back = lax.ppermute(to_left.astype(jnp.bfloat16), "tensor", back)
    if size == 2:
        return parts[0] + jnp.concatenate([going_ahead, going_back], axis=0).astype(jnp.float32)
    return parts[0] + going_ahead.astype(jnp.float32) + going_back.astype(jnp.float32)


def narrow_far(parts):
    return parts[:-1] + [parts[-1].astype(jnp.bfloat16)]


def attend_kernel(scale, query_ref, key_ref, value_ref, out_ref, log_ref):
    block = query_ref.shape[0]
    width = key_ref.shape[1]
    group = query_ref.shape[1] // width
    step = pl.program_id(2)
    below = lax.broadcasted_iota(jnp.int32, (block, block), 0) <= lax.broadcasted_iota(
        jnp.int32, (block, block), 1
    )
    queries = [query_ref[:, g * width : (g + 1) * width] for g in range(group)]

    def visit(start, carry, masked):
        keys = key_ref[pl.ds(start, block), :]
        values = value_ref[pl.ds(start, block), :]
        new = []
        for g in range(group):
            total, acc = carry[g]
            weights = jnp.exp2(contract_cols(keys, queries[g]) * (scale * log2_e))
            if masked:
                weights = jnp.where(below, weights, 0.0)
            total = total + jnp.sum(weights, axis=0, keepdims=True)
            acc = acc + contract_rows(values, weights.astype(jnp.bfloat16))
            new.append((total, acc))
        return tuple(new)

    start_carry = tuple(
        (jnp.zeros((1, block), jnp.float32), jnp.zeros((width, block), jnp.float32))
        for _ in range(group)
    )
    carry = lax.fori_loop(
        0, step, lambda j, c: visit(pl.multiple_of(j * block, block), c, False), start_carry
    )
    carry = visit(pl.multiple_of(step * block, block), carry, True)
    for g in range(group):
        total, acc = carry[g]
        out_ref[:, g * width : (g + 1) * width] = jnp.transpose(acc / total).astype(jnp.bfloat16)
        log_ref[0, 0, g : g + 1, :] = jnp.log2(total)


def attention_forward(query, key, value, block):
    rows = query.shape[0]
    heads = key.shape[1] // HEAD_WIDTH
    steps = SEQUENCE_TOKENS // block
    wide = QUERY_PER_KEY * HEAD_WIDTH
    sequences = rows // SEQUENCE_TOKENS
    area = heads * QUERY_PER_KEY * rows * SEQUENCE_TOKENS // 2
    kernel = lambda *refs: attend_kernel(HEAD_WIDTH ** (-0.5), *refs)
    return pl.pallas_call(
        kernel,
        grid=(heads, sequences, steps),
        in_specs=[
            pl.BlockSpec((block, wide), lambda h, s, i: (s * steps + i, h)),
            pl.BlockSpec((SEQUENCE_TOKENS, HEAD_WIDTH), lambda h, s, i: (s, h)),
            pl.BlockSpec((SEQUENCE_TOKENS, HEAD_WIDTH), lambda h, s, i: (s, h)),
        ],
        out_specs=[
            pl.BlockSpec((block, wide), lambda h, s, i: (s * steps + i, h)),
            pl.BlockSpec(
                (1, 1, QUERY_PER_KEY, block), lambda h, s, i: (h, s * steps + i, 0, 0)
            ),
        ],
        out_shape=[
            jax.ShapeDtypeStruct(query.shape, jnp.bfloat16),
            jax.ShapeDtypeStruct((heads, rows // block, QUERY_PER_KEY, block), jnp.float32),
        ],
        compiler_params=pltpu.CompilerParams(vmem_limit_bytes=48 * 1024 * 1024),
        cost_estimate=pl.CostEstimate(
            flops=8 * area * HEAD_WIDTH, bytes_accessed=8 * rows * wide * heads, transcendentals=area
        ),
        name="attend",
    )(query, key, value)


def attend_back_kernel(
    scale,
    query_ref,
    key_ref,
    value_ref,
    grad_ref,
    context_ref,
    log_ref,
    query_out,
    key_out,
    value_out,
):
    block = query_ref.shape[0]
    width = key_ref.shape[1]
    group = query_ref.shape[1] // width
    step = pl.program_id(2)
    below = lax.broadcasted_iota(jnp.int32, (block, block), 0) <= lax.broadcasted_iota(
        jnp.int32, (block, block), 1
    )

    @pl.when(step == 0)
    def _():
        key_out[...] = jnp.zeros_like(key_out)
        value_out[...] = jnp.zeros_like(value_out)

    queries, grads, logs, dots = [], [], [], []
    for g in range(group):
        cols = slice(g * width, (g + 1) * width)
        queries.append(query_ref[:, cols])
        grads.append(grad_ref[:, cols])
        logs.append(log_ref[0, 0, g : g + 1, :])
        both = grads[g].astype(jnp.float32) * context_ref[:, cols].astype(jnp.float32)
        dots.append(jnp.sum(jnp.transpose(both), axis=0, keepdims=True))

    def visit(start, carry, masked):
        rows = pl.ds(start, block)
        keys = key_ref[rows, :]
        values = value_ref[rows, :]
        new = []
        key_part = value_part = None
        for g in range(group):
            weights = jnp.exp2(contract_cols(keys, queries[g]) * (scale * log2_e) - logs[g])
            if masked:
                weights = jnp.where(below, weights, 0.0)
            slope = contract_cols(values, grads[g])
            score = (weights * (slope - dots[g])).astype(jnp.bfloat16)
            value_g = product(weights.astype(jnp.bfloat16), grads[g])
            key_g = product(score, queries[g])
            key_part = key_g if key_part is None else key_part + key_g
            value_part = value_g if value_part is None else value_part + value_g
            new.append(carry[g] + contract_rows(keys, score))
        key_out[rows, :] += key_part * scale
        value_out[rows, :] += value_part
        return tuple(new)

    carry = tuple(jnp.zeros((width, block), jnp.float32) for _ in range(group))
    carry = lax.fori_loop(
        0, step, lambda j, c: visit(pl.multiple_of(j * block, block), c, False), carry
    )
    carry = visit(pl.multiple_of(step * block, block), carry, True)
    for g in range(group):
        query_out[:, g * width : (g + 1) * width] = jnp.transpose(carry[g]) * scale


def attention_backward(query, key, value, grad, context, logs):
    rows = query.shape[0]
    block = logs.shape[-1]
    heads = key.shape[1] // HEAD_WIDTH
    steps = SEQUENCE_TOKENS // block
    wide = QUERY_PER_KEY * HEAD_WIDTH
    sequences = rows // SEQUENCE_TOKENS
    area = heads * QUERY_PER_KEY * rows * SEQUENCE_TOKENS // 2
    kernel = lambda *refs: attend_back_kernel(HEAD_WIDTH ** (-0.5), *refs)
    query_spec = pl.BlockSpec((block, wide), lambda h, s, i: (s * steps + i, h))
    key_spec = pl.BlockSpec((SEQUENCE_TOKENS, HEAD_WIDTH), lambda h, s, i: (s, h))
    return pl.pallas_call(
        kernel,
        grid=(heads, sequences, steps),
        in_specs=[
            query_spec,
            key_spec,
            key_spec,
            query_spec,
            query_spec,
            pl.BlockSpec((1, 1, QUERY_PER_KEY, block), lambda h, s, i: (h, s * steps + i, 0, 0)),
        ],
        out_specs=[query_spec, key_spec, key_spec],
        out_shape=[
            jax.ShapeDtypeStruct(query.shape, jnp.float32),
            jax.ShapeDtypeStruct(key.shape, jnp.float32),
            jax.ShapeDtypeStruct(key.shape, jnp.float32),
        ],
        compiler_params=pltpu.CompilerParams(vmem_limit_bytes=48 * 1024 * 1024),
        cost_estimate=pl.CostEstimate(
            flops=20 * area * HEAD_WIDTH,
            bytes_accessed=16 * rows * wide * heads,
            transcendentals=area,
        ),
        name="attend_back",
    )(query, key, value, grad, context, logs)


def pick(rows, place, block):
    return lax.dynamic_slice_in_dim(rows, place * block, block, 0)


def local(
    inputs,
    input_projection_weight,
    input_first_moment,
    input_second_moment,
    out_weight,
    out_mean,
    out_square,
    swiglu_weight,
    swiglu_mean,
    swiglu_square,
    down_weight,
    down_mean,
    down_square,
    norm_gains,
    norm_mean,
    norm_square,
    qknorm_gains,
    qknorm_mean,
    qknorm_square,
    cotangent,
):
    size = lax.axis_size("tensor")
    rows = inputs.shape[0]
    group_rows = rows * size
    dp_rows = input_projection_weight.shape[0]
    local_kv = input_projection_weight.shape[1]
    local_ff = swiglu_weight.shape[2]
    wide = QUERY_PER_KEY * HEAD_WIDTH
    offsets = ring_offsets(size)
    me = ring_place(lax.axis_index("tensor"), size)
    places = [ring_place((me + d + size) % size, size) for d in offsets]
    barrier = lax.optimization_barrier

    in_low = input_projection_weight.astype(jnp.bfloat16).reshape(dp_rows, -1)
    out_low = out_weight.astype(jnp.bfloat16)
    swiglu_low = swiglu_weight.astype(jnp.bfloat16).reshape(dp_rows, 2 * local_ff)
    down_low = down_weight.astype(jnp.bfloat16)
    in_matrix = lax.all_gather(in_low, "dp", axis=0, tiled=True)
    out_full = lax.all_gather(out_low, "dp", axis=1, tiled=True)
    swiglu_matrix = lax.all_gather(swiglu_low, "dp", axis=0, tiled=True)
    down_full = lax.all_gather(down_low, "dp", axis=1, tiled=True)

    inputs_f = inputs.astype(jnp.float32)
    normed_f, norm_one_back = jax.vjp(rms_gain, inputs_f, norm_gains[0])
    normed_slots = ring_gather(normed_f.astype(jnp.bfloat16), size)
    cotangent_sent, _ = barrier((cotangent, normed_slots[-1]))
    cot_slots = ring_gather(cotangent_sent, size)

    mixed = jnp.zeros((group_rows, in_matrix.shape[1]), jnp.float32)
    for place, slot in zip(places, normed_slots):
        mixed = lax.dynamic_update_slice_in_dim(
            mixed, product(slot, in_matrix), place * rows, 0
        )
    mixed = mixed.reshape(group_rows, local_kv, QUERY_PER_KEY + 2, HEAD_WIDTH)
    cos_table, sin_table = rotary_tables(group_rows, SEQUENCE_TOKENS, HEAD_WIDTH)

    def rotate_both(query_in, key_in, gains_in):
        return (
            rotate(rms_gain(query_in, gains_in[0]), cos_table, sin_table),
            rotate(rms_gain(key_in, gains_in[1]), cos_table, sin_table),
        )

    (query_rot, key_rot), rotate_back = jax.vjp(
        rotate_both, mixed[:, :, :QUERY_PER_KEY], mixed[:, :, QUERY_PER_KEY], qknorm_gains
    )
    query = query_rot.astype(jnp.bfloat16).reshape(group_rows, local_kv * wide)
    key = key_rot.astype(jnp.bfloat16).reshape(group_rows, local_kv * HEAD_WIDTH)
    value = mixed[:, :, QUERY_PER_KEY + 1].astype(jnp.bfloat16)
    value = value.reshape(group_rows, local_kv * HEAD_WIDTH)
    context, logs = attention_forward(query, key, value, 512)

    attended = ring_scatter(
        narrow_far([product(pick(context, place, rows), out_full) for place in places]), size
    )
    hidden = inputs_f + attended
    normed_two_f, norm_two_back = jax.vjp(rms_gain, hidden, norm_gains[1])
    two_slots = ring_gather(normed_two_f.astype(jnp.bfloat16), size)

    activated_slots, gate_up_slots = [], []
    for two, cot in zip(two_slots, cot_slots):
        gate_up = product(two, swiglu_matrix)
        gate_part, up_part = gate_up[:, :local_ff], gate_up[:, local_ff:]
        sigmoid_gate = jax.nn.sigmoid(gate_part)
        activated_slots.append((gate_part * sigmoid_gate * up_part).astype(jnp.bfloat16))
        activated_grad = contract_cols(cot, down_full)
        gate_grad = (
            activated_grad * up_part * sigmoid_gate * (1.0 + gate_part * (1.0 - sigmoid_gate))
        )
        up_grad = activated_grad * gate_part * sigmoid_gate
        gate_up_slots.append(
            jnp.concatenate([gate_grad, up_grad], axis=1).astype(jnp.bfloat16)
        )
    two_grad = ring_scatter(
        narrow_far([contract_cols(slot, swiglu_matrix) for slot in gate_up_slots]), size
    )
    hidden_norm_grad, mlp_gain_grad = norm_two_back(two_grad)
    hidden_grad = cotangent.astype(jnp.float32) + hidden_norm_grad
    attended_slots = ring_gather(hidden_grad.astype(jnp.bfloat16), size)

    cot_all = jnp.concatenate(cot_slots, axis=0)
    activated_all = jnp.concatenate(activated_slots, axis=0)
    down_part = contract_rows(activated_all, cot_all).astype(jnp.bfloat16)
    swiglu_part = contract_rows(
        jnp.concatenate(two_slots, axis=0), jnp.concatenate(gate_up_slots, axis=0)
    ).astype(jnp.bfloat16)
    swiglu_grad = lax.psum_scatter(swiglu_part, "dp", scatter_dimension=0, tiled=True)
    down_grad = lax.psum_scatter(down_part, "dp", scatter_dimension=1, tiled=True)

    projected_parts = narrow_far([product(slot, down_full) for slot in activated_slots])
    projected_parts[-1], _ = barrier((projected_parts[-1], attended_slots[-1]))
    projected = ring_scatter(projected_parts, size)
    outputs = (hidden + projected).astype(jnp.bfloat16)

    context_grad = jnp.zeros(context.shape, jnp.bfloat16)
    for place, slot in zip(places, attended_slots):
        context_grad = lax.dynamic_update_slice_in_dim(
            context_grad, contract_cols(slot, out_full).astype(jnp.bfloat16), place * rows, 0
        )
    context_ring = jnp.concatenate([pick(context, place, rows) for place in places], axis=0)
    out_part = contract_rows(context_ring, jnp.concatenate(attended_slots, axis=0))
    out_grad = lax.psum_scatter(
        out_part.astype(jnp.bfloat16), "dp", scatter_dimension=1, tiled=True
    )
    query_grad, key_grad, value_grad = attention_backward(
        query, key, value, context_grad, context, logs
    )
    query_pre, key_pre, qknorm_part = rotate_back(
        (
            query_grad.reshape(group_rows, local_kv, QUERY_PER_KEY, HEAD_WIDTH),
            key_grad.reshape(group_rows, local_kv, HEAD_WIDTH),
        )
    )
    mixed_grad = jnp.concatenate(
        [
            query_pre,
            key_pre[:, :, None],
            value_grad.reshape(group_rows, local_kv, 1, HEAD_WIDTH),
        ],
        axis=2,
    )
    mixed_grad = mixed_grad.astype(jnp.bfloat16).reshape(group_rows, -1)
    mixed_slots = [pick(mixed_grad, place, rows) for place in places]
    normed_grad = ring_scatter(
        narrow_far([contract_cols(slot, in_matrix) for slot in mixed_slots]), size
    )
    in_part = contract_rows(
        jnp.concatenate(normed_slots, axis=0), jnp.concatenate(mixed_slots, axis=0)
    )
    in_grad = lax.psum_scatter(
        in_part.astype(jnp.bfloat16), "dp", scatter_dimension=0, tiled=True
    )
    input_norm_grad, attn_gain_grad = norm_one_back(normed_grad)
    input_grad = (hidden_grad + input_norm_grad).astype(jnp.bfloat16)
    norm_grad, qknorm_grad = lax.psum(
        (jnp.stack([attn_gain_grad, mlp_gain_grad]), qknorm_part), ("dp", "tensor")
    )
    in_grad = in_grad.astype(jnp.float32).reshape(input_projection_weight.shape)
    out_grad = out_grad.astype(jnp.float32)
    swiglu_grad = swiglu_grad.astype(jnp.float32).reshape(swiglu_weight.shape)
    down_grad = down_grad.astype(jnp.float32)
    in_new, in_second = adamw(
        input_projection_weight,
        in_grad,
        input_first_moment,
        input_second_moment,
        MODEL_WIDTH ** (-0.5),
    )
    out_new, out_second = adamw(
        out_weight, out_grad, out_mean, out_square, (HQ * HEAD_WIDTH / 8.0) ** (-0.5)
    )
    swiglu_new, swiglu_second = adamw(
        swiglu_weight, swiglu_grad, swiglu_mean, swiglu_square, MODEL_WIDTH ** (-0.5)
    )
    down_new, down_second = adamw(down_weight, down_grad, down_mean, down_square, FF ** (-0.5))
    norm_new, norm_second = adamw(norm_gains, norm_grad, norm_mean, norm_square, gain_rate)
    qknorm_new, qknorm_second = adamw(
        qknorm_gains, qknorm_grad, qknorm_mean, qknorm_square, gain_rate
    )
    return (
        outputs,
        input_grad,
        in_grad,
        in_new,
        in_second,
        out_grad,
        out_new,
        out_second,
        swiglu_grad,
        swiglu_new,
        swiglu_second,
        down_grad,
        down_new,
        down_second,
        norm_grad,
        norm_new,
        norm_second,
        qknorm_grad,
        qknorm_new,
        qknorm_second,
    )


def solution(mesh):
    return jax.shard_map(
        local,
        mesh=mesh,
        in_specs=(
            P(("dp", "tensor"), None),
            P("dp", "tensor", None),
            P("dp", "tensor", None),
            P("dp", "tensor", None),
            P("tensor", "dp"),
            P("tensor", "dp"),
            P("tensor", "dp"),
            P("dp", None, "tensor"),
            P("dp", None, "tensor"),
            P("dp", None, "tensor"),
            P("tensor", "dp"),
            P("tensor", "dp"),
            P("tensor", "dp"),
            P(),
            P(),
            P(),
            P(),
            P(),
            P(),
            P(("dp", "tensor"), None),
        ),
        out_specs=(
            P(("dp", "tensor"), None),
            P(("dp", "tensor"), None),
            P("dp", "tensor", None),
            P("dp", "tensor", None),
            P("dp", "tensor", None),
            P("tensor", "dp"),
            P("tensor", "dp"),
            P("tensor", "dp"),
            P("dp", None, "tensor"),
            P("dp", None, "tensor"),
            P("dp", None, "tensor"),
            P("tensor", "dp"),
            P("tensor", "dp"),
            P("tensor", "dp"),
            P(),
            P(),
            P(),
            P(),
            P(),
            P(),
        ),
        check_vma=False,
    )
```

```python
import jax
import jax.numpy as jnp
from jax import lax
from jax.experimental import pallas as pl
from jax.experimental.pallas import tpu as pltpu
from jax.sharding import PartitionSpec as P

MODEL_WIDTH = 2048
HQ = 16
HEAD_WIDTH = 128
FF = 6144
QUERY_PER_KEY = 2
SEQUENCE_TOKENS = 2048


norm_eps = 1e-06
rope_base = 1000000.0
beta_one = 0.5
beta_two = 0.55
step_count = 5.0
adam_eps = 1e-08
decay_rate = 0.1
gain_rate = 0.3
masked_score = -1e30
log2_e = 1.4426950408889634


def rms_gain(values, gain_row):
    return (
        values * lax.rsqrt(jnp.mean(values * values, axis=-1, keepdims=True) + norm_eps) * gain_row
    )


def rotary_tables(length, width):
    frequency = rope_base ** (
        -2.0 * jnp.arange(width // 2, dtype=jnp.int32).astype(jnp.float32) / width
    )
    angles = jnp.arange(length, dtype=jnp.int32).astype(jnp.float32)[:, None] * frequency[None, :]
    cos, sin = jnp.cos(angles), jnp.sin(angles)
    return jnp.concatenate([cos, cos], axis=1), jnp.concatenate([-sin, sin], axis=1)


def contract_rows(left, right):
    return lax.dot_general(
        left, right, (((0,), (0,)), ((), ())), preferred_element_type=jnp.float32
    )


def contract_cols(left, right):
    return lax.dot_general(
        left, right, (((1,), (1,)), ((), ())), preferred_element_type=jnp.float32
    )


def product(left, right):
    return jnp.dot(left, right, preferred_element_type=jnp.float32)


def adamw(weight, gradient, mean_old, square_old, rate):
    mean_new = beta_one * mean_old + (1.0 - beta_one) * gradient
    square_new = beta_two * square_old + (1.0 - beta_two) * gradient * gradient
    mean_hat = mean_new / (1.0 - beta_one**step_count)
    square_hat = square_new / (1.0 - beta_two**step_count)
    weight_new = weight - rate * (
        mean_hat / (jnp.sqrt(square_hat) + adam_eps) + decay_rate * weight
    )
    return (weight_new, square_new)


def ring_place(index, size):
    return jnp.where(index < size // 2, index, size // 2 + size - 1 - index)


def ring_pairs(size):
    half = size // 2
    order = list(range(half)) + list(range(size - 1, half - 1, -1))
    ahead = [(order[r], order[(r + 1) % size]) for r in range(size)]
    return ahead, [(b, a) for a, b in ahead]


def ring_offsets(size):
    offsets = [0]
    for step in range(1, size // 2):
        offsets += [step, -step]
    return offsets + [size // 2]


class Order:
    def __init__(self):
        self.last = ()

    def turn(self, *values):
        tied = lax.optimization_barrier(values + self.last)[: len(values)]
        return tied[0] if len(values) == 1 else tied

    def mark(self, *values):
        self.last = values
        return values[0] if len(values) == 1 else values


def ring_gather(rows, size, work, order, hold=()):
    ahead, back = ring_pairs(size)
    half = rows.shape[0] // 2
    groups = [[rows]]
    from_left = from_right = rows
    work(0, groups[0])
    for step in range(1, size // 2):
        from_left, from_right = (
            lax.ppermute(from_left, "tensor", ahead),
            lax.ppermute(from_right, "tensor", back),
        )
        held = tuple(hold) if step == size // 2 - 1 else ()
        from_left, from_right = lax.optimization_barrier(
            (from_left, from_right) + held + order.last
        )[:2]
        groups.append([from_right, from_left])
        work(step, groups[-1])
    low = lax.ppermute(from_left[:half], "tensor", ahead)
    high = lax.ppermute(from_right[half:], "tensor", back)
    groups.append(list(lax.optimization_barrier((low, high) + order.last)[:2]))
    work(size // 2, groups[-1])
    return groups


def relay_kernel(pair_ref, ahead_ref, back_ref, right_ref, left_ref):
    rows = right_ref.shape[0]
    taken = ahead_ref.shape[0]
    for first, out_ref, got_ref, low in (
        (0, right_ref, ahead_ref, 0),
        (rows, left_ref, back_ref, rows - taken),
    ):
        out_ref[low : low + taken, :] = (
            pair_ref[first + low : first + low + taken, :].astype(jnp.float32)
            + got_ref[...].astype(jnp.float32)
        ).astype(jnp.bfloat16)
        if taken < rows:
            rest = rows - taken - low
            out_ref[rest : rest + rows - taken, :] = pair_ref[
                first + rest : first + rest + rows - taken, :
            ].astype(jnp.bfloat16)


def relay(pair, going_ahead, going_back):
    rows, width = pair.shape[0] // 2, pair.shape[1]
    tile = tile_of(width, 512)
    spec = lambda count: pl.BlockSpec((count, tile), lambda i: (0, i))
    return pl.pallas_call(
        relay_kernel,
        grid=(width // tile,),
        in_specs=[spec(2 * rows), spec(going_ahead.shape[0]), spec(going_back.shape[0])],
        out_specs=[spec(rows)] * 2,
        out_shape=[jax.ShapeDtypeStruct((rows, width), jnp.bfloat16)] * 2,
        compiler_params=kernel_params(),
        cost_estimate=SMALL_COST,
        name="relay",
    )(pair, going_ahead, going_back)


def ring_scatter(size, part, order, hold=(), first=(), between=None, got=None):
    ahead, back = ring_pairs(size)
    low, high = part(size // 2)
    if hold:
        low, high = lax.optimization_barrier((low, high) + tuple(hold))[:2]
    going_ahead = lax.ppermute(low, "tensor", ahead)
    going_back = lax.ppermute(high, "tensor", back)
    for step in range(size // 2 - 1, 0, -1):
        pair = part(step)
        going_ahead, going_back = order.turn(going_ahead, going_back, *first)[:2]
        to_right, to_left = order.mark(*relay(pair, going_ahead, going_back))
        if got is not None:
            got[:] = [to_right, to_left]
        going_ahead = lax.ppermute(to_right, "tensor", ahead)
        going_back = lax.ppermute(to_left, "tensor", back)
    if between is not None:
        between()
    own = part(0)
    if size == 2:
        return own, (jnp.concatenate([going_ahead, going_back], axis=0),)
    return own, (going_ahead, going_back)


def total(own, received):
    return own + sum(block.astype(jnp.float32) for block in received)


def sum_everywhere(values, axes):
    for axis in axes:
        size = lax.axis_size(axis)
        if size & (size - 1):
            values = lax.psum(values, axis)
            continue
        reach = 1
        while reach < size:
            pairs = [(i, i ^ reach) for i in range(size)]
            values = values + lax.ppermute(values, axis, pairs)
            reach *= 2
    return values


def tile_of(width, most):
    return next(t for t in (most, 512, 256, 128) if t <= most and width % t == 0)


def kernel_params(mebibytes=32):
    return pltpu.CompilerParams(vmem_limit_bytes=mebibytes * 1024 * 1024)


SMALL_COST = pl.CostEstimate(flops=1_000_000, bytes_accessed=1_000_000, transcendentals=0)


class Piece:
    def __init__(self, array, count=None, index=0, entry=None):
        self.array, self.count = array, count or array.shape[0]
        self.index, self.entry = index, entry

    def row(self, table):
        return self.index if self.entry is None else table[self.entry]

    def spec(self, width=None):
        if width is None:
            return pl.BlockSpec(
                (self.count, self.array.shape[1]),
                lambda i, table: (self.row(table), 0),
                pipeline_mode=pl.Buffered(1),
            )
        return pl.BlockSpec((self.count, width), lambda i, table: (self.row(table), i))


def pieces_of(blocks):
    return [Piece(block) for block in blocks]


def stacked(refs):
    values = [ref[...] for ref in refs]
    return values[0] if len(values) == 1 else jnp.concatenate(values, axis=0)


def row_call(kernel, name, table, grid, operands, specs, outs, out_specs, aliases=None):
    return pl.pallas_call(
        kernel,
        grid_spec=pltpu.PrefetchScalarGridSpec(
            num_scalar_prefetch=1, grid=grid, in_specs=specs, out_specs=out_specs
        ),
        out_shape=outs,
        input_output_aliases=aliases or {},
        compiler_params=kernel_params(),
        cost_estimate=SMALL_COST,
        name=name,
    )(table, *operands)


def product_kernel(count, crossed, *refs):
    rows = stacked(refs[1 : 1 + count])
    matrix = refs[1 + count][...]
    result = contract_cols(rows, matrix) if crossed else product(rows, matrix)
    outs = refs[-2:] if refs[-1].shape[0] < rows.shape[0] else refs[-1:]
    size = rows.shape[0] // len(outs)
    for i, out_ref in enumerate(outs):
        out_ref[...] = result[i * size : (i + 1) * size].astype(out_ref.dtype)


def block_product(table, pieces, matrix, crossed, kind=jnp.bfloat16, halves=False, into=None):
    width = matrix.shape[0] if crossed else matrix.shape[1]
    tile = tile_of(width, 512)
    count = sum(piece.count for piece in pieces)
    if crossed:
        matrix_spec = pl.BlockSpec((tile, matrix.shape[1]), lambda i, table: (i, 0))
    else:
        matrix_spec = pl.BlockSpec((matrix.shape[0], tile), lambda i, table: (0, i))
    operands = [piece.array for piece in pieces] + [matrix]
    specs = [piece.spec() for piece in pieces] + [matrix_spec]
    aliases = {}
    index, all_rows = 0, count
    if into is not None:
        all_rows, index, so_far = into
        if so_far is not None:
            operands.append(so_far)
            specs.append(pl.BlockSpec(memory_space=pltpu.HBM))
            aliases = {len(operands): 0}
    if halves:
        count = all_rows = count // 2
    out_spec = pl.BlockSpec((count, tile), lambda i, table: (index, i))
    out = jax.ShapeDtypeStruct((all_rows, width), kind)
    result = row_call(
        lambda *refs: product_kernel(len(pieces), crossed, *refs),
        "block_product",
        table,
        (width // tile,),
        operands,
        specs,
        [out] * (2 if halves else 1),
        [out_spec] * (2 if halves else 1),
        aliases,
    )
    return result if halves else result[0]


def gate_kernel(count, *refs):
    rows = stacked(refs[1 : 1 + count])
    gate_ref, up_ref, activated_ref, gate_out, up_out = refs[1 + count :]
    gate = product(rows, gate_ref[...])
    up = product(rows, up_ref[...])
    activated_ref[...] = (gate * jax.nn.sigmoid(gate) * up).astype(jnp.bfloat16)
    gate_out[...] = gate.astype(gate_out.dtype)
    up_out[...] = up.astype(up_out.dtype)


def gate_up_product(table, pieces, matrix):
    depth, width = matrix.shape[0], matrix.shape[1] // 2
    count = sum(piece.count for piece in pieces)
    tile = tile_of(width, 256)
    steps = width // tile
    return row_call(
        lambda *refs: gate_kernel(len(pieces), *refs),
        "gate_up",
        table,
        (steps,),
        [piece.array for piece in pieces] + [matrix, matrix],
        [piece.spec() for piece in pieces]
        + [
            pl.BlockSpec((depth, tile), lambda i, table: (0, i)),
            pl.BlockSpec((depth, tile), lambda i, table: (0, steps + i)),
        ],
        [jax.ShapeDtypeStruct((count, width), jnp.bfloat16)] * 3,
        [pl.BlockSpec((count, tile), lambda i, table: (0, i))] * 3,
    )


def gate_grad_kernel(count, *refs):
    rows = stacked(refs[1 : 1 + count])
    down_ref, gate_ref, up_ref, out_ref = refs[1 + count :]
    step = pl.program_id(0)
    tile = gate_ref.shape[1]
    width = out_ref.shape[1] // 2
    grad = contract_cols(rows, down_ref[...])
    gate = gate_ref[...].astype(jnp.float32)
    up = up_ref[...].astype(jnp.float32)
    sigmoid_gate = jax.nn.sigmoid(gate)
    scaled = grad * sigmoid_gate
    start = pl.multiple_of(step * tile, tile)
    out_ref[:, pl.ds(start, tile)] = (
        scaled * up * (1.0 + gate * (1.0 - sigmoid_gate))
    ).astype(jnp.bfloat16)
    out_ref[:, pl.ds(pl.multiple_of(width + step * tile, tile), tile)] = (scaled * gate).astype(
        jnp.bfloat16
    )


def gate_up_gradient(table, pieces, down, gate, up):
    count, width = gate.shape
    tile = tile_of(width, 256)
    part = pl.BlockSpec((count, tile), lambda i, table: (0, i))
    return row_call(
        lambda *refs: gate_grad_kernel(len(pieces), *refs),
        "gate_up_grad",
        table,
        (width // tile,),
        [piece.array for piece in pieces] + [down, gate, up],
        [piece.spec() for piece in pieces]
        + [pl.BlockSpec((tile, down.shape[1]), lambda i, table: (i, 0)), part, part],
        [jax.ShapeDtypeStruct((count, 2 * width), jnp.bfloat16)],
        [pl.BlockSpec((count, 2 * width), lambda i, table: (0, 0))],
    )[0]


def rows_kernel(count, *refs):
    out_ref = refs[-1]
    out_ref[...] = sum(
        contract_rows(refs[1 + i][...], refs[1 + count + i][...]) for i in range(count)
    ).astype(out_ref.dtype)


def weight_gradient(table, lefts, rights):
    width, columns = lefts[0].array.shape[1], rights[0].array.shape[1]
    tile = tile_of(width, 256)
    return row_call(
        lambda *refs: rows_kernel(len(lefts), *refs),
        "weight_grad",
        table,
        (width // tile,),
        [piece.array for piece in lefts + rights],
        [piece.spec(tile) for piece in lefts] + [piece.spec() for piece in rights],
        [jax.ShapeDtypeStruct((width, columns), jnp.bfloat16)],
        [pl.BlockSpec((tile, columns), lambda i, table: (i, 0))],
    )[0]


def split_groups(groups, rows):
    own, *pairs, far = groups
    pieces = [Piece(own)]
    for pair in pairs:
        pieces += [Piece(pair, rows, 0), Piece(pair, rows, 1)]
    return pieces + [Piece(far, rows // 2, 0), Piece(far, rows // 2, 1)]


def project_kernel(count, *refs):
    rows = stacked(refs[1 : 1 + count])
    matrix_ref, gain_ref, cos_ref, sin_ref = refs[1 + count : 5 + count]
    query_ref, key_ref, value_ref, query_raw, key_raw = refs[-5:]
    width = HEAD_WIDTH
    mixed = product(rows, matrix_ref[...])
    cos, sin = cos_ref[...], sin_ref[...]
    for part in range(QUERY_PER_KEY + 1):
        values = mixed[:, part * width : (part + 1) * width]
        is_key = part == QUERY_PER_KEY
        gain = gain_ref[1:2, :] if is_key else gain_ref[0:1, :]
        scale = lax.rsqrt(jnp.mean(values * values, axis=1, keepdims=True) + norm_eps)
        scaled = values * scale * gain
        turned = scaled * cos + pltpu.roll(scaled, width // 2, 1) * sin
        if is_key:
            key_ref[...] = turned.astype(jnp.bfloat16)
            key_raw[...] = values
        else:
            query_ref[:, part * width : (part + 1) * width] = turned.astype(jnp.bfloat16)
            query_raw[:, part * width : (part + 1) * width] = values
    value_ref[...] = mixed[:, (QUERY_PER_KEY + 1) * width :].astype(jnp.bfloat16)


def project(blocks, matrix, gains, cos, sin, place, total_rows, before):
    count, depth = sum(block.shape[0] for block in blocks), matrix.shape[0]
    block = (QUERY_PER_KEY + 2) * HEAD_WIDTH
    heads = matrix.shape[1] // block
    wide = QUERY_PER_KEY * HEAD_WIDTH
    per_table = cos.shape[0] // count
    table_spec = pl.BlockSpec(
        (count, HEAD_WIDTH), lambda h, at: (lax.rem(at[0], per_table), 0)
    )
    widths = (wide, HEAD_WIDTH, HEAD_WIDTH, wide, HEAD_WIDTH)
    kinds = (jnp.bfloat16,) * 3 + (jnp.float32,) * 2
    kept = () if before is None else tuple(before)
    return pl.pallas_call(
        lambda *refs: project_kernel(len(blocks), *refs),
        grid_spec=pltpu.PrefetchScalarGridSpec(
            num_scalar_prefetch=1,
            grid=(heads,),
            in_specs=[
                pl.BlockSpec((rows.shape[0], depth), lambda h, at: (0, 0)) for rows in blocks
            ]
            + [
                pl.BlockSpec((depth, block), lambda h, at: (0, h)),
                pl.BlockSpec((2, HEAD_WIDTH), lambda h, at: (0, 0)),
                table_spec,
                table_spec,
            ]
            + [pl.BlockSpec(memory_space=pltpu.HBM)] * len(kept),
            out_specs=[pl.BlockSpec((count, w), lambda h, at: (at[0], h)) for w in widths],
        ),
        out_shape=[
            jax.ShapeDtypeStruct((total_rows, heads * w), kind) for w, kind in zip(widths, kinds)
        ],
        input_output_aliases={5 + len(blocks) + i: i for i in range(len(kept))},
        compiler_params=kernel_params(56),
        cost_estimate=SMALL_COST,
        name="project",
    )(place.reshape(1), *blocks, matrix, gains, cos, sin, *kept)


def attend_kernel(scale, query_ref, key_ref, value_ref, out_ref, log_ref):
    block = query_ref.shape[0]
    width = key_ref.shape[1]
    group = query_ref.shape[1] // width
    step = pl.program_id(2)
    below = lax.broadcasted_iota(jnp.int32, (block, block), 0) <= lax.broadcasted_iota(
        jnp.int32, (block, block), 1
    )
    queries = [query_ref[:, g * width : (g + 1) * width] for g in range(group)]

    def visit(start, carry, masked):
        keys = key_ref[pl.ds(start, block), :]
        values = value_ref[pl.ds(start, block), :]
        new = []
        for g in range(group):
            total, acc = carry[g]
            weights = jnp.exp2(contract_cols(keys, queries[g]) * (scale * log2_e))
            if masked:
                weights = jnp.where(below, weights, 0.0)
            total = total + jnp.sum(weights, axis=0, keepdims=True)
            acc = acc + contract_rows(values, weights.astype(jnp.bfloat16))
            new.append((total, acc))
        return tuple(new)

    start_carry = tuple(
        (jnp.zeros((1, block), jnp.float32), jnp.zeros((width, block), jnp.float32))
        for _ in range(group)
    )
    carry = lax.fori_loop(
        0, step, lambda j, c: visit(pl.multiple_of(j * block, block), c, False), start_carry
    )
    carry = visit(pl.multiple_of(step * block, block), carry, True)
    for g in range(group):
        total, acc = carry[g]
        out_ref[:, g * width : (g + 1) * width] = jnp.transpose(acc / total).astype(jnp.bfloat16)
        log_ref[0, 0, g : g + 1, :] = jnp.log2(total)


def attention_forward(query, key, value, block):
    rows = query.shape[0]
    heads = key.shape[1] // HEAD_WIDTH
    steps = SEQUENCE_TOKENS // block
    wide = QUERY_PER_KEY * HEAD_WIDTH
    sequences = rows // SEQUENCE_TOKENS
    query_spec = pl.BlockSpec((block, wide), lambda h, s, i: (s * steps + i, h))
    key_spec = pl.BlockSpec((SEQUENCE_TOKENS, HEAD_WIDTH), lambda h, s, i: (s, h))
    return pl.pallas_call(
        lambda *refs: attend_kernel(HEAD_WIDTH ** (-0.5), *refs),
        grid=(heads, sequences, steps),
        in_specs=[query_spec, key_spec, key_spec],
        out_specs=[
            query_spec,
            pl.BlockSpec(
                (1, 1, QUERY_PER_KEY, block), lambda h, s, i: (h, s * steps + i, 0, 0)
            ),
        ],
        out_shape=[
            jax.ShapeDtypeStruct(query.shape, jnp.bfloat16),
            jax.ShapeDtypeStruct((heads, rows // block, QUERY_PER_KEY, block), jnp.float32),
        ],
        compiler_params=kernel_params(56),
        cost_estimate=SMALL_COST,
        name="attend",
    )(query, key, value)


def norm_back(values, grad, gain, cos, sin):
    width = values.shape[1]
    turned = grad * cos + pltpu.roll(grad * sin, width // 2, 1)
    scale = lax.rsqrt(jnp.mean(values * values, axis=1, keepdims=True) + norm_eps)
    unit = values * scale
    inner = turned * gain
    back = scale * (inner - unit * jnp.mean(inner * unit, axis=1, keepdims=True))
    return back.astype(jnp.bfloat16), jnp.sum(turned * unit, axis=0, keepdims=True)


def attend_back_kernel(
    scale,
    table_ref,
    query_ref,
    key_ref,
    value_ref,
    grad_ref,
    context_ref,
    log_ref,
    query_raw,
    key_raw,
    gain_ref,
    cos_ref,
    sin_ref,
    *refs,
):
    mixed_out, gain_out, key_sum, value_sum = refs[-4:]
    block = query_ref.shape[0]
    width = key_ref.shape[1]
    group = query_ref.shape[1] // width
    sequence, step = pl.program_id(0), pl.program_id(1)
    below = lax.broadcasted_iota(jnp.int32, (block, block), 0) <= lax.broadcasted_iota(
        jnp.int32, (block, block), 1
    )

    @pl.when(step == 0)
    def _():
        key_sum[...] = jnp.zeros_like(key_sum)
        value_sum[...] = jnp.zeros_like(value_sum)

    @pl.when((step == 0) & (sequence == 0))
    def _():
        gain_out[...] = jnp.zeros_like(gain_out)

    queries, grads, logs, dots = [], [], [], []
    for g in range(group):
        cols = slice(g * width, (g + 1) * width)
        queries.append(query_ref[:, cols])
        grads.append(grad_ref[:, cols])
        logs.append(log_ref[0, 0, g : g + 1, :])
        both = grads[g].astype(jnp.float32) * context_ref[:, cols].astype(jnp.float32)
        dots.append(jnp.sum(jnp.transpose(both), axis=0, keepdims=True))

    def visit(start, carry, masked):
        rows = pl.ds(start, block)
        keys = key_ref[rows, :]
        values = value_ref[rows, :]
        new = []
        key_part = value_part = None
        for g in range(group):
            weights = jnp.exp2(contract_cols(keys, queries[g]) * (scale * log2_e) - logs[g])
            if masked:
                weights = jnp.where(below, weights, 0.0)
            slope = contract_cols(values, grads[g])
            score = (weights * (slope - dots[g])).astype(jnp.bfloat16)
            value_g = product(weights.astype(jnp.bfloat16), grads[g])
            key_g = product(score, queries[g])
            key_part = key_g if key_part is None else key_part + key_g
            value_part = value_g if value_part is None else value_part + value_g
            new.append(carry[g] + contract_rows(keys, score))
        key_sum[rows, :] += key_part
        value_sum[rows, :] += value_part
        return tuple(new)

    carry = tuple(jnp.zeros((width, block), jnp.float32) for _ in range(group))
    carry = lax.fori_loop(
        0, step, lambda j, c: visit(pl.multiple_of(j * block, block), c, False), carry
    )
    carry = visit(pl.multiple_of(step * block, block), carry, True)
    rows = pl.ds(pl.multiple_of(step * block, block), block)
    cos, sin = cos_ref[rows, :], sin_ref[rows, :]
    for g in range(group):
        cols = slice(g * width, (g + 1) * width)
        back, gain = norm_back(
            query_raw[:, cols], jnp.transpose(carry[g]) * scale, gain_ref[0:1, :], cos, sin
        )
        mixed_out[rows, cols] = back
        gain_out[0:1, :] += gain

    @pl.when(step == pl.num_programs(1) - 1)
    def _():
        def finish(j, _):
            rows = pl.ds(pl.multiple_of(j * block, block), block)
            back, gain = norm_back(
                key_raw[rows, :],
                key_sum[rows, :] * scale,
                gain_ref[1:2, :],
                cos_ref[rows, :],
                sin_ref[rows, :],
            )
            mixed_out[rows, group * width : (group + 1) * width] = back
            mixed_out[rows, (group + 1) * width :] = value_sum[rows, :].astype(jnp.bfloat16)
            gain_out[1:2, :] += gain
            return 0

        lax.fori_loop(0, pl.num_programs(1), finish, 0)


def attention_backward(
    slots, query, key, value, grad, context, logs, query_raw, key_raw, gains, cos, sin, head, before
):
    rows = query.shape[0]
    block = logs.shape[-1]
    steps = SEQUENCE_TOKENS // block
    wide = QUERY_PER_KEY * HEAD_WIDTH
    heads = key.shape[1] // HEAD_WIDTH
    sequences = rows // SEQUENCE_TOKENS
    mixed = (QUERY_PER_KEY + 2) * HEAD_WIDTH
    query_spec = pl.BlockSpec((block, wide), lambda s, i, slots: (s * steps + i, head))
    key_spec = pl.BlockSpec((SEQUENCE_TOKENS, HEAD_WIDTH), lambda s, i, slots: (s, head))
    table_spec = pl.BlockSpec((SEQUENCE_TOKENS, HEAD_WIDTH), lambda s, i, slots: (0, 0))
    gain_spec = pl.BlockSpec((2, HEAD_WIDTH), lambda s, i, slots: (0, 0))
    kept = () if before is None else (before,)
    return pl.pallas_call(
        lambda *refs: attend_back_kernel(HEAD_WIDTH ** (-0.5), *refs),
        grid_spec=pltpu.PrefetchScalarGridSpec(
            num_scalar_prefetch=1,
            grid=(sequences, steps),
            in_specs=[
            query_spec,
            key_spec,
            key_spec,
            pl.BlockSpec((block, wide), lambda s, i, slots: (slots[s * steps + i], head)),
            query_spec,
            pl.BlockSpec(
                (1, 1, QUERY_PER_KEY, block), lambda s, i, slots: (head, s * steps + i, 0, 0)
            ),
            query_spec,
            key_spec,
            gain_spec,
            table_spec,
            table_spec,
        ]
        + [pl.BlockSpec(memory_space=pltpu.HBM)] * len(kept),
        out_specs=[
            pl.BlockSpec((SEQUENCE_TOKENS, mixed), lambda s, i, slots: (s, head)),
            gain_spec,
        ],
        scratch_shapes=[pltpu.VMEM((SEQUENCE_TOKENS, HEAD_WIDTH), jnp.float32)] * 2,
        ),
        out_shape=[
            jax.ShapeDtypeStruct((rows, heads * mixed), jnp.bfloat16),
            jax.ShapeDtypeStruct((2, HEAD_WIDTH), jnp.float32),
        ],
        input_output_aliases={12: 0} if kept else {},
        compiler_params=kernel_params(56),
        cost_estimate=SMALL_COST,
        name="attend_back",
    )(slots, query, key, value, grad, context, logs, query_raw, key_raw, gains, cos, sin, *kept)


def local(
    inputs,
    input_projection_weight,
    input_first_moment,
    input_second_moment,
    out_weight,
    out_mean,
    out_square,
    swiglu_weight,
    swiglu_mean,
    swiglu_square,
    down_weight,
    down_mean,
    down_square,
    norm_gains,
    norm_mean,
    norm_square,
    qknorm_gains,
    qknorm_mean,
    qknorm_square,
    cotangent,
):
    size = lax.axis_size("tensor")
    rows = inputs.shape[0]
    half = rows // 2
    group_rows = rows * size
    last = size // 2
    dp_rows = input_projection_weight.shape[0]
    local_kv = input_projection_weight.shape[1]
    local_ff = swiglu_weight.shape[2]
    me = ring_place(lax.axis_index("tensor"), size)
    places = [ring_place((me + d + size) % size, size) for d in ring_offsets(size)]
    group_places = [places[:1]]
    for step in range(1, last):
        group_places.append(places[2 * step - 1 : 2 * step + 1])
    group_places.append(places[-1:])
    table = jnp.stack(places + [2 * places[-1], 2 * places[-1] + 1]).astype(jnp.int32)
    away = (ring_place(jnp.arange(size, dtype=jnp.int32), size) - me + size) % size
    slots = jnp.where(
        away == 0,
        size - 2,
        jnp.where(
            away == last,
            size - 1,
            jnp.where(away < last, 2 * away - 2, 2 * (size - away) - 1),
        ),
    ).astype(jnp.int32)
    order = Order()
    turn, mark = order.turn, order.mark
    tie = lax.optimization_barrier

    def ordered(array, group):
        entries = [0] if group == 0 else [2 * group - 1, 2 * group]
        if group == last:
            entries = [size - 1]
        return [Piece(array, rows, entry=entry) for entry in entries]

    def ordered_finely(array):
        pieces = [Piece(array, rows, entry=entry) for entry in range(size - 1)]
        return pieces + [Piece(array, half, entry=size + i) for i in range(2)]

    def flat(groups):
        return pieces_of([block for group in groups for block in group])

    in_low = input_projection_weight.astype(jnp.bfloat16).reshape(dp_rows, -1)
    out_low = out_weight.astype(jnp.bfloat16)
    swiglu_low = swiglu_weight.astype(jnp.bfloat16).reshape(dp_rows, 2 * local_ff)
    down_low = down_weight.astype(jnp.bfloat16)
    in_matrix = lax.all_gather(in_low, "dp", axis=0, tiled=True)
    out_full = lax.all_gather(out_low, "dp", axis=1, tiled=True)
    swiglu_matrix = lax.all_gather(swiglu_low, "dp", axis=0, tiled=True)
    down_full = lax.all_gather(down_low, "dp", axis=1, tiled=True)

    inputs_f = inputs.astype(jnp.float32)
    normed_f, norm_one_back = jax.vjp(lambda rows: rms_gain(rows, norm_gains[0]), inputs_f)
    cos, sin = rotary_tables(SEQUENCE_TOKENS, HEAD_WIDTH)
    projected = []

    def project_group(group, blocks):
        calls = [blocks] if group in (0, last) else [[block] for block in blocks]
        for place, call in zip(group_places[group], calls):
            call[0] = turn(call[0])
            projected[:] = mark(
                *project(
                    call, in_matrix, qknorm_gains, cos, sin, place, group_rows, projected or None
                )
            )

    normed_groups = ring_gather(
        normed_f.astype(jnp.bfloat16), size, project_group, order, hold=(in_matrix,)
    )
    query, key, value, query_raw, key_raw = projected
    cotangent_sent = tie((cotangent, *normed_groups[-1]))[0]

    context, logs = mark(*attention_forward(query, key, value, rows))
    cot_groups = ring_gather(cotangent_sent, size, lambda group, blocks: None, Order())

    def out_group(group):
        kind = jnp.float32 if group == 0 else jnp.bfloat16
        array = turn(context)
        part = block_product(
            table, ordered(array, group), out_full, False, kind, halves=group == last
        )
        return mark(*part) if group == last else mark(part)

    own, received = ring_scatter(size, out_group, order, first=cot_groups[-1])
    received = tie((*received, swiglu_matrix))[: len(received)]
    hidden = inputs_f + total(own, received)
    normed_two_f, norm_two_back = jax.vjp(rms_gain, hidden, norm_gains[1])

    gate_groups = []
    grads = [None] * (last + 1)

    def gate_group(group, blocks):
        blocks[0] = turn(blocks[0])
        gate_groups.append(mark(*gate_up_product(table, pieces_of(blocks), swiglu_matrix)))
        if group == 0:
            two_own.append(two_group(0))

    def two_group(group):
        cots = [turn(cot_groups[group][0])] + cot_groups[group][1:]
        grads[group] = mark(
            gate_up_gradient(table, pieces_of(cots), down_full, *gate_groups[group][1:])
        )
        kind = jnp.float32 if group == 0 else jnp.bfloat16
        part = block_product(
            table, [Piece(grads[group])], swiglu_matrix, True, kind, halves=group == last
        )
        return mark(*part) if group == last else mark(part)

    two_own = []

    two_groups = ring_gather(
        normed_two_f.astype(jnp.bfloat16), size, gate_group, order, hold=(down_full,)
    )
    activated = [parts[0] for parts in gate_groups]
    early = []

    def down_gradient():
        lefts = split_groups([turn(activated[0])] + activated[1:], rows)
        early.append(mark(weight_gradient(table, lefts, flat(cot_groups))))

    own, received = ring_scatter(
        size,
        lambda group: two_own[0] if group == 0 else two_group(group),
        order,
        between=down_gradient,
    )
    (down_part,) = early
    down_part, *received = tie((down_part, *received))
    down_grad = lax.psum_scatter(down_part, "dp", scatter_dimension=1, tiled=True)
    received = turn(*received) if len(received) > 1 else (turn(*received),)
    two_grad = total(own, received)
    hidden_norm_grad, mlp_gain_grad = norm_two_back(two_grad)
    hidden_grad = cotangent.astype(jnp.float32) + hidden_norm_grad

    context_grad = [None]
    more = []

    def context_group(group, blocks):
        blocks[0] = turn(blocks[0])
        index = size - 2 if group == 0 else size - 1 if group == last else group - 1
        context_grad[0] = mark(
            block_product(
                table, pieces_of(blocks), out_full, True, into=(group_rows, index, context_grad[0])
            )
        )
        if group == 0:
            twos = flat(two_groups)
            twos[0].array = turn(twos[0].array)
            more.append(mark(weight_gradient(table, twos, split_groups(grads, rows))))

    attended_groups = ring_gather(hidden_grad.astype(jnp.bfloat16), size, context_group, order)
    swiglu_part = tie((more[0], *attended_groups[last - 1]))[0]
    swiglu_grad = lax.psum_scatter(swiglu_part, "dp", scatter_dimension=0, tiled=True)
    head_grads, out_parts = [], []

    def head_backward(head):
        head_grads.append(
            mark(
                *attention_backward(
                    slots, turn(query), key, value, context_grad[0], context, logs, query_raw,
                    key_raw, qknorm_gains, cos, sin, head,
                    head_grads[-1][0] if head_grads else None,
                )
            )
        )

    def down_group(group):
        if group == 0:
            for head in range(1, local_kv):
                head_backward(head)
        kind = jnp.float32 if group == 0 else jnp.bfloat16
        part = block_product(
            table, [Piece(turn(activated[group]))], down_full, False, kind, halves=group == last
        )
        part = mark(*part) if group == last else mark(part)
        return part

    def out_gradient():
        out_parts.append(
            mark(weight_gradient(table, ordered_finely(turn(context)), flat(attended_groups)))
        )
        head_backward(0)

    own, received = ring_scatter(
        size, down_group, order, hold=attended_groups[-1], between=out_gradient
    )
    out_part, down_grad = tie((out_parts[0], down_grad, *received, *head_grads[-1]))[:2]
    out_grad = lax.psum_scatter(out_part, "dp", scatter_dimension=1, tiled=True)
    outputs = (hidden + total(own, received)).astype(jnp.bfloat16)
    mixed_grad = head_grads[-1][0]
    qknorm_part = sum(pair[1] for pair in head_grads)
    in_parts, gains = [], []

    def normed_group(group):
        kind = jnp.float32 if group == 0 else jnp.bfloat16
        array = turn(mixed_grad)
        part = block_product(
            table, ordered(array, group), in_matrix, True, kind, halves=group == last
        )
        part = mark(*part) if group == last else mark(part)
        if group == last:
            normeds = flat(normed_groups)
            normeds[0].array = turn(normeds[0].array)
            in_parts.append(
                mark(weight_gradient(table, normeds, ordered_finely(mixed_grad)))
            )
        if group == 1 or last == 1:
            gains.append(
                mark(
                    jnp.sum(
                        turn(in_parts[0]).astype(jnp.float32) * in_matrix.astype(jnp.float32),
                        axis=1,
                    )
                )
            )
        return part

    got = []
    own, received = ring_scatter(size, normed_group, order, hold=(outputs,), got=got)
    in_part, swiglu_grad = tie((in_parts[0], swiglu_grad, *got))[:2]
    in_grad = lax.psum_scatter(in_part, "dp", scatter_dimension=0, tiled=True)
    in_grad = in_grad.astype(jnp.float32).reshape(input_projection_weight.shape)
    out_grad, swiglu_grad, down_grad = tie((out_grad, swiglu_grad, down_grad, *got))[:3]
    swiglu_grad = swiglu_grad.astype(jnp.float32).reshape(swiglu_weight.shape)
    out_grad, down_grad = out_grad.astype(jnp.float32), down_grad.astype(jnp.float32)
    out_new, out_second = adamw(
        out_weight, out_grad, out_mean, out_square, (HQ * HEAD_WIDTH / 8.0) ** (-0.5)
    )
    swiglu_new, swiglu_second = adamw(
        swiglu_weight, swiglu_grad, swiglu_mean, swiglu_square, MODEL_WIDTH ** (-0.5)
    )
    down_new, down_second = adamw(down_weight, down_grad, down_mean, down_square, FF ** (-0.5))
    (
        received,
        own,
        out_grad,
        out_new,
        out_second,
        swiglu_grad,
        swiglu_new,
        swiglu_second,
        down_grad,
        down_new,
        down_second,
    ) = tie(
        (
            received,
            own,
            out_grad,
            out_new,
            out_second,
            swiglu_grad,
            swiglu_new,
            swiglu_second,
            down_grad,
            down_new,
            down_second,
        )
    )
    normed_grad = total(own, received)
    gain_rows = jnp.stack([tie((gains[0], *received))[0] / norm_gains[0], mlp_gain_grad])
    gain_sums = sum_everywhere(
        jnp.concatenate([gain_rows, qknorm_part], axis=1), ("tensor", "dp")
    )
    norm_grad, qknorm_grad = gain_sums[:, :MODEL_WIDTH], gain_sums[:, MODEL_WIDTH:]
    norm_new, norm_second = adamw(norm_gains, norm_grad, norm_mean, norm_square, gain_rate)
    qknorm_new, qknorm_second = adamw(
        qknorm_gains, qknorm_grad, qknorm_mean, qknorm_square, gain_rate
    )
    (input_norm_grad,) = norm_one_back(normed_grad)
    input_grad = (hidden_grad + input_norm_grad).astype(jnp.bfloat16)
    in_new, in_second = adamw(
        input_projection_weight,
        in_grad,
        input_first_moment,
        input_second_moment,
        MODEL_WIDTH ** (-0.5),
    )
    return (
        outputs,
        input_grad,
        in_grad,
        in_new,
        in_second,
        out_grad,
        out_new,
        out_second,
        swiglu_grad,
        swiglu_new,
        swiglu_second,
        down_grad,
        down_new,
        down_second,
        norm_grad,
        norm_new,
        norm_second,
        qknorm_grad,
        qknorm_new,
        qknorm_second,
    )


def solution(mesh):
    return jax.shard_map(
        local,
        mesh=mesh,
        in_specs=(
            P(("dp", "tensor"), None),
            P("dp", "tensor", None),
            P("dp", "tensor", None),
            P("dp", "tensor", None),
            P("tensor", "dp"),
            P("tensor", "dp"),
            P("tensor", "dp"),
            P("dp", None, "tensor"),
            P("dp", None, "tensor"),
            P("dp", None, "tensor"),
            P("tensor", "dp"),
            P("tensor", "dp"),
            P("tensor", "dp"),
            P(),
            P(),
            P(),
            P(),
            P(),
            P(),
            P(("dp", "tensor"), None),
        ),
        out_specs=(
            P(("dp", "tensor"), None),
            P(("dp", "tensor"), None),
            P("dp", "tensor", None),
            P("dp", "tensor", None),
            P("dp", "tensor", None),
            P("tensor", "dp"),
            P("tensor", "dp"),
            P("tensor", "dp"),
            P("dp", None, "tensor"),
            P("dp", None, "tensor"),
            P("dp", None, "tensor"),
            P("tensor", "dp"),
            P("tensor", "dp"),
            P("tensor", "dp"),
            P(),
            P(),
            P(),
            P(),
            P(),
            P(),
        ),
        check_vma=False,
    )
```

```python
import jax
import jax.numpy as jnp
from jax import lax
from jax.experimental import pallas as pl
from jax.experimental.pallas import tpu as pltpu
from jax.sharding import PartitionSpec as P

MODEL_WIDTH = 2048
HQ = 16
HEAD_WIDTH = 128
FF = 6144
QUERY_PER_KEY = 2
SEQUENCE_TOKENS = 2048


norm_eps = 1e-06
rope_base = 1000000.0
beta_one = 0.5
beta_two = 0.55
step_count = 5.0
adam_eps = 1e-08
decay_rate = 0.1
gain_rate = 0.3
masked_score = -1e30
log2_e = 1.4426950408889634


def rms_gain(values, gain_row):
    return (
        values * lax.rsqrt(jnp.mean(values * values, axis=-1, keepdims=True) + norm_eps) * gain_row
    )


def rotary_tables(length, width):
    frequency = rope_base ** (
        -2.0 * jnp.arange(width // 2, dtype=jnp.int32).astype(jnp.float32) / width
    )
    angles = jnp.arange(length, dtype=jnp.int32).astype(jnp.float32)[:, None] * frequency[None, :]
    cos, sin = jnp.cos(angles), jnp.sin(angles)
    return jnp.concatenate([cos, cos], axis=1), jnp.concatenate([-sin, sin], axis=1)


def contract_rows(left, right):
    return lax.dot_general(
        left, right, (((0,), (0,)), ((), ())), preferred_element_type=jnp.float32
    )


def contract_cols(left, right):
    return lax.dot_general(
        left, right, (((1,), (1,)), ((), ())), preferred_element_type=jnp.float32
    )


def product(left, right):
    return jnp.dot(left, right, preferred_element_type=jnp.float32)


def adamw(weight, gradient, mean_old, square_old, rate):
    mean_new = beta_one * mean_old + (1.0 - beta_one) * gradient
    square_new = beta_two * square_old + (1.0 - beta_two) * gradient * gradient
    mean_hat = mean_new / (1.0 - beta_one**step_count)
    square_hat = square_new / (1.0 - beta_two**step_count)
    weight_new = weight - rate * (
        mean_hat / (jnp.sqrt(square_hat) + adam_eps) + decay_rate * weight
    )
    return (weight_new, square_new)


def ring_place(index, size):
    return jnp.where(index < size // 2, index, size // 2 + size - 1 - index)


def ring_pairs(size):
    half = size // 2
    order = list(range(half)) + list(range(size - 1, half - 1, -1))
    ahead = [(order[r], order[(r + 1) % size]) for r in range(size)]
    return ahead, [(b, a) for a, b in ahead]


def ring_offsets(size):
    offsets = [0]
    for step in range(1, size // 2):
        offsets += [step, -step]
    return offsets + [size // 2]


class Order:
    def __init__(self):
        self.last = ()

    def turn(self, *values):
        tied = lax.optimization_barrier(values + self.last)[: len(values)]
        return tied[0] if len(values) == 1 else tied

    def mark(self, *values):
        self.last = values
        return values[0] if len(values) == 1 else values


def ring_near(blocks, size, work, order, hold=()):
    ahead, back = ring_pairs(size)
    tie = lax.optimization_barrier
    groups = [list(blocks)]
    left, right = list(blocks), list(blocks)
    work(0, list(blocks))
    for step in range(1, size // 2):
        left_low = lax.ppermute(left[0], "tensor", ahead)
        right_high = lax.ppermute(right[1], "tensor", back)
        left_high = lax.ppermute(left[1], "tensor", ahead)
        right_low = lax.ppermute(right[0], "tensor", back)
        held = tuple(hold) if step == size // 2 - 1 else ()
        left_low, right_high = tie((left_low, right_high) + held + order.last)[:2]
        left, right = [left_low, left_high], [right_low, right_high]
        pair = tie((*right, *left) + order.last)[:4]
        groups.append(list(pair))
        work(step, list(pair))
    return groups, (left[0], right[1])


def ring_far(groups, carried, size, work, order):
    ahead, back = ring_pairs(size)
    low = lax.ppermute(carried[0], "tensor", ahead)
    high = lax.ppermute(carried[1], "tensor", back)
    groups.append(list(lax.optimization_barrier((low, high) + order.last)[:2]))
    work(size // 2, list(groups[-1]))
    return groups


def ring_gather(blocks, size, work, order, hold=()):
    groups, carried = ring_near(blocks, size, work, order, hold)
    return ring_far(groups, carried, size, work, order)


def relay_kernel(count, *refs):
    for i in range(count):
        refs[2 * count + i][...] = (
            refs[i][...].astype(jnp.float32) + refs[count + i][...].astype(jnp.float32)
        ).astype(jnp.bfloat16)


def relay(terms, got):
    rows, width = terms[0].shape
    spec = pl.BlockSpec((rows, tile_of(width, 512)), lambda i: (0, i))
    count = len(terms)
    return pl.pallas_call(
        lambda *refs: relay_kernel(count, *refs),
        grid=(width // tile_of(width, 512),),
        in_specs=[spec] * (2 * count),
        out_specs=[spec] * count,
        out_shape=[jax.ShapeDtypeStruct((rows, width), jnp.bfloat16)] * count,
        compiler_params=kernel_params(),
        cost_estimate=SMALL_COST,
        name="relay",
    )(*terms, *got)


def ring_scatter(
    size, part, order, hold=(), first=(), between=None, after=None, got=None, came=None,
    eager=True,
):
    ahead, back = ring_pairs(size)
    send = lambda value, pairs: lax.ppermute(value, "tensor", pairs)
    low, high = part(size // 2)
    if hold:
        low, high = lax.optimization_barrier((low, high) + tuple(hold))[:2]
    from_left, from_right = [send(low, ahead), None], [None, send(high, back)]
    for step in range(size // 2 - 1, 0, -1):
        right_low, right_high, left_low, left_high = part(step)
        full = from_left[1] is not None
        if not full:
            if eager:
                early = send(right_high, ahead), send(left_low, back)
            if between is not None:
                between()
        arrived = [from_left[0], from_right[1]] + ([from_left[1], from_right[0]] if full else [])
        waited = (*first, *early) if eager and not full else tuple(first)
        if came is not None and not full:
            came[:] = arrived
        tied = order.turn(*arrived, *waited)
        arrived = tied[: len(arrived)]
        if eager and not full:
            early = tied[len(tied) - 2 :]
        terms = [right_low, left_high] + ([right_high, left_low] if full else [])
        passed = order.mark(*relay(terms, arrived))
        if got is not None:
            got[:] = passed
        if full:
            early = send(passed[2], ahead), send(passed[3], back)
        elif not eager:
            right_high, left_low = order.turn(right_high, left_low)
            early = send(right_high, ahead), send(left_low, back)
        from_left = [send(passed[0], ahead), early[0]]
        from_right = [early[1], send(passed[1], back)]
    if after is not None:
        after()
    own = part(0)
    if size == 2:
        return own, [from_left[0]], [from_right[1]]
    return own, [from_left[0], from_right[0]], [from_left[1], from_right[1]]


def sum_over(values, axis, beside=()):
    size = lax.axis_size(axis)
    if size & (size - 1):
        return lax.psum(values, axis)
    reach, beside = 1, list(beside)
    while reach < size:
        pairs = [(i, i ^ reach) for i in range(size)]
        values = values + lax.ppermute(values, axis, pairs)
        if beside:
            values = lax.optimization_barrier((values, beside.pop(0)))[0]
        reach *= 2
    return values


def tile_of(width, most):
    return next(t for t in (most, 512, 256, 128) if t <= most and width % t == 0)


def kernel_params(mebibytes=56):
    return pltpu.CompilerParams(vmem_limit_bytes=mebibytes * 1024 * 1024)


SMALL_COST = pl.CostEstimate(flops=1_000_000, bytes_accessed=1_000_000, transcendentals=0)


class Piece:
    def __init__(self, array, count=None, index=0, entry=None):
        self.array, self.count = array, count or array.shape[0]
        self.index, self.entry = index, entry

    def row(self, table):
        return self.index if self.entry is None else table[self.entry]

    def spec(self, width=None):
        if width is None:
            return pl.BlockSpec(
                (self.count, self.array.shape[1]),
                lambda i, table: (self.row(table), 0),
                pipeline_mode=pl.Buffered(1),
            )
        return pl.BlockSpec((self.count, width), lambda i, table: (self.row(table), i))


def pieces_of(blocks):
    return [Piece(block) for block in blocks]


def stacked(refs):
    values = [ref[...] for ref in refs]
    return values[0] if len(values) == 1 else jnp.concatenate(values, axis=0)


def row_call(
    kernel, name, table, grid, operands, specs, outs, out_specs, aliases=None, mebibytes=56
):
    return pl.pallas_call(
        kernel,
        grid_spec=pltpu.PrefetchScalarGridSpec(
            num_scalar_prefetch=1, grid=grid, in_specs=specs, out_specs=out_specs
        ),
        out_shape=outs,
        input_output_aliases=aliases or {},
        compiler_params=kernel_params(mebibytes),
        cost_estimate=SMALL_COST,
        name=name,
    )(table, *operands)


def product_kernel(count, crossed, *refs):
    rows = stacked(refs[1 : 1 + count])
    matrix = refs[1 + count][...]
    result = contract_cols(rows, matrix) if crossed else product(rows, matrix)
    size = refs[-1].shape[0]
    outs = refs[-(rows.shape[0] // size) :]
    for i, out_ref in enumerate(outs):
        out_ref[...] = result[i * size : (i + 1) * size].astype(out_ref.dtype)


def block_product(table, pieces, matrix, crossed, parts=1, into=None):
    width = matrix.shape[0] if crossed else matrix.shape[1]
    tile = tile_of(width, 512)
    count = sum(piece.count for piece in pieces)
    if crossed:
        matrix_spec = pl.BlockSpec((tile, matrix.shape[1]), lambda i, table: (i, 0))
    else:
        matrix_spec = pl.BlockSpec((matrix.shape[0], tile), lambda i, table: (0, i))
    operands = [piece.array for piece in pieces] + [matrix]
    specs = [piece.spec() for piece in pieces] + [matrix_spec]
    aliases = {}
    index, all_rows = 0, count
    if into is not None:
        all_rows, index, so_far = into
        if so_far is not None:
            operands.append(so_far)
            specs.append(pl.BlockSpec(memory_space=pltpu.HBM))
            aliases = {len(operands): 0}
    if parts > 1:
        count = all_rows = count // parts
    out_spec = pl.BlockSpec((count, tile), lambda i, table: (index, i))
    out = jax.ShapeDtypeStruct((all_rows, width), jnp.bfloat16)
    result = row_call(
        lambda *refs: product_kernel(len(pieces), crossed, *refs),
        "block_product",
        table,
        (width // tile,),
        operands,
        specs,
        [out] * parts,
        [out_spec] * parts,
        aliases,
        56 if matrix.size > 4 * 1024 * 1024 else 32,
    )
    return result if parts > 1 else result[0]


def gate_kernel(count, *refs):
    rows = stacked(refs[1 : 1 + count])
    gate_ref, up_ref, activated_ref, gate_out, up_out = refs[1 + count :]
    gate = product(rows, gate_ref[...])
    up = product(rows, up_ref[...])
    activated_ref[...] = (gate * jax.nn.sigmoid(gate) * up).astype(jnp.bfloat16)
    gate_out[...] = gate.astype(gate_out.dtype)
    up_out[...] = up.astype(up_out.dtype)


def gate_up_product(table, pieces, matrix):
    depth, width = matrix.shape[0], matrix.shape[1] // 2
    count = sum(piece.count for piece in pieces)
    tile = tile_of(width, 256)
    steps = width // tile
    return row_call(
        lambda *refs: gate_kernel(len(pieces), *refs),
        "gate_up",
        table,
        (steps,),
        [piece.array for piece in pieces] + [matrix, matrix],
        [piece.spec() for piece in pieces]
        + [
            pl.BlockSpec((depth, tile), lambda i, table: (0, i)),
            pl.BlockSpec((depth, tile), lambda i, table: (0, steps + i)),
        ],
        [jax.ShapeDtypeStruct((count, width), jnp.bfloat16)] * 3,
        [pl.BlockSpec((count, tile), lambda i, table: (0, i))] * 3,
    )


def gate_grad_kernel(count, *refs):
    rows = stacked(refs[1 : 1 + count])
    down_ref, gate_ref, up_ref, out_ref = refs[1 + count :]
    step = pl.program_id(0)
    tile = gate_ref.shape[1]
    width = out_ref.shape[1] // 2
    grad = contract_cols(rows, down_ref[...])
    gate = gate_ref[...].astype(jnp.float32)
    up = up_ref[...].astype(jnp.float32)
    sigmoid_gate = jax.nn.sigmoid(gate)
    scaled = grad * sigmoid_gate
    start = pl.multiple_of(step * tile, tile)
    out_ref[:, pl.ds(start, tile)] = (
        scaled * up * (1.0 + gate * (1.0 - sigmoid_gate))
    ).astype(jnp.bfloat16)
    out_ref[:, pl.ds(pl.multiple_of(width + step * tile, tile), tile)] = (scaled * gate).astype(
        jnp.bfloat16
    )


def gate_up_gradient(table, pieces, down, gate, up):
    count, width = gate.shape
    tile = tile_of(width, 256)
    part = pl.BlockSpec((count, tile), lambda i, table: (0, i))
    return row_call(
        lambda *refs: gate_grad_kernel(len(pieces), *refs),
        "gate_up_grad",
        table,
        (width // tile,),
        [piece.array for piece in pieces] + [down, gate, up],
        [piece.spec() for piece in pieces]
        + [pl.BlockSpec((tile, down.shape[1]), lambda i, table: (i, 0)), part, part],
        [jax.ShapeDtypeStruct((count, 2 * width), jnp.bfloat16)],
        [pl.BlockSpec((count, 2 * width), lambda i, table: (0, 0))],
    )[0]


def rows_kernel(count, weighed, *refs):
    out_ref = refs[2 * count + 1 + weighed]
    result = sum(contract_rows(refs[1 + i][...], refs[1 + count + i][...]) for i in range(count))
    out_ref[...] = result.astype(out_ref.dtype)
    if weighed:
        by_column = jnp.transpose(result * refs[2 * count + 1][...].astype(jnp.float32))
        refs[-1][...] = jnp.sum(by_column, axis=0, keepdims=True)


def weight_gradient(table, lefts, rights, weights=None):
    width, columns = lefts[0].array.shape[1], rights[0].array.shape[1]
    tile = tile_of(width, 256)
    weighed = weights is not None
    block_spec = pl.BlockSpec((tile, columns), lambda i, table: (i, 0))
    result = row_call(
        lambda *refs: rows_kernel(len(lefts), weighed, *refs),
        "weight_grad",
        table,
        (width // tile,),
        [piece.array for piece in lefts + rights] + ([weights] if weighed else []),
        [piece.spec(tile) for piece in lefts]
        + [piece.spec() for piece in rights]
        + ([block_spec] if weighed else []),
        [jax.ShapeDtypeStruct((width, columns), jnp.bfloat16)]
        + ([jax.ShapeDtypeStruct((1, width), jnp.float32)] if weighed else []),
        [block_spec] + ([pl.BlockSpec((1, tile), lambda i, table: (0, i))] if weighed else []),
    )
    return result if weighed else result[0]


def split_groups(groups, half):
    return [
        Piece(array, half, i) for array in groups for i in range(array.shape[0] // half)
    ]


def arrived_sum(split, low_refs, high_refs):
    low = sum(ref[...].astype(jnp.float32) for ref in low_refs)
    high = sum(ref[...].astype(jnp.float32) for ref in high_refs)
    return jnp.where(pl.program_id(0) < split, low, high)


def half_specs(tile, split, width):
    return (
        pl.BlockSpec((tile, width), lambda i: (jnp.minimum(i, split - 1), 0)),
        pl.BlockSpec((tile, width), lambda i: (jnp.maximum(i - split, 0), 0)),
    )


def put_half(split, low_ref, high_ref, value):
    @pl.when(pl.program_id(0) < split)
    def _():
        low_ref[...] = value

    @pl.when(pl.program_id(0) >= split)
    def _():
        high_ref[...] = value


def row_kernel_call(kernel, name, whole, lows, highs, gain, outs):
    rows, width = whole[0].shape
    tile = min(rows // 2, 128)
    split = rows // 2 // tile
    spec = pl.BlockSpec((tile, width), lambda i: (i, 0))
    low_spec, high_spec = half_specs(tile, split, width)
    row_spec = pl.BlockSpec((1, width), lambda i: (0, 0))
    shapes, specs = [], []
    for out in outs:
        if out == "halves":
            shapes += [jax.ShapeDtypeStruct((rows // 2, width), jnp.bfloat16)] * 2
            specs += [low_spec, high_spec]
        elif out == "row":
            shapes.append(jax.ShapeDtypeStruct((1, width), jnp.float32))
            specs.append(row_spec)
        else:
            shapes.append(jax.ShapeDtypeStruct((rows, width), out))
            specs.append(spec)
    return pl.pallas_call(
        lambda *refs: kernel(split, len(lows), *refs),
        grid=(2 * split,),
        in_specs=[spec] * len(whole)
        + [low_spec] * len(lows)
        + [high_spec] * len(highs)
        + [row_spec],
        out_specs=specs,
        out_shape=shapes,
        compiler_params=kernel_params(),
        cost_estimate=SMALL_COST,
        name=name,
    )(*whole, *lows, *highs, gain)


def add_norm_kernel(split, count, base_ref, own_ref, *refs):
    gain_ref, sum_ref, low_ref, high_ref = refs[2 * count :]
    values = base_ref[...].astype(jnp.float32) + own_ref[...].astype(jnp.float32)
    values = values + arrived_sum(split, refs[:count], refs[count : 2 * count])
    sum_ref[...] = values
    put_half(split, low_ref, high_ref, rms_gain(values, gain_ref[...]).astype(jnp.bfloat16))


def add_and_norm(base, own, lows, highs, gain):
    outs = (jnp.float32, "halves")
    return row_kernel_call(add_norm_kernel, "add_norm", [base, own], lows, highs, gain, outs)


def add_kernel(split, count, base_ref, own_ref, *refs):
    values = base_ref[...].astype(jnp.float32) + own_ref[...].astype(jnp.float32)
    values = values + arrived_sum(split, refs[:count], refs[count : 2 * count])
    refs[-1][...] = values.astype(jnp.bfloat16)


def norm_gradient_kernel(split, count, base_ref, value_ref, own_ref, *refs):
    gain_ref, outs = refs[2 * count], refs[2 * count + 1 :]
    grad = own_ref[...].astype(jnp.float32)
    grad = grad + arrived_sum(split, refs[:count], refs[count : 2 * count])
    values = value_ref[...].astype(jnp.float32)
    scale = lax.rsqrt(jnp.mean(values * values, axis=1, keepdims=True) + norm_eps)
    unit = values * scale
    inner = grad * gain_ref[...]
    result = base_ref[...].astype(jnp.float32) + scale * (
        inner - unit * jnp.mean(inner * unit, axis=1, keepdims=True)
    )
    if len(outs) == 1:
        outs[0][...] = result.astype(jnp.bfloat16)
        return
    low_ref, high_ref, gain_out = outs
    put_half(split, low_ref, high_ref, result.astype(jnp.bfloat16))

    @pl.when(pl.program_id(0) == 0)
    def _():
        gain_out[...] = jnp.zeros_like(gain_out)

    gain_out[...] += jnp.sum(grad * unit, axis=0, keepdims=True)


def norm_gradient(base, values, own, lows, highs, gain, outs):
    return row_kernel_call(
        norm_gradient_kernel, "norm_gradient", [base, values, own], lows, highs, gain, outs
    )


def project_kernel(count, *refs):
    rows = stacked(refs[1 : 1 + count])
    matrix_ref, gain_ref, cos_ref, sin_ref = refs[1 + count : 5 + count]
    query_ref, key_ref, value_ref, query_raw, key_raw = refs[-5:]
    width = HEAD_WIDTH
    mixed = product(rows, matrix_ref[...])
    cos, sin = cos_ref[...], sin_ref[...]
    for part in range(QUERY_PER_KEY + 1):
        values = mixed[:, part * width : (part + 1) * width]
        is_key = part == QUERY_PER_KEY
        gain = gain_ref[1:2, :] if is_key else gain_ref[0:1, :]
        scale = lax.rsqrt(jnp.mean(values * values, axis=1, keepdims=True) + norm_eps)
        scaled = values * scale * gain
        turned = scaled * cos + pltpu.roll(scaled, width // 2, 1) * sin
        if is_key:
            key_ref[...] = turned.astype(jnp.bfloat16)
            key_raw[...] = values
        else:
            query_ref[:, part * width : (part + 1) * width] = turned.astype(jnp.bfloat16)
            query_raw[:, part * width : (part + 1) * width] = values
    value_ref[...] = mixed[:, (QUERY_PER_KEY + 1) * width :].astype(jnp.bfloat16)


def project(blocks, matrix, gains, cos, sin, place, total_rows, before):
    count, depth = sum(block.shape[0] for block in blocks), matrix.shape[0]
    block = (QUERY_PER_KEY + 2) * HEAD_WIDTH
    heads = matrix.shape[1] // block
    wide = QUERY_PER_KEY * HEAD_WIDTH
    per_table = cos.shape[0] // count
    table_spec = pl.BlockSpec(
        (count, HEAD_WIDTH), lambda h, at: (lax.rem(at[0], per_table), 0)
    )
    widths = (wide, HEAD_WIDTH, HEAD_WIDTH, wide, HEAD_WIDTH)
    kinds = (jnp.bfloat16,) * 3 + (jnp.float32,) * 2
    kept = () if before is None else tuple(before)
    return pl.pallas_call(
        lambda *refs: project_kernel(len(blocks), *refs),
        grid_spec=pltpu.PrefetchScalarGridSpec(
            num_scalar_prefetch=1,
            grid=(heads,),
            in_specs=[
                pl.BlockSpec((rows.shape[0], depth), lambda h, at: (0, 0)) for rows in blocks
            ]
            + [
                pl.BlockSpec((depth, block), lambda h, at: (0, h)),
                pl.BlockSpec((2, HEAD_WIDTH), lambda h, at: (0, 0)),
                table_spec,
                table_spec,
            ]
            + [pl.BlockSpec(memory_space=pltpu.HBM)] * len(kept),
            out_specs=[pl.BlockSpec((count, w), lambda h, at: (at[0], h)) for w in widths],
        ),
        out_shape=[
            jax.ShapeDtypeStruct((total_rows, heads * w), kind) for w, kind in zip(widths, kinds)
        ],
        input_output_aliases={5 + len(blocks) + i: i for i in range(len(kept))},
        compiler_params=kernel_params(56),
        cost_estimate=SMALL_COST,
        name="project",
    )(place.reshape(1), *blocks, matrix, gains, cos, sin, *kept)


def attend_kernel(scale, query_ref, key_ref, value_ref, out_ref, log_ref):
    block = query_ref.shape[0]
    width = key_ref.shape[1]
    group = query_ref.shape[1] // width
    step = pl.program_id(2)
    below = lax.broadcasted_iota(jnp.int32, (block, block), 0) <= lax.broadcasted_iota(
        jnp.int32, (block, block), 1
    )
    queries = [query_ref[:, g * width : (g + 1) * width] for g in range(group)]

    def visit(start, carry, masked):
        keys = key_ref[pl.ds(start, block), :]
        values = value_ref[pl.ds(start, block), :]
        new = []
        for g in range(group):
            total, acc = carry[g]
            weights = jnp.exp2(contract_cols(keys, queries[g]) * (scale * log2_e))
            if masked:
                weights = jnp.where(below, weights, 0.0)
            total = total + jnp.sum(weights, axis=0, keepdims=True)
            acc = acc + contract_rows(values, weights.astype(jnp.bfloat16))
            new.append((total, acc))
        return tuple(new)

    start_carry = tuple(
        (jnp.zeros((1, block), jnp.float32), jnp.zeros((width, block), jnp.float32))
        for _ in range(group)
    )
    carry = lax.fori_loop(
        0, step, lambda j, c: visit(pl.multiple_of(j * block, block), c, False), start_carry
    )
    carry = visit(pl.multiple_of(step * block, block), carry, True)
    for g in range(group):
        total, acc = carry[g]
        out_ref[:, g * width : (g + 1) * width] = jnp.transpose(acc / total).astype(jnp.bfloat16)
        log_ref[0, 0, g : g + 1, :] = jnp.log2(total)


def attention_forward(query, key, value, block):
    rows = query.shape[0]
    heads = key.shape[1] // HEAD_WIDTH
    steps = SEQUENCE_TOKENS // block
    wide = QUERY_PER_KEY * HEAD_WIDTH
    sequences = rows // SEQUENCE_TOKENS
    query_spec = pl.BlockSpec((block, wide), lambda h, s, i: (s * steps + i, h))
    key_spec = pl.BlockSpec((SEQUENCE_TOKENS, HEAD_WIDTH), lambda h, s, i: (s, h))
    return pl.pallas_call(
        lambda *refs: attend_kernel(HEAD_WIDTH ** (-0.5), *refs),
        grid=(heads, sequences, steps),
        in_specs=[query_spec, key_spec, key_spec],
        out_specs=[
            query_spec,
            pl.BlockSpec(
                (1, 1, QUERY_PER_KEY, block), lambda h, s, i: (h, s * steps + i, 0, 0)
            ),
        ],
        out_shape=[
            jax.ShapeDtypeStruct(query.shape, jnp.bfloat16),
            jax.ShapeDtypeStruct((heads, rows // block, QUERY_PER_KEY, block), jnp.float32),
        ],
        compiler_params=kernel_params(56),
        cost_estimate=SMALL_COST,
        name="attend",
    )(query, key, value)


def norm_back(values, grad, gain, cos, sin):
    width = values.shape[1]
    turned = grad * cos + pltpu.roll(grad * sin, width // 2, 1)
    scale = lax.rsqrt(jnp.mean(values * values, axis=1, keepdims=True) + norm_eps)
    unit = values * scale
    inner = turned * gain
    back = scale * (inner - unit * jnp.mean(inner * unit, axis=1, keepdims=True))
    return back.astype(jnp.bfloat16), jnp.sum(turned * unit, axis=0, keepdims=True)


def attend_back_kernel(
    scale,
    table_ref,
    query_ref,
    key_ref,
    value_ref,
    grad_ref,
    context_ref,
    log_ref,
    query_raw,
    key_raw,
    gain_ref,
    cos_ref,
    sin_ref,
    *refs,
):
    mixed_out, gain_out, key_sum, value_sum = refs[-4:]
    block = query_ref.shape[0]
    width = key_ref.shape[1]
    group = query_ref.shape[1] // width
    sequence, step = pl.program_id(0), pl.program_id(1)
    below = lax.broadcasted_iota(jnp.int32, (block, block), 0) <= lax.broadcasted_iota(
        jnp.int32, (block, block), 1
    )

    @pl.when(step == 0)
    def _():
        key_sum[...] = jnp.zeros_like(key_sum)
        value_sum[...] = jnp.zeros_like(value_sum)

    @pl.when((step == 0) & (sequence == 0))
    def _():
        gain_out[...] = jnp.zeros_like(gain_out)

    queries, grads, logs, dots = [], [], [], []
    for g in range(group):
        cols = slice(g * width, (g + 1) * width)
        queries.append(query_ref[:, cols])
        grads.append(grad_ref[:, cols])
        logs.append(log_ref[0, 0, g : g + 1, :])
        both = grads[g].astype(jnp.float32) * context_ref[:, cols].astype(jnp.float32)
        dots.append(jnp.sum(jnp.transpose(both), axis=0, keepdims=True))

    def visit(start, carry, masked):
        rows = pl.ds(start, block)
        keys = key_ref[rows, :]
        values = value_ref[rows, :]
        new = []
        key_part = value_part = None
        for g in range(group):
            weights = jnp.exp2(contract_cols(keys, queries[g]) * (scale * log2_e) - logs[g])
            if masked:
                weights = jnp.where(below, weights, 0.0)
            slope = contract_cols(values, grads[g])
            score = (weights * (slope - dots[g])).astype(jnp.bfloat16)
            value_g = product(weights.astype(jnp.bfloat16), grads[g])
            key_g = product(score, queries[g])
            key_part = key_g if key_part is None else key_part + key_g
            value_part = value_g if value_part is None else value_part + value_g
            new.append(carry[g] + contract_rows(keys, score))
        key_sum[rows, :] += key_part
        value_sum[rows, :] += value_part
        return tuple(new)

    carry = tuple(jnp.zeros((width, block), jnp.float32) for _ in range(group))
    carry = lax.fori_loop(
        0, step, lambda j, c: visit(pl.multiple_of(j * block, block), c, False), carry
    )
    carry = visit(pl.multiple_of(step * block, block), carry, True)
    rows = pl.ds(pl.multiple_of(step * block, block), block)
    cos, sin = cos_ref[rows, :], sin_ref[rows, :]
    for g in range(group):
        cols = slice(g * width, (g + 1) * width)
        back, gain = norm_back(
            query_raw[:, cols], jnp.transpose(carry[g]) * scale, gain_ref[0:1, :], cos, sin
        )
        mixed_out[rows, cols] = back
        gain_out[0:1, :] += gain

    @pl.when(step == pl.num_programs(1) - 1)
    def _():
        def finish(j, _):
            rows = pl.ds(pl.multiple_of(j * block, block), block)
            back, gain = norm_back(
                key_raw[rows, :],
                key_sum[rows, :] * scale,
                gain_ref[1:2, :],
                cos_ref[rows, :],
                sin_ref[rows, :],
            )
            mixed_out[rows, group * width : (group + 1) * width] = back
            mixed_out[rows, (group + 1) * width :] = value_sum[rows, :].astype(jnp.bfloat16)
            gain_out[1:2, :] += gain
            return 0

        lax.fori_loop(0, pl.num_programs(1), finish, 0)


def attention_backward(
    slots, query, key, value, grad, context, logs, query_raw, key_raw, gains, cos, sin, head, before
):
    rows = query.shape[0]
    block = logs.shape[-1]
    steps = SEQUENCE_TOKENS // block
    wide = QUERY_PER_KEY * HEAD_WIDTH
    heads = key.shape[1] // HEAD_WIDTH
    sequences = rows // SEQUENCE_TOKENS
    mixed = (QUERY_PER_KEY + 2) * HEAD_WIDTH
    query_spec = pl.BlockSpec((block, wide), lambda s, i, slots: (s * steps + i, head))
    key_spec = pl.BlockSpec((SEQUENCE_TOKENS, HEAD_WIDTH), lambda s, i, slots: (s, head))
    table_spec = pl.BlockSpec((SEQUENCE_TOKENS, HEAD_WIDTH), lambda s, i, slots: (0, 0))
    gain_spec = pl.BlockSpec((2, HEAD_WIDTH), lambda s, i, slots: (0, 0))
    kept = () if before is None else (before,)
    return pl.pallas_call(
        lambda *refs: attend_back_kernel(HEAD_WIDTH ** (-0.5), *refs),
        grid_spec=pltpu.PrefetchScalarGridSpec(
            num_scalar_prefetch=1,
            grid=(sequences, steps),
            in_specs=[
            query_spec,
            key_spec,
            key_spec,
            pl.BlockSpec((block, wide), lambda s, i, slots: (slots[s * steps + i], head)),
            query_spec,
            pl.BlockSpec(
                (1, 1, QUERY_PER_KEY, block), lambda s, i, slots: (head, s * steps + i, 0, 0)
            ),
            query_spec,
            key_spec,
            gain_spec,
            table_spec,
            table_spec,
        ]
        + [pl.BlockSpec(memory_space=pltpu.HBM)] * len(kept),
        out_specs=[
            pl.BlockSpec((SEQUENCE_TOKENS, mixed), lambda s, i, slots: (s, head)),
            gain_spec,
        ],
        scratch_shapes=[pltpu.VMEM((SEQUENCE_TOKENS, HEAD_WIDTH), jnp.float32)] * 2,
        ),
        out_shape=[
            jax.ShapeDtypeStruct((rows, heads * mixed), jnp.bfloat16),
            jax.ShapeDtypeStruct((2, HEAD_WIDTH), jnp.float32),
        ],
        input_output_aliases={12: 0} if kept else {},
        compiler_params=kernel_params(56),
        cost_estimate=SMALL_COST,
        name="attend_back",
    )(slots, query, key, value, grad, context, logs, query_raw, key_raw, gains, cos, sin, *kept)


def local(
    inputs,
    input_projection_weight,
    input_first_moment,
    input_second_moment,
    out_weight,
    out_mean,
    out_square,
    swiglu_weight,
    swiglu_mean,
    swiglu_square,
    down_weight,
    down_mean,
    down_square,
    norm_gains,
    norm_mean,
    norm_square,
    qknorm_gains,
    qknorm_mean,
    qknorm_square,
    cotangent,
):
    size = lax.axis_size("tensor")
    rows = inputs.shape[0]
    half = rows // 2
    group_rows = rows * size
    last = size // 2
    dp_rows = input_projection_weight.shape[0]
    local_kv = input_projection_weight.shape[1]
    local_ff = swiglu_weight.shape[2]
    me = ring_place(lax.axis_index("tensor"), size)
    places = [ring_place((me + d + size) % size, size) for d in ring_offsets(size)]
    group_places = [places[:1]]
    for step in range(1, last):
        group_places.append(places[2 * step - 1 : 2 * step + 1])
    group_places.append(places[-1:])
    halves = [2 * place + i for place in places for i in range(2)]
    table = jnp.stack(places + halves).astype(jnp.int32)
    away = (ring_place(jnp.arange(size, dtype=jnp.int32), size) - me + size) % size
    slots = jnp.where(
        away == 0,
        size - 2,
        jnp.where(
            away == last,
            size - 1,
            jnp.where(away < last, 2 * away - 2, 2 * (size - away) - 1),
        ),
    ).astype(jnp.int32)
    order = Order()
    turn, mark = order.turn, order.mark
    tie = lax.optimization_barrier

    def ordered(array, group):
        entries = [0] if group == 0 else [2 * group - 1, 2 * group]
        if group == last:
            entries = [size - 1]
        return [Piece(array, rows, entry=entry) for entry in entries]

    def ordered_finely(array):
        return [Piece(array, half, entry=size + i) for i in range(2 * size)]

    def flat(groups):
        return pieces_of([block for group in groups for block in group])

    def parts_of(group):
        return 1 if group == 0 else 2 if group == last else 4

    def marked(part):
        return mark(*part) if isinstance(part, (list, tuple)) else mark(part)

    in_low = input_projection_weight.astype(jnp.bfloat16).reshape(dp_rows, -1)
    out_low = out_weight.astype(jnp.bfloat16)
    swiglu_low = swiglu_weight.astype(jnp.bfloat16).reshape(dp_rows, 2 * local_ff)
    down_low = down_weight.astype(jnp.bfloat16)
    in_matrix = lax.all_gather(in_low, "dp", axis=0, tiled=True)
    out_full = lax.all_gather(out_low, "dp", axis=1, tiled=True)
    swiglu_matrix = lax.all_gather(swiglu_low, "dp", axis=0, tiled=True)
    down_full = lax.all_gather(down_low, "dp", axis=1, tiled=True)

    normed_f = rms_gain(inputs.astype(jnp.float32), norm_gains[0])
    cos, sin = rotary_tables(SEQUENCE_TOKENS, HEAD_WIDTH)
    projected = []

    def project_group(group, blocks):
        calls = [blocks] if group in (0, last) else [blocks[:2], blocks[2:]]
        for place, call in zip(group_places[group], calls):
            call[0] = turn(call[0])
            projected[:] = mark(
                *project(
                    call, in_matrix, qknorm_gains, cos, sin, place, group_rows, projected or None
                )
            )

    normed = normed_f.astype(jnp.bfloat16)
    normed_groups = ring_gather(
        (normed[:half], normed[half:]), size, project_group, order, hold=(in_matrix,)
    )
    query, key, value, query_raw, key_raw = projected
    cotangent_sent = tie((cotangent, *normed_groups[-1]))[0]

    context, logs = mark(*attention_forward(query, key, value, rows))
    cot_groups, cot_carried = ring_near(
        (cotangent_sent[:half], cotangent_sent[half:]), size, lambda group, blocks: None, Order()
    )

    def out_group(group):
        return marked(
            block_product(
                table, ordered(turn(context), group), out_full, False, parts_of(group)
            )
        )

    own, lows, highs = ring_scatter(
        size, out_group, order, first=[half for group in cot_groups[1:] for half in group]
    )
    lows, highs = tie((lows, highs, swiglu_matrix))[:2]
    hidden, *two_halves = mark(*add_and_norm(inputs, own, lows, highs, norm_gains[1:2]))

    gate_groups = []
    grads = [None] * (last + 1)

    def gate_group(group, blocks):
        blocks[0] = turn(blocks[0])
        gate_groups.append(mark(*gate_up_product(table, pieces_of(blocks), swiglu_matrix)))

    two_groups, two_carried = ring_near(two_halves, size, gate_group, order)
    two_groups = ring_far(two_groups, two_carried, size, gate_group, order)
    cot_carried = tie((*cot_carried, *gate_groups[last - 1]))[:2]
    cot_groups = ring_far(cot_groups, cot_carried, size, lambda group, blocks: None, order)
    activated = [parts[0] for parts in gate_groups]
    two_parts = [None] * (last + 1)

    def two_grads(group):
        cots = [turn(cot_groups[group][0])] + cot_groups[group][1:]
        grads[group] = mark(
            gate_up_gradient(table, pieces_of(cots), down_full, *gate_groups[group][1:])
        )

    def two_product(group):
        two_parts[group] = marked(
            block_product(
                table, [Piece(turn(grads[group]))], swiglu_matrix, True, parts_of(group)
            )
        )

    for group in range(1, last):
        two_grads(group)
    lefts = split_groups([turn(activated[0])] + activated[1:], half)
    down_part = mark(weight_gradient(table, lefts, flat(cot_groups)))
    down_grad = lax.psum_scatter(down_part, "dp", scatter_dimension=1, tiled=True)
    for group in range(1, last):
        two_product(group)
    two_grads(last)
    two_product(last)
    more = []

    def own_part():
        two_grads(0)
        two_product(0)

    def swiglu_gradient():
        twos = flat(two_groups)
        twos[0].array = turn(twos[0].array)
        more.append(mark(weight_gradient(table, twos, split_groups(grads, half))))

    if last == 1:
        own_part()
    own, lows, highs = ring_scatter(
        size, lambda group: two_parts[group], order, between=own_part, after=swiglu_gradient
    )
    swiglu_part, lows, highs = tie((more[0], lows, highs))
    swiglu_grad = lax.psum_scatter(swiglu_part, "dp", scatter_dimension=0, tiled=True)
    *attended_halves, mlp_gain_grad = mark(
        *norm_gradient(
            cotangent, hidden, own, lows, highs, norm_gains[1:2], ("halves", "row")
        )
    )

    context_grad, down_parts, new_down, head_grads = [None], [None] * (last + 1), [], []

    def context_group(group, blocks):
        blocks[0] = turn(blocks[0])
        index = size - 2 if group == 0 else size - 1 if group == last else group - 1
        context_grad[0] = mark(
            block_product(
                table, pieces_of(blocks), out_full, True, into=(group_rows, index, context_grad[0])
            )
        )
        if group == 0:
            for other in range(last, -1, -1):
                down_parts[other] = marked(
                    block_product(
                        table, [Piece(turn(activated[other]))], down_full, False, parts_of(other)
                    )
                )
            new_down[:] = mark(
                turn(down_grad).astype(jnp.float32),
                *adamw(
                    down_weight,
                    turn(down_grad).astype(jnp.float32),
                    down_mean,
                    down_square,
                    FF ** (-0.5),
                ),
            )

    attended_groups = ring_gather(attended_halves, size, context_group, order)

    def head_backward(head):
        head_grads.append(
            mark(
                *attention_backward(
                    slots, turn(query), key, value, context_grad[0], context, logs, query_raw,
                    key_raw, qknorm_gains, cos, sin, head,
                    head_grads[-1][0] if head_grads else None,
                )
            )
        )

    out_part = mark(
        weight_gradient(table, ordered_finely(turn(context)), flat(attended_groups))
    )
    if last == 1:
        head_backward(0)

    def other_heads():
        for head in range(1, local_kv):
            head_backward(head)

    own, lows, highs = ring_scatter(
        size,
        lambda group: down_parts[group],
        order,
        hold=attended_groups[-1],
        between=lambda: head_backward(0),
        after=other_heads,
    )
    (outputs,) = row_kernel_call(
        add_kernel, "add", [hidden, own], lows, highs, norm_gains[0:1], (jnp.bfloat16,)
    )
    sent = lows + highs
    mixed_grad = head_grads[-1][0]
    qknorm_part = sum(pair[1] for pair in head_grads)
    in_parts = []

    def normed_group(group):
        return marked(
            block_product(
                table, ordered(turn(mixed_grad), group), in_matrix, True, parts_of(group)
            )
        )

    def in_gradient():
        normeds = flat(normed_groups)
        normeds[0].array = turn(normeds[0].array)
        in_parts[:] = mark(
            *weight_gradient(table, normeds, ordered_finely(mixed_grad), in_matrix)
        )

    got, came = [], []
    own, lows, highs = ring_scatter(
        size, normed_group, order, between=in_gradient, got=got, came=came, eager=False
    )
    if not in_parts:
        in_gradient()
    rows_of_gains = jnp.concatenate([in_parts[1] / norm_gains[0:1], mlp_gain_grad], axis=0)
    gain_sums = tie((jnp.concatenate([rows_of_gains, qknorm_part], axis=1), *got))[0]
    gain_sums = sum_over(gain_sums, "tensor")
    out_part, down_grad = tie((out_part, down_grad, *sent, mixed_grad))[:2]
    out_grad = lax.psum_scatter(out_part, "dp", scatter_dimension=1, tiled=True)
    in_part, swiglu_grad = tie((in_parts[0], swiglu_grad, *came))[:2]
    in_grad = lax.psum_scatter(in_part, "dp", scatter_dimension=0, tiled=True)
    in_grad = in_grad.astype(jnp.float32).reshape(input_projection_weight.shape)
    out_grad, swiglu_grad, outputs = tie((out_grad, swiglu_grad, outputs, *got))[:3]
    out_grad = out_grad.astype(jnp.float32)
    swiglu_grad = swiglu_grad.astype(jnp.float32).reshape(swiglu_weight.shape)
    out_new, out_second = adamw(
        out_weight, out_grad, out_mean, out_square, (HQ * HEAD_WIDTH / 8.0) ** (-0.5)
    )
    swiglu_new, swiglu_second = adamw(
        swiglu_weight, swiglu_grad, swiglu_mean, swiglu_square, MODEL_WIDTH ** (-0.5)
    )
    down_grad, down_new, down_second = new_down
    (
        lows,
        highs,
        own,
        outputs,
        out_grad,
        out_new,
        out_second,
        swiglu_grad,
        swiglu_new,
        swiglu_second,
    ) = tie(
        (
            lows,
            highs,
            own,
            outputs,
            out_grad,
            out_new,
            out_second,
            swiglu_grad,
            swiglu_new,
            swiglu_second,
        )
    )
    hidden_grad = jnp.concatenate(attended_halves, axis=0)
    (input_grad,) = norm_gradient(
        hidden_grad, inputs, own, lows, highs, norm_gains[0:1], (jnp.bfloat16,)
    )
    in_new, in_second = adamw(
        input_projection_weight,
        in_grad,
        input_first_moment,
        input_second_moment,
        MODEL_WIDTH ** (-0.5),
    )
    gain_sums = sum_over(tie((gain_sums, *lows, *highs))[0], "dp", (input_grad, in_new))
    norm_grad, qknorm_grad = gain_sums[:, :MODEL_WIDTH], gain_sums[:, MODEL_WIDTH:]
    norm_new, norm_second = adamw(norm_gains, norm_grad, norm_mean, norm_square, gain_rate)
    qknorm_new, qknorm_second = adamw(
        qknorm_gains, qknorm_grad, qknorm_mean, qknorm_square, gain_rate
    )
    return (
        outputs,
        input_grad,
        in_grad,
        in_new,
        in_second,
        out_grad,
        out_new,
        out_second,
        swiglu_grad,
        swiglu_new,
        swiglu_second,
        down_grad,
        down_new,
        down_second,
        norm_grad,
        norm_new,
        norm_second,
        qknorm_grad,
        qknorm_new,
        qknorm_second,
    )


def solution(mesh):
    return jax.shard_map(
        local,
        mesh=mesh,
        in_specs=(
            P(("dp", "tensor"), None),
            P("dp", "tensor", None),
            P("dp", "tensor", None),
            P("dp", "tensor", None),
            P("tensor", "dp"),
            P("tensor", "dp"),
            P("tensor", "dp"),
            P("dp", None, "tensor"),
            P("dp", None, "tensor"),
            P("dp", None, "tensor"),
            P("tensor", "dp"),
            P("tensor", "dp"),
            P("tensor", "dp"),
            P(),
            P(),
            P(),
            P(),
            P(),
            P(),
            P(("dp", "tensor"), None),
        ),
        out_specs=(
            P(("dp", "tensor"), None),
            P(("dp", "tensor"), None),
            P("dp", "tensor", None),
            P("dp", "tensor", None),
            P("dp", "tensor", None),
            P("tensor", "dp"),
            P("tensor", "dp"),
            P("tensor", "dp"),
            P("dp", None, "tensor"),
            P("dp", None, "tensor"),
            P("dp", None, "tensor"),
            P("tensor", "dp"),
            P("tensor", "dp"),
            P("tensor", "dp"),
            P(),
            P(),
            P(),
            P(),
            P(),
            P(),
        ),
        check_vma=False,
    )
```

```python
import jax
import jax.numpy as jnp
from jax import lax
from jax.experimental import pallas as pl
from jax.experimental.pallas import tpu as pltpu
from jax.sharding import PartitionSpec as P

MODEL_WIDTH = 2048
HQ = 16
HEAD_WIDTH = 128
FF = 6144
QUERY_PER_KEY = 2
SEQUENCE_TOKENS = 2048


norm_eps = 1e-06
rope_base = 1000000.0
beta_one = 0.5
beta_two = 0.55
step_count = 5.0
adam_eps = 1e-08
decay_rate = 0.1
gain_rate = 0.3
masked_score = -1e30
log2_e = 1.4426950408889634


def rms_gain(values, gain_row):
    return (
        values * lax.rsqrt(jnp.mean(values * values, axis=-1, keepdims=True) + norm_eps) * gain_row
    )


def rotary_tables(length, width):
    frequency = rope_base ** (
        -2.0 * jnp.arange(width // 2, dtype=jnp.int32).astype(jnp.float32) / width
    )
    angles = jnp.arange(length, dtype=jnp.int32).astype(jnp.float32)[:, None] * frequency[None, :]
    cos, sin = jnp.cos(angles), jnp.sin(angles)
    return jnp.concatenate([cos, cos], axis=1), jnp.concatenate([-sin, sin], axis=1)


def contract_rows(left, right):
    return lax.dot_general(
        left, right, (((0,), (0,)), ((), ())), preferred_element_type=jnp.float32
    )


def contract_cols(left, right):
    return lax.dot_general(
        left, right, (((1,), (1,)), ((), ())), preferred_element_type=jnp.float32
    )


def product(left, right):
    return jnp.dot(left, right, preferred_element_type=jnp.float32)


def adamw(weight, gradient, mean_old, square_old, rate):
    mean_new = beta_one * mean_old + (1.0 - beta_one) * gradient
    square_new = beta_two * square_old + (1.0 - beta_two) * gradient * gradient
    mean_hat = mean_new / (1.0 - beta_one**step_count)
    square_hat = square_new / (1.0 - beta_two**step_count)
    weight_new = weight - rate * (
        mean_hat / (jnp.sqrt(square_hat) + adam_eps) + decay_rate * weight
    )
    return (weight_new, square_new)


def adam_kernel(rate, weight_ref, mean_ref, square_ref, *refs):
    *grad_refs, grad_out, new_out, second_out = refs
    width = weight_ref.shape[2]
    for part in range(weight_ref.shape[1]):
        start = part * width
        for grad_ref in grad_refs:
            if start < grad_ref.shape[1]:
                break
            start -= grad_ref.shape[1]
        grad = grad_ref[:, start : start + width].astype(jnp.float32)
        new, second = adamw(
            weight_ref[:, part, :], grad, mean_ref[:, part, :], square_ref[:, part, :], rate
        )
        grad_out[:, part, :] = grad
        new_out[:, part, :] = new
        second_out[:, part, :] = second


def adamw_parts(weight, grads, mean_old, square_old, rate):
    rows, parts, width = weight.shape
    tile = min(rows, 64)
    spec = pl.BlockSpec((tile, parts, width), lambda i: (i, 0, 0))
    return pl.pallas_call(
        lambda *refs: adam_kernel(rate, *refs),
        grid=(rows // tile,),
        in_specs=[spec] * 3
        + [pl.BlockSpec((tile, grad.shape[1]), lambda i: (i, 0)) for grad in grads],
        out_specs=[spec] * 3,
        out_shape=[jax.ShapeDtypeStruct(weight.shape, jnp.float32)] * 3,
        compiler_params=kernel_params(),
        cost_estimate=SMALL_COST,
        name="adamw",
    )(weight, mean_old, square_old, *grads)


def ring_place(index, size):
    return jnp.where(index < size // 2, index, size // 2 + size - 1 - index)


def ring_pairs(size):
    half = size // 2
    order = list(range(half)) + list(range(size - 1, half - 1, -1))
    ahead = [(order[r], order[(r + 1) % size]) for r in range(size)]
    return ahead, [(b, a) for a, b in ahead]


def ring_offsets(size):
    offsets = [0]
    for step in range(1, size // 2):
        offsets += [step, -step]
    return offsets + [size // 2]


class Order:
    def __init__(self):
        self.last = ()

    def turn(self, *values):
        tied = lax.optimization_barrier(values + self.last)[: len(values)]
        return tied[0] if len(values) == 1 else tied

    def mark(self, *values):
        self.last = values
        return values[0] if len(values) == 1 else values


def ring_near(blocks, size, work, order, hold=()):
    ahead, back = ring_pairs(size)
    tie = lax.optimization_barrier
    groups = [list(blocks)]
    left, right = list(blocks), list(blocks)
    work(0, list(blocks))
    for step in range(1, size // 2):
        left_low = lax.ppermute(left[0], "tensor", ahead)
        right_high = lax.ppermute(right[1], "tensor", back)
        left_high = lax.ppermute(left[1], "tensor", ahead)
        right_low = lax.ppermute(right[0], "tensor", back)
        held = tuple(hold) if step == size // 2 - 1 else ()
        left_low, right_high = tie((left_low, right_high) + held + order.last)[:2]
        left, right = [left_low, left_high], [right_low, right_high]
        pair = tie((*right, *left) + order.last)[:4]
        groups.append(list(pair))
        work(step, list(pair))
    return groups, (left[0], right[1])


def ring_far(groups, carried, size, work, order):
    ahead, back = ring_pairs(size)
    low = lax.ppermute(carried[0], "tensor", ahead)
    high = lax.ppermute(carried[1], "tensor", back)
    groups.append(list(lax.optimization_barrier((low, high) + order.last)[:2]))
    work(size // 2, list(groups[-1]))
    return groups


def ring_gather(blocks, size, work, order, hold=()):
    groups, carried = ring_near(blocks, size, work, order, hold)
    return ring_far(groups, carried, size, work, order)


def relay_kernel(count, *refs):
    for i in range(count):
        refs[2 * count + i][...] = (
            refs[i][...].astype(jnp.float32) + refs[count + i][...].astype(jnp.float32)
        ).astype(jnp.bfloat16)


def relay(terms, got):
    rows, width = terms[0].shape
    tile = min(rows, 64)
    spec = pl.BlockSpec((tile, width), lambda i: (i, 0))
    count = len(terms)
    return pl.pallas_call(
        lambda *refs: relay_kernel(count, *refs),
        grid=(rows // tile,),
        in_specs=[spec] * (2 * count),
        out_specs=[spec] * count,
        out_shape=[jax.ShapeDtypeStruct((rows, width), jnp.bfloat16)] * count,
        compiler_params=kernel_params(),
        cost_estimate=SMALL_COST,
        name="relay",
    )(*terms, *got)


def ring_scatter(
    size, part, order, hold=(), first=(), between=None, after=None, got=None, came=None,
    eager=True,
):
    ahead, back = ring_pairs(size)
    send = lambda value, pairs: lax.ppermute(value, "tensor", pairs)
    low, high = part(size // 2)
    if hold:
        low, high = lax.optimization_barrier((low, high) + tuple(hold))[:2]
    from_left, from_right = [send(low, ahead), None], [None, send(high, back)]
    for step in range(size // 2 - 1, 0, -1):
        right_low, right_high, left_low, left_high = part(step)
        full = from_left[1] is not None
        if not full:
            if eager:
                early = send(right_high, ahead), send(left_low, back)
            if between is not None:
                between()
        arrived = [from_left[0], from_right[1]] + ([from_left[1], from_right[0]] if full else [])
        waited = (*first, *early) if eager and not full else tuple(first)
        if came is not None and not full:
            came[:] = arrived
        tied = order.turn(*arrived, *waited)
        arrived = tied[: len(arrived)]
        if eager and not full:
            early = tied[len(tied) - 2 :]
        terms = [right_low, left_high] + ([right_high, left_low] if full else [])
        passed = order.mark(*relay(terms, arrived))
        if got is not None:
            got[:] = passed
        if full:
            early = send(passed[2], ahead), send(passed[3], back)
        elif not eager:
            right_high, left_low = order.turn(right_high, left_low)
            early = send(right_high, ahead), send(left_low, back)
        from_left = [send(passed[0], ahead), early[0]]
        from_right = [early[1], send(passed[1], back)]
    if after is not None:
        after()
    own = part(0)
    if size == 2:
        return own, [from_left[0]], [from_right[1]]
    return own, [from_left[0], from_right[0]], [from_left[1], from_right[1]]


def sum_over(values, axis, beside=()):
    size = lax.axis_size(axis)
    if size & (size - 1):
        return lax.psum(values, axis)
    reach, beside = 1, list(beside)
    while reach < size:
        ways = 4 if size >= 4 * reach else 2
        values = values + sum(
            lax.ppermute(values, axis, [(i, i ^ (way * reach)) for i in range(size)])
            for way in range(1, ways)
        )
        if beside:
            values = lax.optimization_barrier((values, beside.pop(0)))[0]
        reach *= ways
    return values


def tile_of(width, most):
    return next(t for t in (most, 512, 256, 128) if t <= most and width % t == 0)


def kernel_params(mebibytes=56):
    return pltpu.CompilerParams(vmem_limit_bytes=mebibytes * 1024 * 1024)


SMALL_COST = pl.CostEstimate(flops=1_000_000, bytes_accessed=1_000_000, transcendentals=0)


class Piece:
    def __init__(self, array, count=None, index=0, entry=None, side=0, sides=1):
        self.array, self.count = array, count or array.shape[0]
        self.index, self.entry = index, entry
        self.side, self.columns = side, array.shape[1] // sides

    def row(self, table):
        return self.index if self.entry is None else table[self.entry]

    def spec(self, width=None):
        if width is None:
            return pl.BlockSpec(
                (self.count, self.columns),
                lambda i, table: (self.row(table), self.side),
                pipeline_mode=pl.Buffered(1),
            )
        return pl.BlockSpec((self.count, width), lambda i, table: (self.row(table), i))


def pieces_of(blocks):
    return [Piece(block) for block in blocks]


def stacked(refs):
    values = [ref[...] for ref in refs]
    return values[0] if len(values) == 1 else jnp.concatenate(values, axis=0)


def row_call(
    kernel, name, table, grid, operands, specs, outs, out_specs, aliases=None, mebibytes=56
):
    return pl.pallas_call(
        kernel,
        grid_spec=pltpu.PrefetchScalarGridSpec(
            num_scalar_prefetch=1, grid=grid, in_specs=specs, out_specs=out_specs
        ),
        out_shape=outs,
        input_output_aliases=aliases or {},
        compiler_params=kernel_params(mebibytes),
        cost_estimate=SMALL_COST,
        name=name,
    )(table, *operands)


def product_kernel(count, crossed, *refs):
    rows = stacked(refs[1 : 1 + count])
    matrix = refs[1 + count][...]
    result = contract_cols(rows, matrix) if crossed else product(rows, matrix)
    size = refs[-1].shape[0]
    outs = refs[-(rows.shape[0] // size) :]
    for i, out_ref in enumerate(outs):
        out_ref[...] = result[i * size : (i + 1) * size].astype(out_ref.dtype)


def block_product(table, pieces, matrix, crossed, parts=1, into=None):
    width = matrix.shape[0] if crossed else matrix.shape[1]
    tile = tile_of(width, 512)
    count = sum(piece.count for piece in pieces)
    if crossed:
        matrix_spec = pl.BlockSpec((tile, matrix.shape[1]), lambda i, table: (i, 0))
    else:
        matrix_spec = pl.BlockSpec((matrix.shape[0], tile), lambda i, table: (0, i))
    operands = [piece.array for piece in pieces] + [matrix]
    specs = [piece.spec() for piece in pieces] + [matrix_spec]
    aliases = {}
    index, all_rows = 0, count
    if into is not None:
        all_rows, index, so_far = into
        if so_far is not None:
            operands.append(so_far)
            specs.append(pl.BlockSpec(memory_space=pltpu.HBM))
            aliases = {len(operands): 0}
    if parts > 1:
        count = all_rows = count // parts
    out_spec = pl.BlockSpec((count, tile), lambda i, table: (index, i))
    out = jax.ShapeDtypeStruct((all_rows, width), jnp.bfloat16)
    result = row_call(
        lambda *refs: product_kernel(len(pieces), crossed, *refs),
        "block_product",
        table,
        (width // tile,),
        operands,
        specs,
        [out] * parts,
        [out_spec] * parts,
        aliases,
        56 if matrix.size > 4 * 1024 * 1024 else 32,
    )
    return result if parts > 1 else result[0]


def gate_kernel(count, *refs):
    rows = stacked(refs[1 : 1 + count])
    gate_ref, up_ref, activated_ref, gate_out, up_out = refs[1 + count :]
    gate = product(rows, gate_ref[...])
    up = product(rows, up_ref[...])
    activated_ref[...] = (gate * jax.nn.sigmoid(gate) * up).astype(jnp.bfloat16)
    gate_out[...] = gate.astype(gate_out.dtype)
    up_out[...] = up.astype(up_out.dtype)


def gate_up_product(table, pieces, matrix):
    depth, width = matrix.shape[0], matrix.shape[1] // 2
    count = sum(piece.count for piece in pieces)
    tile = tile_of(width, 256)
    steps = width // tile
    return row_call(
        lambda *refs: gate_kernel(len(pieces), *refs),
        "gate_up",
        table,
        (steps,),
        [piece.array for piece in pieces] + [matrix, matrix],
        [piece.spec() for piece in pieces]
        + [
            pl.BlockSpec((depth, tile), lambda i, table: (0, i)),
            pl.BlockSpec((depth, tile), lambda i, table: (0, steps + i)),
        ],
        [jax.ShapeDtypeStruct((count, width), jnp.bfloat16)] * 3,
        [pl.BlockSpec((count, tile), lambda i, table: (0, i))] * 3,
    )


def gate_grad_kernel(count, *refs):
    rows = stacked(refs[1 : 1 + count])
    down_ref, gate_ref, up_ref, out_ref = refs[1 + count :]
    step = pl.program_id(0)
    tile = gate_ref.shape[1]
    width = out_ref.shape[1] // 2
    grad = contract_cols(rows, down_ref[...])
    gate = gate_ref[...].astype(jnp.float32)
    up = up_ref[...].astype(jnp.float32)
    sigmoid_gate = jax.nn.sigmoid(gate)
    scaled = grad * sigmoid_gate
    start = pl.multiple_of(step * tile, tile)
    out_ref[:, pl.ds(start, tile)] = (
        scaled * up * (1.0 + gate * (1.0 - sigmoid_gate))
    ).astype(jnp.bfloat16)
    out_ref[:, pl.ds(pl.multiple_of(width + step * tile, tile), tile)] = (scaled * gate).astype(
        jnp.bfloat16
    )


def gate_up_gradient(table, pieces, down, gate, up):
    count, width = gate.shape
    tile = tile_of(width, 256)
    part = pl.BlockSpec((count, tile), lambda i, table: (0, i))
    return row_call(
        lambda *refs: gate_grad_kernel(len(pieces), *refs),
        "gate_up_grad",
        table,
        (width // tile,),
        [piece.array for piece in pieces] + [down, gate, up],
        [piece.spec() for piece in pieces]
        + [pl.BlockSpec((tile, down.shape[1]), lambda i, table: (i, 0)), part, part],
        [jax.ShapeDtypeStruct((count, 2 * width), jnp.bfloat16)],
        [pl.BlockSpec((count, 2 * width), lambda i, table: (0, 0))],
    )[0]


def rows_kernel(count, weighed, *refs):
    out_ref = refs[2 * count + 1 + weighed]
    result = sum(contract_rows(refs[1 + i][...], refs[1 + count + i][...]) for i in range(count))
    out_ref[...] = result.astype(out_ref.dtype)
    if weighed:
        by_column = jnp.transpose(result * refs[2 * count + 1][...].astype(jnp.float32))
        refs[-1][...] = jnp.sum(by_column, axis=0, keepdims=True)


def weight_gradient(table, lefts, rights, weights=None):
    width, columns = lefts[0].array.shape[1], rights[0].columns
    tile = tile_of(width, 256)
    weighed = weights is not None
    block_spec = pl.BlockSpec((tile, columns), lambda i, table: (i, 0))
    result = row_call(
        lambda *refs: rows_kernel(len(lefts), weighed, *refs),
        "weight_grad",
        table,
        (width // tile,),
        [piece.array for piece in lefts + rights] + ([weights] if weighed else []),
        [piece.spec(tile) for piece in lefts]
        + [piece.spec() for piece in rights]
        + ([block_spec] if weighed else []),
        [jax.ShapeDtypeStruct((width, columns), jnp.bfloat16)]
        + ([jax.ShapeDtypeStruct((1, width), jnp.float32)] if weighed else []),
        [block_spec] + ([pl.BlockSpec((1, tile), lambda i, table: (0, i))] if weighed else []),
    )
    return result if weighed else result[0]


def split_groups(groups, half, side=0, sides=1):
    return [
        Piece(array, half, i, side=side, sides=sides)
        for array in groups
        for i in range(array.shape[0] // half)
    ]


def arrived_sum(split, low_refs, high_refs):
    low = sum(ref[...].astype(jnp.float32) for ref in low_refs)
    high = sum(ref[...].astype(jnp.float32) for ref in high_refs)
    return jnp.where(pl.program_id(0) < split, low, high)


def half_specs(tile, split, width):
    return (
        pl.BlockSpec((tile, width), lambda i: (jnp.minimum(i, split - 1), 0)),
        pl.BlockSpec((tile, width), lambda i: (jnp.maximum(i - split, 0), 0)),
    )


def put_half(split, low_ref, high_ref, value):
    @pl.when(pl.program_id(0) < split)
    def _():
        low_ref[...] = value

    @pl.when(pl.program_id(0) >= split)
    def _():
        high_ref[...] = value


def row_kernel_call(kernel, name, whole, lows, highs, gain, outs):
    rows, width = whole[0].shape
    tile = min(rows // 2, 128)
    split = rows // 2 // tile
    spec = pl.BlockSpec((tile, width), lambda i: (i, 0))
    low_spec, high_spec = half_specs(tile, split, width)
    row_spec = pl.BlockSpec((1, width), lambda i: (0, 0))
    shapes, specs = [], []
    for out in outs:
        if out == "halves":
            shapes += [jax.ShapeDtypeStruct((rows // 2, width), jnp.bfloat16)] * 2
            specs += [low_spec, high_spec]
        elif out == "row":
            shapes.append(jax.ShapeDtypeStruct((1, width), jnp.float32))
            specs.append(row_spec)
        else:
            shapes.append(jax.ShapeDtypeStruct((rows, width), out))
            specs.append(spec)
    return pl.pallas_call(
        lambda *refs: kernel(split, len(lows), *refs),
        grid=(2 * split,),
        in_specs=[spec] * len(whole)
        + [low_spec] * len(lows)
        + [high_spec] * len(highs)
        + [row_spec],
        out_specs=specs,
        out_shape=shapes,
        compiler_params=kernel_params(),
        cost_estimate=SMALL_COST,
        name=name,
    )(*whole, *lows, *highs, gain)


def add_norm_kernel(split, count, base_ref, own_ref, *refs):
    gain_ref, sum_ref, low_ref, high_ref = refs[2 * count :]
    values = base_ref[...].astype(jnp.float32) + own_ref[...].astype(jnp.float32)
    values = values + arrived_sum(split, refs[:count], refs[count : 2 * count])
    sum_ref[...] = values
    put_half(split, low_ref, high_ref, rms_gain(values, gain_ref[...]).astype(jnp.bfloat16))


def add_and_norm(base, own, lows, highs, gain):
    outs = (jnp.float32, "halves")
    return row_kernel_call(add_norm_kernel, "add_norm", [base, own], lows, highs, gain, outs)


def add_kernel(split, count, base_ref, own_ref, *refs):
    values = base_ref[...].astype(jnp.float32) + own_ref[...].astype(jnp.float32)
    values = values + arrived_sum(split, refs[:count], refs[count : 2 * count])
    refs[-1][...] = values.astype(jnp.bfloat16)


def norm_gradient_kernel(split, count, base_ref, value_ref, own_ref, *refs):
    gain_ref, outs = refs[2 * count], refs[2 * count + 1 :]
    grad = own_ref[...].astype(jnp.float32)
    grad = grad + arrived_sum(split, refs[:count], refs[count : 2 * count])
    values = value_ref[...].astype(jnp.float32)
    scale = lax.rsqrt(jnp.mean(values * values, axis=1, keepdims=True) + norm_eps)
    unit = values * scale
    inner = grad * gain_ref[...]
    result = base_ref[...].astype(jnp.float32) + scale * (
        inner - unit * jnp.mean(inner * unit, axis=1, keepdims=True)
    )
    if len(outs) == 1:
        outs[0][...] = result.astype(jnp.bfloat16)
        return
    low_ref, high_ref, whole_ref, gain_out = outs
    whole_ref[...] = result.astype(jnp.bfloat16)
    put_half(split, low_ref, high_ref, result.astype(jnp.bfloat16))

    @pl.when(pl.program_id(0) == 0)
    def _():
        gain_out[...] = jnp.zeros_like(gain_out)

    gain_out[...] += jnp.sum(grad * unit, axis=0, keepdims=True)


def norm_gradient(base, values, own, lows, highs, gain, outs):
    return row_kernel_call(
        norm_gradient_kernel, "norm_gradient", [base, values, own], lows, highs, gain, outs
    )


def project_kernel(count, *refs):
    rows = stacked(refs[1 : 1 + count])
    matrix_ref, gain_ref, cos_ref, sin_ref = refs[1 + count : 5 + count]
    query_ref, key_ref, value_ref, query_raw, key_raw = refs[-5:]
    width = HEAD_WIDTH
    mixed = product(rows, matrix_ref[...])
    cos, sin = cos_ref[...], sin_ref[...]
    for part in range(QUERY_PER_KEY + 1):
        values = mixed[:, part * width : (part + 1) * width]
        is_key = part == QUERY_PER_KEY
        gain = gain_ref[1:2, :] if is_key else gain_ref[0:1, :]
        scale = lax.rsqrt(jnp.mean(values * values, axis=1, keepdims=True) + norm_eps)
        scaled = values * scale * gain
        turned = scaled * cos + pltpu.roll(scaled, width // 2, 1) * sin
        if is_key:
            key_ref[...] = turned.astype(jnp.bfloat16)
            key_raw[...] = values
        else:
            query_ref[:, part * width : (part + 1) * width] = turned.astype(jnp.bfloat16)
            query_raw[:, part * width : (part + 1) * width] = values
    value_ref[...] = mixed[:, (QUERY_PER_KEY + 1) * width :].astype(jnp.bfloat16)


def project(blocks, matrix, gains, cos, sin, place, total_rows, before):
    count, depth = sum(block.shape[0] for block in blocks), matrix.shape[0]
    block = (QUERY_PER_KEY + 2) * HEAD_WIDTH
    heads = matrix.shape[1] // block
    wide = QUERY_PER_KEY * HEAD_WIDTH
    per_table = cos.shape[0] // count
    table_spec = pl.BlockSpec(
        (count, HEAD_WIDTH), lambda h, at: (lax.rem(at[0], per_table), 0)
    )
    widths = (wide, HEAD_WIDTH, HEAD_WIDTH, wide, HEAD_WIDTH)
    kinds = (jnp.bfloat16,) * 3 + (jnp.float32,) * 2
    kept = () if before is None else tuple(before)
    return pl.pallas_call(
        lambda *refs: project_kernel(len(blocks), *refs),
        grid_spec=pltpu.PrefetchScalarGridSpec(
            num_scalar_prefetch=1,
            grid=(heads,),
            in_specs=[
                pl.BlockSpec((rows.shape[0], depth), lambda h, at: (0, 0)) for rows in blocks
            ]
            + [
                pl.BlockSpec((depth, block), lambda h, at: (0, h)),
                pl.BlockSpec((2, HEAD_WIDTH), lambda h, at: (0, 0)),
                table_spec,
                table_spec,
            ]
            + [pl.BlockSpec(memory_space=pltpu.HBM)] * len(kept),
            out_specs=[pl.BlockSpec((count, w), lambda h, at: (at[0], h)) for w in widths],
        ),
        out_shape=[
            jax.ShapeDtypeStruct((total_rows, heads * w), kind) for w, kind in zip(widths, kinds)
        ],
        input_output_aliases={5 + len(blocks) + i: i for i in range(len(kept))},
        compiler_params=kernel_params(56),
        cost_estimate=SMALL_COST,
        name="project",
    )(place.reshape(1), *blocks, matrix, gains, cos, sin, *kept)


def causal(keys, queries):
    rows = lax.broadcasted_iota(jnp.int32, (keys, queries), 0)
    return rows <= lax.broadcasted_iota(jnp.int32, (keys, queries), 1)


def add_after(whole, part, low):
    if low == 0:
        return whole + part
    return jnp.concatenate([whole[:, :low], whole[:, low:] + part], axis=1)


def walk(visit, step, block, carry, pieces):
    carry = lax.fori_loop(
        0,
        step,
        lambda j, c: visit(pl.multiple_of(j * block, block), c, block, 0, False),
        carry,
    )
    start = pl.multiple_of(step * block, block)
    count = block // pieces
    for low in range(0, block, count):
        carry = visit(start + low, carry, count, low, True)
    return carry


def attend_kernel(scale, query_ref, key_ref, value_ref, out_ref, log_ref):
    block = query_ref.shape[0]
    width = key_ref.shape[1]
    group = query_ref.shape[1] // width
    step = pl.program_id(2)
    queries = [query_ref[:, g * width : (g + 1) * width] for g in range(group)]

    def visit(start, carry, count, low, masked):
        keys = key_ref[pl.ds(start, count), :]
        values = value_ref[pl.ds(start, count), :]
        new = []
        for g in range(group):
            total, acc = carry[g]
            weights = jnp.exp2(contract_cols(keys, queries[g][low:]) * (scale * log2_e))
            if masked:
                weights = jnp.where(causal(count, block - low), weights, 0.0)
            total = add_after(total, jnp.sum(weights, axis=0, keepdims=True), low)
            acc = add_after(acc, contract_rows(values, weights.astype(jnp.bfloat16)), low)
            new.append((total, acc))
        return tuple(new)

    carry = tuple(
        (jnp.zeros((1, block), jnp.float32), jnp.zeros((width, block), jnp.float32))
        for _ in range(group)
    )
    carry = walk(visit, step, block, carry, 1)
    for g in range(group):
        total, acc = carry[g]
        out_ref[:, g * width : (g + 1) * width] = jnp.transpose(acc / total).astype(jnp.bfloat16)
        log_ref[0, 0, g : g + 1, :] = jnp.log2(total)


def attention_forward(query, key, value, block):
    rows = query.shape[0]
    heads = key.shape[1] // HEAD_WIDTH
    steps = SEQUENCE_TOKENS // block
    wide = QUERY_PER_KEY * HEAD_WIDTH
    sequences = rows // SEQUENCE_TOKENS
    query_spec = pl.BlockSpec((block, wide), lambda h, s, i: (s * steps + i, h))
    key_spec = pl.BlockSpec((SEQUENCE_TOKENS, HEAD_WIDTH), lambda h, s, i: (s, h))
    return pl.pallas_call(
        lambda *refs: attend_kernel(HEAD_WIDTH ** (-0.5), *refs),
        grid=(heads, sequences, steps),
        in_specs=[query_spec, key_spec, key_spec],
        out_specs=[
            query_spec,
            pl.BlockSpec(
                (1, 1, QUERY_PER_KEY, block), lambda h, s, i: (h, s * steps + i, 0, 0)
            ),
        ],
        out_shape=[
            jax.ShapeDtypeStruct(query.shape, jnp.bfloat16),
            jax.ShapeDtypeStruct((heads, rows // block, QUERY_PER_KEY, block), jnp.float32),
        ],
        compiler_params=kernel_params(56),
        cost_estimate=SMALL_COST,
        name="attend",
    )(query, key, value)


def norm_back(values, grad, gain, cos, sin):
    width = values.shape[1]
    turned = grad * cos + pltpu.roll(grad * sin, width // 2, 1)
    scale = lax.rsqrt(jnp.mean(values * values, axis=1, keepdims=True) + norm_eps)
    unit = values * scale
    inner = turned * gain
    back = scale * (inner - unit * jnp.mean(inner * unit, axis=1, keepdims=True))
    return back.astype(jnp.bfloat16), jnp.sum(turned * unit, axis=0, keepdims=True)


def attend_back_kernel(
    scale,
    table_ref,
    query_ref,
    key_ref,
    value_ref,
    grad_ref,
    context_ref,
    log_ref,
    query_raw,
    key_raw,
    gain_ref,
    cos_ref,
    sin_ref,
    *refs,
):
    mixed_out, gain_out, key_sum, value_sum = refs[-4:]
    block = query_ref.shape[0]
    width = key_ref.shape[1]
    group = query_ref.shape[1] // width
    sequence, step = pl.program_id(0), pl.program_id(1)
    @pl.when(step == 0)
    def _():
        key_sum[...] = jnp.zeros_like(key_sum)
        value_sum[...] = jnp.zeros_like(value_sum)

    @pl.when((step == 0) & (sequence == 0))
    def _():
        gain_out[...] = jnp.zeros_like(gain_out)

    queries, grads, logs, dots = [], [], [], []
    for g in range(group):
        cols = slice(g * width, (g + 1) * width)
        queries.append(query_ref[:, cols])
        grads.append(grad_ref[:, cols])
        logs.append(log_ref[0, 0, g : g + 1, :])
        both = grads[g].astype(jnp.float32) * context_ref[:, cols].astype(jnp.float32)
        dots.append(jnp.sum(jnp.transpose(both), axis=0, keepdims=True))

    def visit(start, carry, count, low, masked):
        rows = pl.ds(start, count)
        keys = key_ref[rows, :]
        values = value_ref[rows, :]
        new = []
        key_part = value_part = None
        for g in range(group):
            seen, sought = queries[g][low:], grads[g][low:]
            weights = jnp.exp2(contract_cols(keys, seen) * (scale * log2_e) - logs[g][:, low:])
            if masked:
                weights = jnp.where(causal(count, block - low), weights, 0.0)
            slope = contract_cols(values, sought)
            score = (weights * (slope - dots[g][:, low:])).astype(jnp.bfloat16)
            value_g = product(weights.astype(jnp.bfloat16), sought)
            key_g = product(score, seen)
            key_part = key_g if key_part is None else key_part + key_g
            value_part = value_g if value_part is None else value_part + value_g
            new.append(add_after(carry[g], contract_rows(keys, score), low))
        key_sum[rows, :] += key_part
        value_sum[rows, :] += value_part
        return tuple(new)

    carry = tuple(jnp.zeros((width, block), jnp.float32) for _ in range(group))
    carry = walk(visit, step, block, carry, 2)
    rows = pl.ds(pl.multiple_of(step * block, block), block)
    cos, sin = cos_ref[rows, :], sin_ref[rows, :]
    for g in range(group):
        cols = slice(g * width, (g + 1) * width)
        back, gain = norm_back(
            query_raw[:, cols], jnp.transpose(carry[g]) * scale, gain_ref[0:1, :], cos, sin
        )
        mixed_out[rows, cols] = back
        gain_out[0:1, :] += gain

    @pl.when(step == pl.num_programs(1) - 1)
    def _():
        def finish(j, _):
            rows = pl.ds(pl.multiple_of(j * block, block), block)
            back, gain = norm_back(
                key_raw[rows, :],
                key_sum[rows, :] * scale,
                gain_ref[1:2, :],
                cos_ref[rows, :],
                sin_ref[rows, :],
            )
            mixed_out[rows, group * width : (group + 1) * width] = back
            mixed_out[rows, (group + 1) * width :] = value_sum[rows, :].astype(jnp.bfloat16)
            gain_out[1:2, :] += gain
            return 0

        lax.fori_loop(0, pl.num_programs(1), finish, 0)


def attention_backward(
    slots, query, key, value, grad, context, logs, query_raw, key_raw, gains, cos, sin, head, before
):
    rows = query.shape[0]
    block = logs.shape[-1]
    steps = SEQUENCE_TOKENS // block
    wide = QUERY_PER_KEY * HEAD_WIDTH
    heads = key.shape[1] // HEAD_WIDTH
    sequences = rows // SEQUENCE_TOKENS
    mixed = (QUERY_PER_KEY + 2) * HEAD_WIDTH
    query_spec = pl.BlockSpec((block, wide), lambda s, i, slots: (s * steps + i, head))
    key_spec = pl.BlockSpec((SEQUENCE_TOKENS, HEAD_WIDTH), lambda s, i, slots: (s, head))
    table_spec = pl.BlockSpec((SEQUENCE_TOKENS, HEAD_WIDTH), lambda s, i, slots: (0, 0))
    gain_spec = pl.BlockSpec((2, HEAD_WIDTH), lambda s, i, slots: (0, 0))
    kept = () if before is None else (before,)
    return pl.pallas_call(
        lambda *refs: attend_back_kernel(HEAD_WIDTH ** (-0.5), *refs),
        grid_spec=pltpu.PrefetchScalarGridSpec(
            num_scalar_prefetch=1,
            grid=(sequences, steps),
            in_specs=[
            query_spec,
            key_spec,
            key_spec,
            pl.BlockSpec((block, wide), lambda s, i, slots: (slots[s * steps + i], head)),
            query_spec,
            pl.BlockSpec(
                (1, 1, QUERY_PER_KEY, block), lambda s, i, slots: (head, s * steps + i, 0, 0)
            ),
            query_spec,
            key_spec,
            gain_spec,
            table_spec,
            table_spec,
        ]
        + [pl.BlockSpec(memory_space=pltpu.HBM)] * len(kept),
        out_specs=[
            pl.BlockSpec((SEQUENCE_TOKENS, mixed), lambda s, i, slots: (s, head)),
            gain_spec,
        ],
        scratch_shapes=[pltpu.VMEM((SEQUENCE_TOKENS, HEAD_WIDTH), jnp.float32)] * 2,
        ),
        out_shape=[
            jax.ShapeDtypeStruct((rows, heads * mixed), jnp.bfloat16),
            jax.ShapeDtypeStruct((2, HEAD_WIDTH), jnp.float32),
        ],
        input_output_aliases={12: 0} if kept else {},
        compiler_params=kernel_params(56),
        cost_estimate=SMALL_COST,
        name="attend_back",
    )(slots, query, key, value, grad, context, logs, query_raw, key_raw, gains, cos, sin, *kept)


def local(
    inputs,
    input_projection_weight,
    input_first_moment,
    input_second_moment,
    out_weight,
    out_mean,
    out_square,
    swiglu_weight,
    swiglu_mean,
    swiglu_square,
    down_weight,
    down_mean,
    down_square,
    norm_gains,
    norm_mean,
    norm_square,
    qknorm_gains,
    qknorm_mean,
    qknorm_square,
    cotangent,
):
    size = lax.axis_size("tensor")
    rows = inputs.shape[0]
    half = rows // 2
    group_rows = rows * size
    last = size // 2
    dp_rows = input_projection_weight.shape[0]
    local_kv = input_projection_weight.shape[1]
    local_ff = swiglu_weight.shape[2]
    me = ring_place(lax.axis_index("tensor"), size)
    places = [ring_place((me + d + size) % size, size) for d in ring_offsets(size)]
    group_places = [places[:1]]
    for step in range(1, last):
        group_places.append(places[2 * step - 1 : 2 * step + 1])
    group_places.append(places[-1:])
    halves = [2 * place + i for place in places for i in range(2)]
    table = jnp.stack(places + halves).astype(jnp.int32)
    away = (ring_place(jnp.arange(size, dtype=jnp.int32), size) - me + size) % size
    slots = jnp.where(
        away == 0,
        size - 2,
        jnp.where(
            away == last,
            size - 1,
            jnp.where(away < last, 2 * away - 2, 2 * (size - away) - 1),
        ),
    ).astype(jnp.int32)
    order = Order()
    turn, mark = order.turn, order.mark
    tie = lax.optimization_barrier

    def ordered(array, group):
        entries = [0] if group == 0 else [2 * group - 1, 2 * group]
        if group == last:
            entries = [size - 1]
        return [Piece(array, rows, entry=entry) for entry in entries]

    def ordered_finely(array):
        return [Piece(array, half, entry=size + i) for i in range(2 * size)]

    def flat(groups):
        return pieces_of([block for group in groups for block in group])

    def parts_of(group):
        return 1 if group == 0 else 2 if group == last else 4

    def marked(part):
        return mark(*part) if isinstance(part, (list, tuple)) else mark(part)

    in_low = input_projection_weight.astype(jnp.bfloat16).reshape(dp_rows, -1)
    out_low = out_weight.astype(jnp.bfloat16)
    swiglu_low = swiglu_weight.astype(jnp.bfloat16).reshape(dp_rows, 2 * local_ff)
    down_low = down_weight.astype(jnp.bfloat16)
    in_matrix = lax.all_gather(in_low, "dp", axis=0, tiled=True)
    out_full = lax.all_gather(out_low, "dp", axis=1, tiled=True)
    swiglu_matrix = lax.all_gather(swiglu_low, "dp", axis=0, tiled=True)
    down_full = lax.all_gather(down_low, "dp", axis=1, tiled=True)

    normed_f = rms_gain(inputs.astype(jnp.float32), norm_gains[0])
    cos, sin = rotary_tables(SEQUENCE_TOKENS, HEAD_WIDTH)
    projected = []

    def project_group(group, blocks):
        calls = [blocks] if group in (0, last) else [blocks[:2], blocks[2:]]
        for place, call in zip(group_places[group], calls):
            call[0] = turn(call[0])
            projected[:] = mark(
                *project(
                    call, in_matrix, qknorm_gains, cos, sin, place, group_rows, projected or None
                )
            )

    normed = normed_f.astype(jnp.bfloat16)
    normed_groups = ring_gather(
        (normed[:half], normed[half:]), size, project_group, order, hold=(in_matrix,)
    )
    query, key, value, query_raw, key_raw = projected
    cotangent_sent = tie((cotangent, *normed_groups[-1]))[0]

    context, logs = mark(*attention_forward(query, key, value, rows))
    cot_groups, cot_carried = ring_near(
        (cotangent_sent[:half], cotangent_sent[half:]), size, lambda group, blocks: None, Order()
    )

    def out_group(group):
        return marked(
            block_product(
                table, ordered(turn(context), group), out_full, False, parts_of(group)
            )
        )

    own, lows, highs = ring_scatter(
        size, out_group, order, first=[half for group in cot_groups[1:] for half in group]
    )
    lows, highs = tie((lows, highs, swiglu_matrix))[:2]
    hidden, *two_halves = mark(*add_and_norm(inputs, own, lows, highs, norm_gains[1:2]))

    gate_groups = []
    grads = [None] * (last + 1)

    def gate_group(group, blocks):
        blocks[0] = turn(blocks[0])
        gate_groups.append(mark(*gate_up_product(table, pieces_of(blocks), swiglu_matrix)))

    two_groups, two_carried = ring_near(two_halves, size, gate_group, order)
    two_groups = ring_far(two_groups, two_carried, size, gate_group, order)
    cot_carried = tie((*cot_carried, *gate_groups[last - 1]))[:2]
    cot_groups = ring_far(cot_groups, cot_carried, size, lambda group, blocks: None, order)
    activated = [parts[0] for parts in gate_groups]
    two_parts = [None] * (last + 1)

    def two_grads(group):
        cots = [turn(cot_groups[group][0])] + cot_groups[group][1:]
        grads[group] = mark(
            gate_up_gradient(table, pieces_of(cots), down_full, *gate_groups[group][1:])
        )

    def two_product(group):
        two_parts[group] = marked(
            block_product(
                table, [Piece(turn(grads[group]))], swiglu_matrix, True, parts_of(group)
            )
        )

    for group in range(1, last):
        two_grads(group)
    lefts = split_groups([turn(activated[0])] + activated[1:], half)
    down_part = mark(weight_gradient(table, lefts, flat(cot_groups)))
    down_grad = lax.psum_scatter(down_part, "dp", scatter_dimension=1, tiled=True)
    for group in range(1, last):
        two_product(group)
    two_grads(last)
    two_product(last)
    more = []

    def own_part():
        two_grads(0)
        two_product(0)

    def swiglu_gradient():
        twos = flat(two_groups)
        twos[0].array = turn(twos[0].array)
        side = len(more)
        more.append(mark(weight_gradient(table, twos, split_groups(grads, half, side, 2))))

    if last == 1:
        own_part()
    own, lows, highs = ring_scatter(
        size, lambda group: two_parts[group], order, between=own_part, after=swiglu_gradient
    )
    swiglu_part, lows, highs = tie((more[0], lows, highs))
    gate_weight_grad = lax.psum_scatter(swiglu_part, "dp", scatter_dimension=0, tiled=True)
    *attended_halves, hidden_grad, mlp_gain_grad = mark(
        *norm_gradient(
            cotangent, hidden, own, lows, highs, norm_gains[1:2], ("halves", jnp.bfloat16, "row")
        )
    )

    context_grad, down_parts, new_down, head_grads = [None], [None] * (last + 1), [], []

    def context_group(group, blocks):
        blocks[0] = turn(blocks[0])
        index = size - 2 if group == 0 else size - 1 if group == last else group - 1
        context_grad[0] = mark(
            block_product(
                table, pieces_of(blocks), out_full, True, into=(group_rows, index, context_grad[0])
            )
        )
        if group == 0:
            for other in range(last, -1, -1):
                down_parts[other] = marked(
                    block_product(
                        table, [Piece(turn(activated[other]))], down_full, False, parts_of(other)
                    )
                )
            new_down[:] = mark(
                turn(down_grad).astype(jnp.float32),
                *adamw(
                    down_weight,
                    turn(down_grad).astype(jnp.float32),
                    down_mean,
                    down_square,
                    FF ** (-0.5),
                ),
            )
        if group == last - 1:
            swiglu_gradient()

    attended_groups = ring_gather(attended_halves, size, context_group, order)
    swiglu_part = tie((more[1], *attended_groups[last]))[0]
    up_weight_grad = lax.psum_scatter(swiglu_part, "dp", scatter_dimension=0, tiled=True)

    def head_backward(head):
        head_grads.append(
            mark(
                *attention_backward(
                    slots, turn(query), key, value, context_grad[0], context, logs, query_raw,
                    key_raw, qknorm_gains, cos, sin, head,
                    head_grads[-1][0] if head_grads else None,
                )
            )
        )

    out_part = mark(
        weight_gradient(table, ordered_finely(turn(context)), flat(attended_groups))
    )
    if last == 1:
        head_backward(0)

    def other_heads():
        for head in range(1, local_kv):
            head_backward(head)

    own, lows, highs = ring_scatter(
        size,
        lambda group: down_parts[group],
        order,
        hold=attended_groups[-1],
        between=lambda: head_backward(0),
        after=other_heads,
    )
    sent, outputs = (own, lows, highs), []
    mixed_grad = head_grads[-1][0]
    qknorm_part = sum(pair[1] for pair in head_grads)
    in_parts = []

    def normed_group(group):
        return marked(
            block_product(
                table, ordered(turn(mixed_grad), group), in_matrix, True, parts_of(group)
            )
        )

    def in_gradient():
        normeds = flat(normed_groups)
        normeds[0].array = turn(normeds[0].array)
        in_parts[:] = mark(
            *weight_gradient(table, normeds, ordered_finely(mixed_grad), in_matrix)
        )
        own, lows, highs = sent
        outputs[:] = mark(
            *row_kernel_call(
                add_kernel,
                "add",
                [hidden, turn(own)],
                lows,
                highs,
                norm_gains[0:1],
                (jnp.bfloat16,),
            ),
            in_parts[0],
        )[:1]

    got = []
    own, lows, highs = ring_scatter(size, normed_group, order, between=in_gradient, got=got)
    if not in_parts:
        in_gradient()
    rows_of_gains = jnp.concatenate([in_parts[1] / norm_gains[0:1], mlp_gain_grad], axis=0)
    gain_sums = jnp.concatenate([rows_of_gains, qknorm_part], axis=1)
    (outputs,) = outputs
    gain_sums = tie((gain_sums, own, *got))[0]
    gain_sums = sum_over(gain_sums, "tensor")
    out_part, gate_weight_grad = tie((out_part, gate_weight_grad, sent, mixed_grad))[:2]
    out_grad = lax.psum_scatter(out_part, "dp", scatter_dimension=1, tiled=True)
    in_part, up_weight_grad = tie((in_parts[0], up_weight_grad, *got))[:2]
    in_grad = lax.psum_scatter(in_part, "dp", scatter_dimension=0, tiled=True)
    out_grad, gate_weight_grad = tie((out_grad, gate_weight_grad, *got))[:2]
    out_grad = out_grad.astype(jnp.float32)
    out_new, out_second = adamw(
        out_weight, out_grad, out_mean, out_square, (HQ * HEAD_WIDTH / 8.0) ** (-0.5)
    )
    swiglu_grad, swiglu_new, swiglu_second = adamw_parts(
        swiglu_weight,
        (gate_weight_grad, up_weight_grad),
        swiglu_mean,
        swiglu_square,
        MODEL_WIDTH ** (-0.5),
    )
    down_grad, down_new, down_second = new_down
    (
        lows,
        highs,
        own,
        outputs,
        out_grad,
        out_new,
        out_second,
        swiglu_grad,
        swiglu_new,
        swiglu_second,
    ) = tie(
        (
            lows,
            highs,
            own,
            outputs,
            out_grad,
            out_new,
            out_second,
            swiglu_grad,
            swiglu_new,
            swiglu_second,
        )
    )
    (input_grad,) = norm_gradient(
        hidden_grad, inputs, own, lows, highs, norm_gains[0:1], (jnp.bfloat16,)
    )
    in_grad, in_new, in_second = adamw_parts(
        input_projection_weight,
        (in_grad,),
        input_first_moment,
        input_second_moment,
        MODEL_WIDTH ** (-0.5),
    )
    gain_sums = sum_over(tie((gain_sums, *lows, *highs))[0], "dp", (input_grad, in_new))
    norm_grad, qknorm_grad = gain_sums[:, :MODEL_WIDTH], gain_sums[:, MODEL_WIDTH:]
    norm_new, norm_second = adamw(norm_gains, norm_grad, norm_mean, norm_square, gain_rate)
    qknorm_new, qknorm_second = adamw(
        qknorm_gains, qknorm_grad, qknorm_mean, qknorm_square, gain_rate
    )
    return (
        outputs,
        input_grad,
        in_grad,
        in_new,
        in_second,
        out_grad,
        out_new,
        out_second,
        swiglu_grad,
        swiglu_new,
        swiglu_second,
        down_grad,
        down_new,
        down_second,
        norm_grad,
        norm_new,
        norm_second,
        qknorm_grad,
        qknorm_new,
        qknorm_second,
    )


def solution(mesh):
    return jax.shard_map(
        local,
        mesh=mesh,
        in_specs=(
            P(("dp", "tensor"), None),
            P("dp", "tensor", None),
            P("dp", "tensor", None),
            P("dp", "tensor", None),
            P("tensor", "dp"),
            P("tensor", "dp"),
            P("tensor", "dp"),
            P("dp", None, "tensor"),
            P("dp", None, "tensor"),
            P("dp", None, "tensor"),
            P("tensor", "dp"),
            P("tensor", "dp"),
            P("tensor", "dp"),
            P(),
            P(),
            P(),
            P(),
            P(),
            P(),
            P(("dp", "tensor"), None),
        ),
        out_specs=(
            P(("dp", "tensor"), None),
            P(("dp", "tensor"), None),
            P("dp", "tensor", None),
            P("dp", "tensor", None),
            P("dp", "tensor", None),
            P("tensor", "dp"),
            P("tensor", "dp"),
            P("tensor", "dp"),
            P("dp", None, "tensor"),
            P("dp", None, "tensor"),
            P("dp", None, "tensor"),
            P("tensor", "dp"),
            P("tensor", "dp"),
            P("tensor", "dp"),
            P(),
            P(),
            P(),
            P(),
            P(),
            P(),
        ),
        check_vma=False,
    )
```

```python
import jax
import jax.numpy as jnp
from jax import lax
from jax.experimental import pallas as pl
from jax.experimental.pallas import tpu as pltpu
from jax.sharding import PartitionSpec as P

MODEL_WIDTH = 2048
HQ = 16
HEAD_WIDTH = 128
FF = 6144
QUERY_PER_KEY = 2
SEQUENCE_TOKENS = 2048


norm_eps = 1e-06
rope_base = 1000000.0
beta_one = 0.5
beta_two = 0.55
step_count = 5.0
adam_eps = 1e-08
decay_rate = 0.1
gain_rate = 0.3
masked_score = -1e30
log2_e = 1.4426950408889634


def rms_gain(values, gain_row):
    return (
        values * lax.rsqrt(jnp.mean(values * values, axis=-1, keepdims=True) + norm_eps) * gain_row
    )


def rotary_tables(length, width):
    frequency = rope_base ** (
        -2.0 * jnp.arange(width // 2, dtype=jnp.int32).astype(jnp.float32) / width
    )
    angles = jnp.arange(length, dtype=jnp.int32).astype(jnp.float32)[:, None] * frequency[None, :]
    cos, sin = jnp.cos(angles), jnp.sin(angles)
    return jnp.concatenate([cos, cos], axis=1), jnp.concatenate([-sin, sin], axis=1)


def contract_rows(left, right):
    return lax.dot_general(
        left, right, (((0,), (0,)), ((), ())), preferred_element_type=jnp.float32
    )


def contract_cols(left, right):
    return lax.dot_general(
        left, right, (((1,), (1,)), ((), ())), preferred_element_type=jnp.float32
    )


def product(left, right):
    return jnp.dot(left, right, preferred_element_type=jnp.float32)


def adamw(weight, gradient, mean_old, square_old, rate):
    mean_new = beta_one * mean_old + (1.0 - beta_one) * gradient
    square_new = beta_two * square_old + (1.0 - beta_two) * gradient * gradient
    mean_hat = mean_new / (1.0 - beta_one**step_count)
    square_hat = square_new / (1.0 - beta_two**step_count)
    weight_new = weight - rate * (
        mean_hat / (jnp.sqrt(square_hat) + adam_eps) + decay_rate * weight
    )
    return (weight_new, square_new)


def adam_kernel(rate, weight_ref, mean_ref, square_ref, *refs):
    *grad_refs, grad_out, new_out, second_out = refs
    width = weight_ref.shape[2]
    for part in range(weight_ref.shape[1]):
        start = part * width
        for grad_ref in grad_refs:
            if start < grad_ref.shape[1]:
                break
            start -= grad_ref.shape[1]
        grad = grad_ref[:, start : start + width].astype(jnp.float32)
        new, second = adamw(
            weight_ref[:, part, :], grad, mean_ref[:, part, :], square_ref[:, part, :], rate
        )
        grad_out[:, part, :] = grad
        new_out[:, part, :] = new
        second_out[:, part, :] = second


def adamw_parts(weight, grads, mean_old, square_old, rate):
    rows, parts, width = weight.shape
    tile = min(rows, 64)
    spec = pl.BlockSpec((tile, parts, width), lambda i: (i, 0, 0))
    return pl.pallas_call(
        lambda *refs: adam_kernel(rate, *refs),
        grid=(rows // tile,),
        in_specs=[spec] * 3
        + [pl.BlockSpec((tile, grad.shape[1]), lambda i: (i, 0)) for grad in grads],
        out_specs=[spec] * 3,
        out_shape=[jax.ShapeDtypeStruct(weight.shape, jnp.float32)] * 3,
        compiler_params=kernel_params(),
        cost_estimate=SMALL_COST,
        name="adamw",
    )(weight, mean_old, square_old, *grads)


def ring_place(index, size):
    return jnp.where(index < size // 2, index, size // 2 + size - 1 - index)


def ring_pairs(size):
    half = size // 2
    order = list(range(half)) + list(range(size - 1, half - 1, -1))
    ahead = [(order[r], order[(r + 1) % size]) for r in range(size)]
    return ahead, [(b, a) for a, b in ahead]


def ring_offsets(size):
    offsets = [0]
    for step in range(1, size // 2):
        offsets += [step, -step]
    return offsets + [size // 2]


class Order:
    def __init__(self):
        self.last = ()

    def turn(self, *values):
        tied = lax.optimization_barrier(values + self.last)[: len(values)]
        return tied[0] if len(values) == 1 else tied

    def mark(self, *values):
        self.last = values
        return values[0] if len(values) == 1 else values


def ring_near(blocks, size, work, order, hold=()):
    ahead, back = ring_pairs(size)
    tie = lax.optimization_barrier
    groups = [list(blocks)]
    left, right = list(blocks), list(blocks)
    work(0, list(blocks))
    for step in range(1, size // 2):
        left_low = lax.ppermute(left[0], "tensor", ahead)
        right_high = lax.ppermute(right[1], "tensor", back)
        left_high = lax.ppermute(left[1], "tensor", ahead)
        right_low = lax.ppermute(right[0], "tensor", back)
        held = tuple(hold) if step == size // 2 - 1 else ()
        left_low, right_high = tie((left_low, right_high) + held + order.last)[:2]
        left, right = [left_low, left_high], [right_low, right_high]
        pair = tie((*right, *left) + order.last)[:4]
        groups.append(list(pair))
        work(step, list(pair))
    return groups, (left[0], right[1])


def ring_far(groups, carried, size, work, order):
    ahead, back = ring_pairs(size)
    low = lax.ppermute(carried[0], "tensor", ahead)
    high = lax.ppermute(carried[1], "tensor", back)
    groups.append(list(lax.optimization_barrier((low, high) + order.last)[:2]))
    work(size // 2, list(groups[-1]))
    return groups


def ring_gather(blocks, size, work, order, hold=()):
    groups, carried = ring_near(blocks, size, work, order, hold)
    return ring_far(groups, carried, size, work, order)


def relay_kernel(count, *refs):
    for i in range(count):
        refs[2 * count + i][...] = (
            refs[i][...].astype(jnp.float32) + refs[count + i][...].astype(jnp.float32)
        ).astype(jnp.bfloat16)


def relay(terms, got):
    rows, width = terms[0].shape
    tile = min(rows, 64)
    spec = pl.BlockSpec((tile, width), lambda i: (i, 0))
    count = len(terms)
    return pl.pallas_call(
        lambda *refs: relay_kernel(count, *refs),
        grid=(rows // tile,),
        in_specs=[spec] * (2 * count),
        out_specs=[spec] * count,
        out_shape=[jax.ShapeDtypeStruct((rows, width), jnp.bfloat16)] * count,
        compiler_params=kernel_params(),
        cost_estimate=SMALL_COST,
        name="relay",
    )(*terms, *got)


def ring_scatter(
    size, part, order, hold=(), first=(), between=None, after=None, got=None, came=None,
    eager=True,
):
    ahead, back = ring_pairs(size)
    send = lambda value, pairs: lax.ppermute(value, "tensor", pairs)
    low, high = part(size // 2)
    if hold:
        low, high = lax.optimization_barrier((low, high) + tuple(hold))[:2]
    from_left, from_right = [send(low, ahead), None], [None, send(high, back)]
    for step in range(size // 2 - 1, 0, -1):
        right_low, right_high, left_low, left_high = part(step)
        full = from_left[1] is not None
        if not full:
            if eager:
                early = send(right_high, ahead), send(left_low, back)
            if between is not None:
                between()
        arrived = [from_left[0], from_right[1]] + ([from_left[1], from_right[0]] if full else [])
        waited = (*first, *early) if eager and not full else tuple(first)
        if came is not None and not full:
            came[:] = arrived
        tied = order.turn(*arrived, *waited)
        arrived = tied[: len(arrived)]
        if eager and not full:
            early = tied[len(tied) - 2 :]
        terms = [right_low, left_high] + ([right_high, left_low] if full else [])
        passed = order.mark(*relay(terms, arrived))
        if got is not None:
            got[:] = passed
        if full:
            early = send(passed[2], ahead), send(passed[3], back)
        elif not eager:
            right_high, left_low = order.turn(right_high, left_low)
            early = send(right_high, ahead), send(left_low, back)
        from_left = [send(passed[0], ahead), early[0]]
        from_right = [early[1], send(passed[1], back)]
    if after is not None:
        after()
    own = part(0)
    if size == 2:
        return own, [from_left[0]], [from_right[1]]
    return own, [from_left[0], from_right[0]], [from_left[1], from_right[1]]


def sum_over(values, axis, beside=()):
    size = lax.axis_size(axis)
    if size & (size - 1):
        return lax.psum(values, axis)
    reach, beside = 1, list(beside)
    while reach < size:
        ways = 4 if size >= 4 * reach else 2
        values = values + sum(
            lax.ppermute(values, axis, [(i, i ^ (way * reach)) for i in range(size)])
            for way in range(1, ways)
        )
        if beside:
            values = lax.optimization_barrier((values, beside.pop(0)))[0]
        reach *= ways
    return values


def tile_of(width, most):
    return next(t for t in (most, 512, 256, 128) if t <= most and width % t == 0)


def kernel_params(mebibytes=56):
    return pltpu.CompilerParams(vmem_limit_bytes=mebibytes * 1024 * 1024)


SMALL_COST = pl.CostEstimate(flops=1_000_000, bytes_accessed=1_000_000, transcendentals=0)


class Piece:
    def __init__(self, array, count=None, index=0, entry=None, side=0, sides=1):
        self.array, self.count = array, count or array.shape[0]
        self.index, self.entry = index, entry
        self.side, self.columns = side, array.shape[1] // sides

    def row(self, table):
        return self.index if self.entry is None else table[self.entry]

    def spec(self, width=None):
        if width is None:
            return pl.BlockSpec(
                (self.count, self.columns),
                lambda i, table: (self.row(table), self.side),
                pipeline_mode=pl.Buffered(1),
            )
        return pl.BlockSpec((self.count, width), lambda i, table: (self.row(table), i))


def pieces_of(blocks):
    return [Piece(block) for block in blocks]


def stacked(refs):
    values = [ref[...] for ref in refs]
    return values[0] if len(values) == 1 else jnp.concatenate(values, axis=0)


def row_call(
    kernel, name, table, grid, operands, specs, outs, out_specs, aliases=None, mebibytes=56
):
    return pl.pallas_call(
        kernel,
        grid_spec=pltpu.PrefetchScalarGridSpec(
            num_scalar_prefetch=1, grid=grid, in_specs=specs, out_specs=out_specs
        ),
        out_shape=outs,
        input_output_aliases=aliases or {},
        compiler_params=kernel_params(mebibytes),
        cost_estimate=SMALL_COST,
        name=name,
    )(table, *operands)


def product_kernel(count, crossed, *refs):
    rows = stacked(refs[1 : 1 + count])
    matrix = refs[1 + count][...]
    result = contract_cols(rows, matrix) if crossed else product(rows, matrix)
    size = refs[-1].shape[0]
    outs = refs[-(rows.shape[0] // size) :]
    for i, out_ref in enumerate(outs):
        out_ref[...] = result[i * size : (i + 1) * size].astype(out_ref.dtype)


def block_product(table, pieces, matrix, crossed, parts=1, into=None):
    width = matrix.shape[0] if crossed else matrix.shape[1]
    tile = tile_of(width, 512)
    count = sum(piece.count for piece in pieces)
    if crossed:
        matrix_spec = pl.BlockSpec((tile, matrix.shape[1]), lambda i, table: (i, 0))
    else:
        matrix_spec = pl.BlockSpec((matrix.shape[0], tile), lambda i, table: (0, i))
    operands = [piece.array for piece in pieces] + [matrix]
    specs = [piece.spec() for piece in pieces] + [matrix_spec]
    aliases = {}
    index, all_rows = 0, count
    if into is not None:
        all_rows, index, so_far = into
        if so_far is not None:
            operands.append(so_far)
            specs.append(pl.BlockSpec(memory_space=pltpu.HBM))
            aliases = {len(operands): 0}
    if parts > 1:
        count = all_rows = count // parts
    out_spec = pl.BlockSpec((count, tile), lambda i, table: (index, i))
    out = jax.ShapeDtypeStruct((all_rows, width), jnp.bfloat16)
    result = row_call(
        lambda *refs: product_kernel(len(pieces), crossed, *refs),
        "block_product",
        table,
        (width // tile,),
        operands,
        specs,
        [out] * parts,
        [out_spec] * parts,
        aliases,
        56 if matrix.size > 4 * 1024 * 1024 else 32,
    )
    return result if parts > 1 else result[0]


def gate_kernel(count, *refs):
    rows = stacked(refs[1 : 1 + count])
    gate_ref, up_ref, activated_ref, gate_out, up_out = refs[1 + count :]
    gate = product(rows, gate_ref[...])
    up = product(rows, up_ref[...])
    activated_ref[...] = (gate * jax.nn.sigmoid(gate) * up).astype(jnp.bfloat16)
    gate_out[...] = gate.astype(gate_out.dtype)
    up_out[...] = up.astype(up_out.dtype)


def gate_up_product(table, pieces, matrix):
    depth, width = matrix.shape[0], matrix.shape[1] // 2
    count = sum(piece.count for piece in pieces)
    tile = tile_of(width, 256)
    steps = width // tile
    return row_call(
        lambda *refs: gate_kernel(len(pieces), *refs),
        "gate_up",
        table,
        (steps,),
        [piece.array for piece in pieces] + [matrix, matrix],
        [piece.spec() for piece in pieces]
        + [
            pl.BlockSpec((depth, tile), lambda i, table: (0, i)),
            pl.BlockSpec((depth, tile), lambda i, table: (0, steps + i)),
        ],
        [jax.ShapeDtypeStruct((count, width), jnp.bfloat16)] * 3,
        [pl.BlockSpec((count, tile), lambda i, table: (0, i))] * 3,
    )


def gate_grad_kernel(count, steps, *refs):
    down_ref, gate_ref, up_ref, matrix_ref, out_ref = refs[1 + count : 6 + count]
    part_refs = refs[6 + count :]
    step = pl.program_id(0)
    tile = gate_ref.shape[1]
    width = out_ref.shape[1] // 2

    @pl.when(step < steps)
    def _():
        grad = contract_cols(stacked(refs[1 : 1 + count]), down_ref[...])
        gate = gate_ref[...].astype(jnp.float32)
        up = up_ref[...].astype(jnp.float32)
        sigmoid_gate = jax.nn.sigmoid(gate)
        scaled = grad * sigmoid_gate
        start = pl.multiple_of(step * tile, tile)
        out_ref[:, pl.ds(start, tile)] = (
            scaled * up * (1.0 + gate * (1.0 - sigmoid_gate))
        ).astype(jnp.bfloat16)
        out_ref[:, pl.ds(pl.multiple_of(width + step * tile, tile), tile)] = (
            scaled * gate
        ).astype(jnp.bfloat16)

    @pl.when(step >= steps)
    def _():
        result = contract_cols(out_ref[...], matrix_ref[...])
        size = part_refs[0].shape[0]
        for i, part_ref in enumerate(part_refs):
            part_ref[...] = result[i * size : (i + 1) * size].astype(part_ref.dtype)


def gate_up_gradient(table, pieces, down, gate, up, matrix, parts):
    count, width = gate.shape
    tile = tile_of(width, 256)
    steps = width // tile
    out_width = matrix.shape[0]
    out_tile = tile_of(out_width, 512)
    first = lambda i: jnp.minimum(i, steps - 1)
    later = lambda i: jnp.maximum(i - steps, 0)
    part = pl.BlockSpec((count, tile), lambda i, table: (0, first(i)))
    grads, *products = row_call(
        lambda *refs: gate_grad_kernel(len(pieces), steps, *refs),
        "gate_up_grad",
        table,
        (steps + out_width // out_tile,),
        [piece.array for piece in pieces] + [down, gate, up, matrix],
        [piece.spec() for piece in pieces]
        + [
            pl.BlockSpec((tile, down.shape[1]), lambda i, table: (first(i), 0)),
            part,
            part,
            pl.BlockSpec((out_tile, 2 * width), lambda i, table: (later(i), 0)),
        ],
        [jax.ShapeDtypeStruct((count, 2 * width), jnp.bfloat16)]
        + [jax.ShapeDtypeStruct((count // parts, out_width), jnp.bfloat16)] * parts,
        [pl.BlockSpec((count, 2 * width), lambda i, table: (0, 0))]
        + [pl.BlockSpec((count // parts, out_tile), lambda i, table: (0, later(i)))] * parts,
    )
    return grads, products if parts > 1 else products[0]


def rows_kernel(count, weighed, *refs):
    out_ref = refs[2 * count + 1 + weighed]
    result = sum(contract_rows(refs[1 + i][...], refs[1 + count + i][...]) for i in range(count))
    out_ref[...] = result.astype(out_ref.dtype)
    if weighed:
        by_column = jnp.transpose(result * refs[2 * count + 1][...].astype(jnp.float32))
        refs[-1][...] = jnp.sum(by_column, axis=0, keepdims=True)


def weight_gradient(table, lefts, rights, weights=None):
    width, columns = lefts[0].array.shape[1], rights[0].columns
    tile = tile_of(width, 256)
    weighed = weights is not None
    block_spec = pl.BlockSpec((tile, columns), lambda i, table: (i, 0))
    result = row_call(
        lambda *refs: rows_kernel(len(lefts), weighed, *refs),
        "weight_grad",
        table,
        (width // tile,),
        [piece.array for piece in lefts + rights] + ([weights] if weighed else []),
        [piece.spec(tile) for piece in lefts]
        + [piece.spec() for piece in rights]
        + ([block_spec] if weighed else []),
        [jax.ShapeDtypeStruct((width, columns), jnp.bfloat16)]
        + ([jax.ShapeDtypeStruct((1, width), jnp.float32)] if weighed else []),
        [block_spec] + ([pl.BlockSpec((1, tile), lambda i, table: (0, i))] if weighed else []),
    )
    return result if weighed else result[0]


def split_groups(groups, half, side=0, sides=1):
    return [
        Piece(array, half, i, side=side, sides=sides)
        for array in groups
        for i in range(array.shape[0] // half)
    ]


def arrived_sum(split, low_refs, high_refs):
    low = sum(ref[...].astype(jnp.float32) for ref in low_refs)
    high = sum(ref[...].astype(jnp.float32) for ref in high_refs)
    return jnp.where(pl.program_id(0) < split, low, high)


def half_specs(tile, split, width):
    return (
        pl.BlockSpec((tile, width), lambda i: (jnp.minimum(i, split - 1), 0)),
        pl.BlockSpec((tile, width), lambda i: (jnp.maximum(i - split, 0), 0)),
    )


def put_half(split, low_ref, high_ref, value):
    @pl.when(pl.program_id(0) < split)
    def _():
        low_ref[...] = value

    @pl.when(pl.program_id(0) >= split)
    def _():
        high_ref[...] = value


def row_kernel_call(kernel, name, whole, lows, highs, gain, outs):
    rows, width = whole[0].shape
    tile = min(rows // 2, 128)
    split = rows // 2 // tile
    spec = pl.BlockSpec((tile, width), lambda i: (i, 0))
    low_spec, high_spec = half_specs(tile, split, width)
    row_spec = pl.BlockSpec((1, width), lambda i: (0, 0))
    shapes, specs = [], []
    for out in outs:
        if out == "halves":
            shapes += [jax.ShapeDtypeStruct((rows // 2, width), jnp.bfloat16)] * 2
            specs += [low_spec, high_spec]
        elif out == "row":
            shapes.append(jax.ShapeDtypeStruct((1, width), jnp.float32))
            specs.append(row_spec)
        else:
            shapes.append(jax.ShapeDtypeStruct((rows, width), out))
            specs.append(spec)
    return pl.pallas_call(
        lambda *refs: kernel(split, len(lows), *refs),
        grid=(2 * split,),
        in_specs=[spec] * len(whole)
        + [low_spec] * len(lows)
        + [high_spec] * len(highs)
        + [row_spec],
        out_specs=specs,
        out_shape=shapes,
        compiler_params=kernel_params(),
        cost_estimate=SMALL_COST,
        name=name,
    )(*whole, *lows, *highs, gain)


def add_norm_kernel(split, count, base_ref, own_ref, *refs):
    gain_ref, sum_ref, low_ref, high_ref = refs[2 * count :]
    values = base_ref[...].astype(jnp.float32) + own_ref[...].astype(jnp.float32)
    values = values + arrived_sum(split, refs[:count], refs[count : 2 * count])
    sum_ref[...] = values
    put_half(split, low_ref, high_ref, rms_gain(values, gain_ref[...]).astype(jnp.bfloat16))


def add_and_norm(base, own, lows, highs, gain):
    outs = (jnp.float32, "halves")
    return row_kernel_call(add_norm_kernel, "add_norm", [base, own], lows, highs, gain, outs)


def add_kernel(split, count, base_ref, own_ref, *refs):
    values = base_ref[...].astype(jnp.float32) + own_ref[...].astype(jnp.float32)
    values = values + arrived_sum(split, refs[:count], refs[count : 2 * count])
    refs[-1][...] = values.astype(jnp.bfloat16)


def norm_gradient_kernel(split, count, base_ref, value_ref, own_ref, *refs):
    gain_ref, outs = refs[2 * count], refs[2 * count + 1 :]
    grad = own_ref[...].astype(jnp.float32)
    grad = grad + arrived_sum(split, refs[:count], refs[count : 2 * count])
    values = value_ref[...].astype(jnp.float32)
    scale = lax.rsqrt(jnp.mean(values * values, axis=1, keepdims=True) + norm_eps)
    unit = values * scale
    inner = grad * gain_ref[...]
    result = base_ref[...].astype(jnp.float32) + scale * (
        inner - unit * jnp.mean(inner * unit, axis=1, keepdims=True)
    )
    if len(outs) == 1:
        outs[0][...] = result.astype(jnp.bfloat16)
        return
    low_ref, high_ref, whole_ref, gain_out = outs
    whole_ref[...] = result.astype(jnp.bfloat16)
    put_half(split, low_ref, high_ref, result.astype(jnp.bfloat16))

    @pl.when(pl.program_id(0) == 0)
    def _():
        gain_out[...] = jnp.zeros_like(gain_out)

    gain_out[...] += jnp.sum(grad * unit, axis=0, keepdims=True)


def norm_gradient(base, values, own, lows, highs, gain, outs):
    return row_kernel_call(
        norm_gradient_kernel, "norm_gradient", [base, values, own], lows, highs, gain, outs
    )


def project_kernel(count, *refs):
    rows = stacked(refs[1 : 1 + count])
    matrix_ref, gain_ref, cos_ref, sin_ref = refs[1 + count : 5 + count]
    query_ref, key_ref, value_ref, query_raw, key_raw = refs[-5:]
    width = HEAD_WIDTH
    mixed = product(rows, matrix_ref[...])
    cos, sin = cos_ref[...], sin_ref[...]
    for part in range(QUERY_PER_KEY + 1):
        values = mixed[:, part * width : (part + 1) * width]
        is_key = part == QUERY_PER_KEY
        gain = gain_ref[1:2, :] if is_key else gain_ref[0:1, :]
        scale = lax.rsqrt(jnp.mean(values * values, axis=1, keepdims=True) + norm_eps)
        scaled = values * scale * gain
        turned = scaled * cos + pltpu.roll(scaled, width // 2, 1) * sin
        if is_key:
            key_ref[...] = turned.astype(jnp.bfloat16)
            key_raw[...] = values
        else:
            query_ref[:, part * width : (part + 1) * width] = turned.astype(jnp.bfloat16)
            query_raw[:, part * width : (part + 1) * width] = values
    value_ref[...] = mixed[:, (QUERY_PER_KEY + 1) * width :].astype(jnp.bfloat16)


def project(blocks, matrix, gains, cos, sin, place, total_rows, before):
    count, depth = sum(block.shape[0] for block in blocks), matrix.shape[0]
    block = (QUERY_PER_KEY + 2) * HEAD_WIDTH
    heads = matrix.shape[1] // block
    wide = QUERY_PER_KEY * HEAD_WIDTH
    per_table = cos.shape[0] // count
    table_spec = pl.BlockSpec(
        (count, HEAD_WIDTH), lambda h, at: (lax.rem(at[0], per_table), 0)
    )
    widths = (wide, HEAD_WIDTH, HEAD_WIDTH, wide, HEAD_WIDTH)
    kinds = (jnp.bfloat16,) * 3 + (jnp.float32,) * 2
    kept = () if before is None else tuple(before)
    return pl.pallas_call(
        lambda *refs: project_kernel(len(blocks), *refs),
        grid_spec=pltpu.PrefetchScalarGridSpec(
            num_scalar_prefetch=1,
            grid=(heads,),
            in_specs=[
                pl.BlockSpec((rows.shape[0], depth), lambda h, at: (0, 0)) for rows in blocks
            ]
            + [
                pl.BlockSpec((depth, block), lambda h, at: (0, h)),
                pl.BlockSpec((2, HEAD_WIDTH), lambda h, at: (0, 0)),
                table_spec,
                table_spec,
            ]
            + [pl.BlockSpec(memory_space=pltpu.HBM)] * len(kept),
            out_specs=[pl.BlockSpec((count, w), lambda h, at: (at[0], h)) for w in widths],
        ),
        out_shape=[
            jax.ShapeDtypeStruct((total_rows, heads * w), kind) for w, kind in zip(widths, kinds)
        ],
        input_output_aliases={5 + len(blocks) + i: i for i in range(len(kept))},
        compiler_params=kernel_params(56),
        cost_estimate=SMALL_COST,
        name="project",
    )(place.reshape(1), *blocks, matrix, gains, cos, sin, *kept)


def causal(keys, queries):
    rows = lax.broadcasted_iota(jnp.int32, (keys, queries), 0)
    return rows <= lax.broadcasted_iota(jnp.int32, (keys, queries), 1)


def add_after(whole, part, low):
    if low == 0:
        return whole + part
    return jnp.concatenate([whole[:, :low], whole[:, low:] + part], axis=1)


def walk(visit, step, block, carry, pieces):
    carry = lax.fori_loop(
        0,
        step,
        lambda j, c: visit(pl.multiple_of(j * block, block), c, block, 0, False),
        carry,
    )
    start = pl.multiple_of(step * block, block)
    count = block // pieces
    for low in range(0, block, count):
        carry = visit(start + low, carry, count, low, True)
    return carry


def attend_kernel(scale, query_ref, key_ref, value_ref, out_ref, log_ref):
    block = query_ref.shape[0]
    width = key_ref.shape[1]
    group = query_ref.shape[1] // width
    step = pl.program_id(2)
    queries = [query_ref[:, g * width : (g + 1) * width] for g in range(group)]

    def visit(start, carry, count, low, masked):
        keys = key_ref[pl.ds(start, count), :]
        values = value_ref[pl.ds(start, count), :]
        new = []
        for g in range(group):
            total, acc = carry[g]
            weights = jnp.exp2(contract_cols(keys, queries[g][low:]) * (scale * log2_e))
            if masked:
                weights = jnp.where(causal(count, block - low), weights, 0.0)
            total = add_after(total, jnp.sum(weights, axis=0, keepdims=True), low)
            acc = add_after(acc, contract_rows(values, weights.astype(jnp.bfloat16)), low)
            new.append((total, acc))
        return tuple(new)

    carry = tuple(
        (jnp.zeros((1, block), jnp.float32), jnp.zeros((width, block), jnp.float32))
        for _ in range(group)
    )
    carry = walk(visit, step, block, carry, 1)
    for g in range(group):
        total, acc = carry[g]
        out_ref[:, g * width : (g + 1) * width] = jnp.transpose(acc / total).astype(jnp.bfloat16)
        log_ref[0, 0, g : g + 1, :] = jnp.log2(total)


def attention_forward(query, key, value, block):
    rows = query.shape[0]
    heads = key.shape[1] // HEAD_WIDTH
    steps = SEQUENCE_TOKENS // block
    wide = QUERY_PER_KEY * HEAD_WIDTH
    sequences = rows // SEQUENCE_TOKENS
    query_spec = pl.BlockSpec((block, wide), lambda h, s, i: (s * steps + i, h))
    key_spec = pl.BlockSpec((SEQUENCE_TOKENS, HEAD_WIDTH), lambda h, s, i: (s, h))
    return pl.pallas_call(
        lambda *refs: attend_kernel(HEAD_WIDTH ** (-0.5), *refs),
        grid=(heads, sequences, steps),
        in_specs=[query_spec, key_spec, key_spec],
        out_specs=[
            query_spec,
            pl.BlockSpec(
                (1, 1, QUERY_PER_KEY, block), lambda h, s, i: (h, s * steps + i, 0, 0)
            ),
        ],
        out_shape=[
            jax.ShapeDtypeStruct(query.shape, jnp.bfloat16),
            jax.ShapeDtypeStruct((heads, rows // block, QUERY_PER_KEY, block), jnp.float32),
        ],
        compiler_params=kernel_params(56),
        cost_estimate=SMALL_COST,
        name="attend",
    )(query, key, value)


def norm_back(values, grad, gain, cos, sin):
    width = values.shape[1]
    turned = grad * cos + pltpu.roll(grad * sin, width // 2, 1)
    scale = lax.rsqrt(jnp.mean(values * values, axis=1, keepdims=True) + norm_eps)
    unit = values * scale
    inner = turned * gain
    back = scale * (inner - unit * jnp.mean(inner * unit, axis=1, keepdims=True))
    return back.astype(jnp.bfloat16), jnp.sum(turned * unit, axis=0, keepdims=True)


def attend_back_kernel(
    scale,
    table_ref,
    query_ref,
    key_ref,
    value_ref,
    grad_ref,
    context_ref,
    log_ref,
    query_raw,
    key_raw,
    gain_ref,
    cos_ref,
    sin_ref,
    *refs,
):
    mixed_out, gain_out, key_sum, value_sum = refs[-4:]
    block = query_ref.shape[0]
    width = key_ref.shape[1]
    group = query_ref.shape[1] // width
    sequence, step = pl.program_id(0), pl.program_id(1)
    @pl.when(step == 0)
    def _():
        key_sum[...] = jnp.zeros_like(key_sum)
        value_sum[...] = jnp.zeros_like(value_sum)

    @pl.when((step == 0) & (sequence == 0))
    def _():
        gain_out[...] = jnp.zeros_like(gain_out)

    queries, grads, logs, dots = [], [], [], []
    for g in range(group):
        cols = slice(g * width, (g + 1) * width)
        queries.append(query_ref[:, cols])
        grads.append(grad_ref[:, cols])
        logs.append(log_ref[0, 0, g : g + 1, :])
        both = grads[g].astype(jnp.float32) * context_ref[:, cols].astype(jnp.float32)
        dots.append(jnp.sum(jnp.transpose(both), axis=0, keepdims=True))

    def visit(start, carry, count, low, masked):
        rows = pl.ds(start, count)
        keys = key_ref[rows, :]
        values = value_ref[rows, :]
        new = []
        key_part = value_part = None
        for g in range(group):
            seen, sought = queries[g][low:], grads[g][low:]
            weights = jnp.exp2(contract_cols(keys, seen) * (scale * log2_e) - logs[g][:, low:])
            if masked:
                weights = jnp.where(causal(count, block - low), weights, 0.0)
            slope = contract_cols(values, sought)
            score = (weights * (slope - dots[g][:, low:])).astype(jnp.bfloat16)
            value_g = product(weights.astype(jnp.bfloat16), sought)
            key_g = product(score, seen)
            key_part = key_g if key_part is None else key_part + key_g
            value_part = value_g if value_part is None else value_part + value_g
            new.append(add_after(carry[g], contract_rows(keys, score), low))
        key_sum[rows, :] += key_part
        value_sum[rows, :] += value_part
        return tuple(new)

    carry = tuple(jnp.zeros((width, block), jnp.float32) for _ in range(group))
    carry = walk(visit, step, block, carry, 2)
    rows = pl.ds(pl.multiple_of(step * block, block), block)
    cos, sin = cos_ref[rows, :], sin_ref[rows, :]
    for g in range(group):
        cols = slice(g * width, (g + 1) * width)
        back, gain = norm_back(
            query_raw[:, cols], jnp.transpose(carry[g]) * scale, gain_ref[0:1, :], cos, sin
        )
        mixed_out[rows, cols] = back
        gain_out[0:1, :] += gain

    @pl.when(step == pl.num_programs(1) - 1)
    def _():
        def finish(j, _):
            rows = pl.ds(pl.multiple_of(j * block, block), block)
            back, gain = norm_back(
                key_raw[rows, :],
                key_sum[rows, :] * scale,
                gain_ref[1:2, :],
                cos_ref[rows, :],
                sin_ref[rows, :],
            )
            mixed_out[rows, group * width : (group + 1) * width] = back
            mixed_out[rows, (group + 1) * width :] = value_sum[rows, :].astype(jnp.bfloat16)
            gain_out[1:2, :] += gain
            return 0

        lax.fori_loop(0, pl.num_programs(1), finish, 0)


def attention_backward(
    slots, query, key, value, grad, context, logs, query_raw, key_raw, gains, cos, sin, head, before
):
    rows = query.shape[0]
    block = logs.shape[-1]
    steps = SEQUENCE_TOKENS // block
    wide = QUERY_PER_KEY * HEAD_WIDTH
    heads = key.shape[1] // HEAD_WIDTH
    sequences = rows // SEQUENCE_TOKENS
    mixed = (QUERY_PER_KEY + 2) * HEAD_WIDTH
    query_spec = pl.BlockSpec((block, wide), lambda s, i, slots: (s * steps + i, head))
    key_spec = pl.BlockSpec((SEQUENCE_TOKENS, HEAD_WIDTH), lambda s, i, slots: (s, head))
    table_spec = pl.BlockSpec((SEQUENCE_TOKENS, HEAD_WIDTH), lambda s, i, slots: (0, 0))
    gain_spec = pl.BlockSpec((2, HEAD_WIDTH), lambda s, i, slots: (0, 0))
    kept = () if before is None else (before,)
    return pl.pallas_call(
        lambda *refs: attend_back_kernel(HEAD_WIDTH ** (-0.5), *refs),
        grid_spec=pltpu.PrefetchScalarGridSpec(
            num_scalar_prefetch=1,
            grid=(sequences, steps),
            in_specs=[
            query_spec,
            key_spec,
            key_spec,
            pl.BlockSpec((block, wide), lambda s, i, slots: (slots[s * steps + i], head)),
            query_spec,
            pl.BlockSpec(
                (1, 1, QUERY_PER_KEY, block), lambda s, i, slots: (head, s * steps + i, 0, 0)
            ),
            query_spec,
            key_spec,
            gain_spec,
            table_spec,
            table_spec,
        ]
        + [pl.BlockSpec(memory_space=pltpu.HBM)] * len(kept),
        out_specs=[
            pl.BlockSpec((SEQUENCE_TOKENS, mixed), lambda s, i, slots: (s, head)),
            gain_spec,
        ],
        scratch_shapes=[pltpu.VMEM((SEQUENCE_TOKENS, HEAD_WIDTH), jnp.float32)] * 2,
        ),
        out_shape=[
            jax.ShapeDtypeStruct((rows, heads * mixed), jnp.bfloat16),
            jax.ShapeDtypeStruct((2, HEAD_WIDTH), jnp.float32),
        ],
        input_output_aliases={12: 0} if kept else {},
        compiler_params=kernel_params(56),
        cost_estimate=SMALL_COST,
        name="attend_back",
    )(slots, query, key, value, grad, context, logs, query_raw, key_raw, gains, cos, sin, *kept)


def local(
    inputs,
    input_projection_weight,
    input_first_moment,
    input_second_moment,
    out_weight,
    out_mean,
    out_square,
    swiglu_weight,
    swiglu_mean,
    swiglu_square,
    down_weight,
    down_mean,
    down_square,
    norm_gains,
    norm_mean,
    norm_square,
    qknorm_gains,
    qknorm_mean,
    qknorm_square,
    cotangent,
):
    size = lax.axis_size("tensor")
    rows = inputs.shape[0]
    half = rows // 2
    group_rows = rows * size
    last = size // 2
    dp_rows = input_projection_weight.shape[0]
    local_kv = input_projection_weight.shape[1]
    local_ff = swiglu_weight.shape[2]
    me = ring_place(lax.axis_index("tensor"), size)
    places = [ring_place((me + d + size) % size, size) for d in ring_offsets(size)]
    group_places = [places[:1]]
    for step in range(1, last):
        group_places.append(places[2 * step - 1 : 2 * step + 1])
    group_places.append(places[-1:])
    halves = [2 * place + i for place in places for i in range(2)]
    table = jnp.stack(places + halves).astype(jnp.int32)
    away = (ring_place(jnp.arange(size, dtype=jnp.int32), size) - me + size) % size
    slots = jnp.where(
        away == 0,
        size - 2,
        jnp.where(
            away == last,
            size - 1,
            jnp.where(away < last, 2 * away - 2, 2 * (size - away) - 1),
        ),
    ).astype(jnp.int32)
    order = Order()
    turn, mark = order.turn, order.mark
    tie = lax.optimization_barrier

    def ordered(array, group):
        entries = [0] if group == 0 else [2 * group - 1, 2 * group]
        if group == last:
            entries = [size - 1]
        return [Piece(array, rows, entry=entry) for entry in entries]

    def ordered_finely(array):
        return [Piece(array, half, entry=size + i) for i in range(2 * size)]

    def flat(groups):
        return pieces_of([block for group in groups for block in group])

    def parts_of(group):
        return 1 if group == 0 else 2 if group == last else 4

    def marked(part):
        return mark(*part) if isinstance(part, (list, tuple)) else mark(part)

    in_low = input_projection_weight.astype(jnp.bfloat16).reshape(dp_rows, -1)
    out_low = out_weight.astype(jnp.bfloat16)
    swiglu_low = swiglu_weight.astype(jnp.bfloat16).reshape(dp_rows, 2 * local_ff)
    down_low = down_weight.astype(jnp.bfloat16)
    in_matrix = lax.all_gather(in_low, "dp", axis=0, tiled=True)
    out_full = lax.all_gather(out_low, "dp", axis=1, tiled=True)
    swiglu_matrix = lax.all_gather(swiglu_low, "dp", axis=0, tiled=True)
    down_full = lax.all_gather(down_low, "dp", axis=1, tiled=True)

    normed_f = rms_gain(inputs.astype(jnp.float32), norm_gains[0])
    cos, sin = rotary_tables(SEQUENCE_TOKENS, HEAD_WIDTH)
    projected = []

    def project_group(group, blocks):
        calls = [blocks] if group in (0, last) else [blocks[:2], blocks[2:]]
        for place, call in zip(group_places[group], calls):
            call[0] = turn(call[0])
            projected[:] = mark(
                *project(
                    call, in_matrix, qknorm_gains, cos, sin, place, group_rows, projected or None
                )
            )

    normed = normed_f.astype(jnp.bfloat16)
    normed_groups = ring_gather(
        (normed[:half], normed[half:]), size, project_group, order, hold=(in_matrix,)
    )
    query, key, value, query_raw, key_raw = projected
    cotangent_sent = tie((cotangent, *normed_groups[-1]))[0]

    context, logs = mark(*attention_forward(query, key, value, rows))
    cot_groups, cot_carried = ring_near(
        (cotangent_sent[:half], cotangent_sent[half:]), size, lambda group, blocks: None, Order()
    )

    def out_group(group):
        return marked(
            block_product(
                table, ordered(turn(context), group), out_full, False, parts_of(group)
            )
        )

    own, lows, highs = ring_scatter(
        size, out_group, order, first=[half for group in cot_groups[1:] for half in group]
    )
    lows, highs = tie((lows, highs, swiglu_matrix))[:2]
    hidden, *two_halves = mark(*add_and_norm(inputs, own, lows, highs, norm_gains[1:2]))

    gate_groups = []
    grads = [None] * (last + 1)

    def gate_group(group, blocks):
        blocks[0] = turn(blocks[0])
        gate_groups.append(mark(*gate_up_product(table, pieces_of(blocks), swiglu_matrix)))

    two_groups, two_carried = ring_near(two_halves, size, gate_group, order)
    two_groups = ring_far(two_groups, two_carried, size, gate_group, order)
    cot_carried = tie((*cot_carried, *gate_groups[last - 1]))[:2]
    cot_groups = ring_far(cot_groups, cot_carried, size, lambda group, blocks: None, order)
    activated = [parts[0] for parts in gate_groups]
    two_parts = [None] * (last + 1)

    def two_part(group):
        cots = [turn(cot_groups[group][0])] + cot_groups[group][1:]
        grads[group], part = gate_up_gradient(
            table,
            pieces_of(cots),
            down_full,
            *gate_groups[group][1:],
            swiglu_matrix,
            parts_of(group),
        )
        two_parts[group] = marked(part)

    for group in range(1, last):
        two_part(group)
    lefts = split_groups([turn(activated[0])] + activated[1:], half)
    down_part = mark(weight_gradient(table, lefts, flat(cot_groups)))
    down_grad = lax.psum_scatter(down_part, "dp", scatter_dimension=1, tiled=True)
    two_part(last)
    more = []

    def own_part():
        two_part(0)

    def swiglu_gradient():
        twos = flat(two_groups)
        twos[0].array = turn(twos[0].array)
        side = len(more)
        more.append(mark(weight_gradient(table, twos, split_groups(grads, half, side, 2))))

    if last == 1:
        own_part()
    own, lows, highs = ring_scatter(
        size, lambda group: two_parts[group], order, between=own_part, after=swiglu_gradient
    )
    swiglu_part, lows, highs = tie((more[0], lows, highs))
    gate_weight_grad = lax.psum_scatter(swiglu_part, "dp", scatter_dimension=0, tiled=True)
    *attended_halves, hidden_grad, mlp_gain_grad = mark(
        *norm_gradient(
            cotangent, hidden, own, lows, highs, norm_gains[1:2], ("halves", jnp.bfloat16, "row")
        )
    )

    context_grad, down_parts, new_down, head_grads = [None], [None] * (last + 1), [], []

    def context_group(group, blocks):
        blocks[0] = turn(blocks[0])
        index = size - 2 if group == 0 else size - 1 if group == last else group - 1
        context_grad[0] = mark(
            block_product(
                table, pieces_of(blocks), out_full, True, into=(group_rows, index, context_grad[0])
            )
        )
        if group == 0:
            for other in range(last, -1, -1):
                down_parts[other] = marked(
                    block_product(
                        table, [Piece(turn(activated[other]))], down_full, False, parts_of(other)
                    )
                )
            new_down[:] = mark(
                turn(down_grad).astype(jnp.float32),
                *adamw(
                    down_weight,
                    turn(down_grad).astype(jnp.float32),
                    down_mean,
                    down_square,
                    FF ** (-0.5),
                ),
            )
        if group == last - 1:
            swiglu_gradient()

    attended_groups = ring_gather(attended_halves, size, context_group, order)
    swiglu_part = tie((more[1], *attended_groups[last]))[0]
    up_weight_grad = lax.psum_scatter(swiglu_part, "dp", scatter_dimension=0, tiled=True)

    def head_backward(head):
        head_grads.append(
            mark(
                *attention_backward(
                    slots, turn(query), key, value, context_grad[0], context, logs, query_raw,
                    key_raw, qknorm_gains, cos, sin, head,
                    head_grads[-1][0] if head_grads else None,
                )
            )
        )

    out_part = mark(
        weight_gradient(table, ordered_finely(turn(context)), flat(attended_groups))
    )
    if last == 1:
        head_backward(0)

    def other_heads():
        for head in range(1, local_kv):
            head_backward(head)

    own, lows, highs = ring_scatter(
        size,
        lambda group: down_parts[group],
        order,
        hold=attended_groups[-1],
        between=lambda: head_backward(0),
        after=other_heads,
    )
    sent, outputs = (own, lows, highs), []
    mixed_grad = head_grads[-1][0]
    qknorm_part = sum(pair[1] for pair in head_grads)
    in_parts = []

    def normed_group(group):
        return marked(
            block_product(
                table, ordered(turn(mixed_grad), group), in_matrix, True, parts_of(group)
            )
        )

    def in_gradient():
        normeds = flat(normed_groups)
        normeds[0].array = turn(normeds[0].array)
        in_parts[:] = mark(
            *weight_gradient(table, normeds, ordered_finely(mixed_grad), in_matrix)
        )
        own, lows, highs = sent
        outputs[:] = mark(
            *row_kernel_call(
                add_kernel,
                "add",
                [hidden, turn(own)],
                lows,
                highs,
                norm_gains[0:1],
                (jnp.bfloat16,),
            ),
            in_parts[0],
        )[:1]

    got = []
    own, lows, highs = ring_scatter(size, normed_group, order, between=in_gradient, got=got)
    if not in_parts:
        in_gradient()
    rows_of_gains = jnp.concatenate([in_parts[1] / norm_gains[0:1], mlp_gain_grad], axis=0)
    gain_sums = jnp.concatenate([rows_of_gains, qknorm_part], axis=1)
    (outputs,) = outputs
    gain_sums = tie((gain_sums, own, *got))[0]
    gain_sums = sum_over(gain_sums, "tensor")
    out_part, gate_weight_grad = tie((out_part, gate_weight_grad, sent, mixed_grad))[:2]
    out_grad = lax.psum_scatter(out_part, "dp", scatter_dimension=1, tiled=True)
    in_part, up_weight_grad = tie((in_parts[0], up_weight_grad, *got))[:2]
    in_grad = lax.psum_scatter(in_part, "dp", scatter_dimension=0, tiled=True)
    out_grad, gate_weight_grad = tie((out_grad, gate_weight_grad, *got))[:2]
    out_grad = out_grad.astype(jnp.float32)
    out_new, out_second = adamw(
        out_weight, out_grad, out_mean, out_square, (HQ * HEAD_WIDTH / 8.0) ** (-0.5)
    )
    swiglu_grad, swiglu_new, swiglu_second = adamw_parts(
        swiglu_weight,
        (gate_weight_grad, up_weight_grad),
        swiglu_mean,
        swiglu_square,
        MODEL_WIDTH ** (-0.5),
    )
    down_grad, down_new, down_second = new_down
    (
        lows,
        highs,
        own,
        outputs,
        out_grad,
        out_new,
        out_second,
        swiglu_grad,
        swiglu_new,
        swiglu_second,
    ) = tie(
        (
            lows,
            highs,
            own,
            outputs,
            out_grad,
            out_new,
            out_second,
            swiglu_grad,
            swiglu_new,
            swiglu_second,
        )
    )
    (input_grad,) = norm_gradient(
        hidden_grad, inputs, own, lows, highs, norm_gains[0:1], (jnp.bfloat16,)
    )
    in_grad, in_new, in_second = adamw_parts(
        input_projection_weight,
        (in_grad,),
        input_first_moment,
        input_second_moment,
        MODEL_WIDTH ** (-0.5),
    )
    gain_sums = sum_over(tie((gain_sums, *lows, *highs))[0], "dp", (input_grad, in_new))
    norm_grad, qknorm_grad = gain_sums[:, :MODEL_WIDTH], gain_sums[:, MODEL_WIDTH:]
    norm_new, norm_second = adamw(norm_gains, norm_grad, norm_mean, norm_square, gain_rate)
    qknorm_new, qknorm_second = adamw(
        qknorm_gains, qknorm_grad, qknorm_mean, qknorm_square, gain_rate
    )
    return (
        outputs,
        input_grad,
        in_grad,
        in_new,
        in_second,
        out_grad,
        out_new,
        out_second,
        swiglu_grad,
        swiglu_new,
        swiglu_second,
        down_grad,
        down_new,
        down_second,
        norm_grad,
        norm_new,
        norm_second,
        qknorm_grad,
        qknorm_new,
        qknorm_second,
    )


def solution(mesh):
    return jax.shard_map(
        local,
        mesh=mesh,
        in_specs=(
            P(("dp", "tensor"), None),
            P("dp", "tensor", None),
            P("dp", "tensor", None),
            P("dp", "tensor", None),
            P("tensor", "dp"),
            P("tensor", "dp"),
            P("tensor", "dp"),
            P("dp", None, "tensor"),
            P("dp", None, "tensor"),
            P("dp", None, "tensor"),
            P("tensor", "dp"),
            P("tensor", "dp"),
            P("tensor", "dp"),
            P(),
            P(),
            P(),
            P(),
            P(),
            P(),
            P(("dp", "tensor"), None),
        ),
        out_specs=(
            P(("dp", "tensor"), None),
            P(("dp", "tensor"), None),
            P("dp", "tensor", None),
            P("dp", "tensor", None),
            P("dp", "tensor", None),
            P("tensor", "dp"),
            P("tensor", "dp"),
            P("tensor", "dp"),
            P("dp", None, "tensor"),
            P("dp", None, "tensor"),
            P("dp", None, "tensor"),
            P("tensor", "dp"),
            P("tensor", "dp"),
            P("tensor", "dp"),
            P(),
            P(),
            P(),
            P(),
            P(),
            P(),
        ),
        check_vma=False,
    )
```

```python
import jax
import jax.numpy as jnp
from jax import lax
from jax.experimental import pallas as pl
from jax.experimental.pallas import tpu as pltpu
from jax.sharding import PartitionSpec as P

MODEL_WIDTH = 2048
HQ = 16
HEAD_WIDTH = 128
FF = 6144
QUERY_PER_KEY = 2
SEQUENCE_TOKENS = 2048


norm_eps = 1e-06
rope_base = 1000000.0
beta_one = 0.5
beta_two = 0.55
step_count = 5.0
adam_eps = 1e-08
decay_rate = 0.1
gain_rate = 0.3
masked_score = -1e30
log2_e = 1.4426950408889634


def rms_gain(values, gain_row):
    return (
        values * lax.rsqrt(jnp.mean(values * values, axis=-1, keepdims=True) + norm_eps) * gain_row
    )


def rotary_tables(length, width):
    frequency = rope_base ** (
        -2.0 * jnp.arange(width // 2, dtype=jnp.int32).astype(jnp.float32) / width
    )
    angles = jnp.arange(length, dtype=jnp.int32).astype(jnp.float32)[:, None] * frequency[None, :]
    cos, sin = jnp.cos(angles), jnp.sin(angles)
    return jnp.concatenate([cos, cos], axis=1), jnp.concatenate([-sin, sin], axis=1)


def contract_rows(left, right):
    return lax.dot_general(
        left, right, (((0,), (0,)), ((), ())), preferred_element_type=jnp.float32
    )


def contract_cols(left, right):
    return lax.dot_general(
        left, right, (((1,), (1,)), ((), ())), preferred_element_type=jnp.float32
    )


def product(left, right):
    return jnp.dot(left, right, preferred_element_type=jnp.float32)


def adamw(weight, gradient, mean_old, square_old, rate):
    mean_new = beta_one * mean_old + (1.0 - beta_one) * gradient
    square_new = beta_two * square_old + (1.0 - beta_two) * gradient * gradient
    mean_hat = mean_new / (1.0 - beta_one**step_count)
    square_hat = square_new / (1.0 - beta_two**step_count)
    weight_new = weight - rate * (
        mean_hat / (jnp.sqrt(square_hat) + adam_eps) + decay_rate * weight
    )
    return (weight_new, square_new)


def adam_kernel(rate, weight_ref, mean_ref, square_ref, *refs):
    *grad_refs, grad_out, new_out, second_out = refs
    width = weight_ref.shape[2]
    for part in range(weight_ref.shape[1]):
        start = part * width
        for grad_ref in grad_refs:
            if start < grad_ref.shape[1]:
                break
            start -= grad_ref.shape[1]
        grad = grad_ref[:, start : start + width].astype(jnp.float32)
        new, second = adamw(
            weight_ref[:, part, :], grad, mean_ref[:, part, :], square_ref[:, part, :], rate
        )
        grad_out[:, part, :] = grad
        new_out[:, part, :] = new
        second_out[:, part, :] = second


def adamw_parts(weight, grads, mean_old, square_old, rate):
    rows, parts, width = weight.shape
    tile = min(rows, 64)
    spec = pl.BlockSpec((tile, parts, width), lambda i: (i, 0, 0))
    return pl.pallas_call(
        lambda *refs: adam_kernel(rate, *refs),
        grid=(rows // tile,),
        in_specs=[spec] * 3
        + [pl.BlockSpec((tile, grad.shape[1]), lambda i: (i, 0)) for grad in grads],
        out_specs=[spec] * 3,
        out_shape=[jax.ShapeDtypeStruct(weight.shape, jnp.float32)] * 3,
        compiler_params=kernel_params(),
        cost_estimate=SMALL_COST,
        name="adamw",
    )(weight, mean_old, square_old, *grads)


def ring_place(index, size):
    return jnp.where(index < size // 2, index, size // 2 + size - 1 - index)


def ring_pairs(size):
    half = size // 2
    order = list(range(half)) + list(range(size - 1, half - 1, -1))
    ahead = [(order[r], order[(r + 1) % size]) for r in range(size)]
    return ahead, [(b, a) for a, b in ahead]


def ring_offsets(size):
    offsets = [0]
    for step in range(1, size // 2):
        offsets += [step, -step]
    return offsets + [size // 2]


class Order:
    def __init__(self):
        self.last = ()

    def turn(self, *values):
        tied = lax.optimization_barrier(values + self.last)[: len(values)]
        return tied[0] if len(values) == 1 else tied

    def mark(self, *values):
        self.last = values
        return values[0] if len(values) == 1 else values


def ring_near(blocks, size, work, order, hold=()):
    ahead, back = ring_pairs(size)
    tie = lax.optimization_barrier
    groups = [list(blocks)]
    left, right = list(blocks), list(blocks)
    work(0, list(blocks))
    for step in range(1, size // 2):
        left_low = lax.ppermute(left[0], "tensor", ahead)
        right_high = lax.ppermute(right[1], "tensor", back)
        left_high = lax.ppermute(left[1], "tensor", ahead)
        right_low = lax.ppermute(right[0], "tensor", back)
        held = tuple(hold) if step == size // 2 - 1 else ()
        left_low, right_high = tie((left_low, right_high) + held + order.last)[:2]
        left, right = [left_low, left_high], [right_low, right_high]
        pair = tie((*right, *left) + order.last)[:4]
        groups.append(list(pair))
        work(step, list(pair))
    return groups, (left[0], right[1])


def ring_far(groups, carried, size, work, order):
    ahead, back = ring_pairs(size)
    low = lax.ppermute(carried[0], "tensor", ahead)
    high = lax.ppermute(carried[1], "tensor", back)
    groups.append(list(lax.optimization_barrier((low, high) + order.last)[:2]))
    work(size // 2, list(groups[-1]))
    return groups


def ring_gather(blocks, size, work, order, hold=()):
    groups, carried = ring_near(blocks, size, work, order, hold)
    return ring_far(groups, carried, size, work, order)


def relay_kernel(count, *refs):
    for i in range(count):
        refs[2 * count + i][...] = (
            refs[i][...].astype(jnp.float32) + refs[count + i][...].astype(jnp.float32)
        ).astype(jnp.bfloat16)


def relay(terms, got):
    rows, width = terms[0].shape
    tile = min(rows, 64)
    spec = pl.BlockSpec((tile, width), lambda i: (i, 0))
    count = len(terms)
    return pl.pallas_call(
        lambda *refs: relay_kernel(count, *refs),
        grid=(rows // tile,),
        in_specs=[spec] * (2 * count),
        out_specs=[spec] * count,
        out_shape=[jax.ShapeDtypeStruct((rows, width), jnp.bfloat16)] * count,
        compiler_params=kernel_params(),
        cost_estimate=SMALL_COST,
        name="relay",
    )(*terms, *got)


def ring_scatter(
    size, part, order, hold=(), first=(), between=None, after=None, got=None, came=None,
    eager=True,
):
    ahead, back = ring_pairs(size)
    send = lambda value, pairs: lax.ppermute(value, "tensor", pairs)
    low, high = part(size // 2)
    if hold:
        low, high = lax.optimization_barrier((low, high) + tuple(hold))[:2]
    from_left, from_right = [send(low, ahead), None], [None, send(high, back)]
    for step in range(size // 2 - 1, 0, -1):
        right_low, right_high, left_low, left_high = part(step)
        full = from_left[1] is not None
        if not full:
            if eager:
                early = send(right_high, ahead), send(left_low, back)
            if between is not None:
                between()
        arrived = [from_left[0], from_right[1]] + ([from_left[1], from_right[0]] if full else [])
        waited = (*first, *early) if eager and not full else tuple(first)
        if came is not None and not full:
            came[:] = arrived
        tied = order.turn(*arrived, *waited)
        arrived = tied[: len(arrived)]
        if eager and not full:
            early = tied[len(tied) - 2 :]
        terms = [right_low, left_high] + ([right_high, left_low] if full else [])
        passed = order.mark(*relay(terms, arrived))
        if got is not None:
            got[:] = passed
        if full:
            early = send(passed[2], ahead), send(passed[3], back)
        elif not eager:
            right_high, left_low = order.turn(right_high, left_low)
            early = send(right_high, ahead), send(left_low, back)
        from_left = [send(passed[0], ahead), early[0]]
        from_right = [early[1], send(passed[1], back)]
    if after is not None:
        after()
    own = part(0)
    if size == 2:
        return own, [from_left[0]], [from_right[1]]
    return own, [from_left[0], from_right[0]], [from_left[1], from_right[1]]


def sum_over(values, axis, beside=()):
    size = lax.axis_size(axis)
    if size & (size - 1):
        return lax.psum(values, axis)
    reach, beside = 1, list(beside)
    while reach < size:
        ways = 4 if size >= 4 * reach else 2
        values = values + sum(
            lax.ppermute(values, axis, [(i, i ^ (way * reach)) for i in range(size)])
            for way in range(1, ways)
        )
        if beside:
            values = lax.optimization_barrier((values, beside.pop(0)))[0]
        reach *= ways
    return values


def tile_of(width, most):
    return next(t for t in (most, 512, 256, 128) if t <= most and width % t == 0)


def kernel_params(mebibytes=56):
    return pltpu.CompilerParams(vmem_limit_bytes=mebibytes * 1024 * 1024)


SMALL_COST = pl.CostEstimate(flops=1_000_000, bytes_accessed=1_000_000, transcendentals=0)


class Piece:
    def __init__(self, array, count=None, index=0, entry=None, side=0, sides=1):
        self.array, self.count = array, count or array.shape[0]
        self.index, self.entry = index, entry
        self.side, self.columns = side, array.shape[1] // sides

    def row(self, table):
        return self.index if self.entry is None else table[self.entry]

    def spec(self, width=None):
        if width is None:
            return pl.BlockSpec(
                (self.count, self.columns),
                lambda i, table: (self.row(table), self.side),
                pipeline_mode=pl.Buffered(1),
            )
        return pl.BlockSpec((self.count, width), lambda i, table: (self.row(table), i))


def pieces_of(blocks):
    return [Piece(block) for block in blocks]


def stacked(refs):
    values = [ref[...] for ref in refs]
    return values[0] if len(values) == 1 else jnp.concatenate(values, axis=0)


def row_call(
    kernel, name, table, grid, operands, specs, outs, out_specs, aliases=None, mebibytes=56
):
    return pl.pallas_call(
        kernel,
        grid_spec=pltpu.PrefetchScalarGridSpec(
            num_scalar_prefetch=1, grid=grid, in_specs=specs, out_specs=out_specs
        ),
        out_shape=outs,
        input_output_aliases=aliases or {},
        compiler_params=kernel_params(mebibytes),
        cost_estimate=SMALL_COST,
        name=name,
    )(table, *operands)


def product_kernel(count, crossed, *refs):
    rows = stacked(refs[1 : 1 + count])
    matrix = refs[1 + count][...]
    result = contract_cols(rows, matrix) if crossed else product(rows, matrix)
    size = refs[-1].shape[0]
    outs = refs[-(rows.shape[0] // size) :]
    for i, out_ref in enumerate(outs):
        out_ref[...] = result[i * size : (i + 1) * size].astype(out_ref.dtype)


def block_product(table, pieces, matrix, crossed, parts=1, into=None):
    width = matrix.shape[0] if crossed else matrix.shape[1]
    tile = tile_of(width, 512)
    count = sum(piece.count for piece in pieces)
    if crossed:
        matrix_spec = pl.BlockSpec((tile, matrix.shape[1]), lambda i, table: (i, 0))
    else:
        matrix_spec = pl.BlockSpec((matrix.shape[0], tile), lambda i, table: (0, i))
    operands = [piece.array for piece in pieces] + [matrix]
    specs = [piece.spec() for piece in pieces] + [matrix_spec]
    aliases = {}
    index, all_rows = 0, count
    if into is not None:
        all_rows, index, so_far = into
        if so_far is not None:
            operands.append(so_far)
            specs.append(pl.BlockSpec(memory_space=pltpu.HBM))
            aliases = {len(operands): 0}
    if parts > 1:
        count = all_rows = count // parts
    out_spec = pl.BlockSpec((count, tile), lambda i, table: (index, i))
    out = jax.ShapeDtypeStruct((all_rows, width), jnp.bfloat16)
    result = row_call(
        lambda *refs: product_kernel(len(pieces), crossed, *refs),
        "block_product",
        table,
        (width // tile,),
        operands,
        specs,
        [out] * parts,
        [out_spec] * parts,
        aliases,
        56 if matrix.size > 4 * 1024 * 1024 else 32,
    )
    return result if parts > 1 else result[0]


def gate_kernel(count, *refs):
    rows = stacked(refs[1 : 1 + count])
    gate_ref, up_ref, activated_ref, gate_out, up_out = refs[1 + count :]
    gate = product(rows, gate_ref[...])
    up = product(rows, up_ref[...])
    activated_ref[...] = (gate * jax.nn.sigmoid(gate) * up).astype(jnp.bfloat16)
    gate_out[...] = gate.astype(gate_out.dtype)
    up_out[...] = up.astype(up_out.dtype)


def gate_up_product(table, pieces, matrix):
    depth, width = matrix.shape[0], matrix.shape[1] // 2
    count = sum(piece.count for piece in pieces)
    tile = tile_of(width, 256)
    steps = width // tile
    return row_call(
        lambda *refs: gate_kernel(len(pieces), *refs),
        "gate_up",
        table,
        (steps,),
        [piece.array for piece in pieces] + [matrix, matrix],
        [piece.spec() for piece in pieces]
        + [
            pl.BlockSpec((depth, tile), lambda i, table: (0, i)),
            pl.BlockSpec((depth, tile), lambda i, table: (0, steps + i)),
        ],
        [jax.ShapeDtypeStruct((count, width), jnp.bfloat16)] * 3,
        [pl.BlockSpec((count, tile), lambda i, table: (0, i))] * 3,
    )


def gate_grad_kernel(count, steps, *refs):
    down_ref, gate_ref, up_ref, matrix_ref, out_ref = refs[1 + count : 6 + count]
    part_refs = refs[6 + count :]
    step = pl.program_id(0)
    tile = gate_ref.shape[1]
    width = out_ref.shape[1] // 2

    @pl.when(step < steps)
    def _():
        grad = contract_cols(stacked(refs[1 : 1 + count]), down_ref[...])
        gate = gate_ref[...].astype(jnp.float32)
        up = up_ref[...].astype(jnp.float32)
        sigmoid_gate = jax.nn.sigmoid(gate)
        scaled = grad * sigmoid_gate
        start = pl.multiple_of(step * tile, tile)
        out_ref[:, pl.ds(start, tile)] = (
            scaled * up * (1.0 + gate * (1.0 - sigmoid_gate))
        ).astype(jnp.bfloat16)
        out_ref[:, pl.ds(pl.multiple_of(width + step * tile, tile), tile)] = (
            scaled * gate
        ).astype(jnp.bfloat16)

    @pl.when(step >= steps)
    def _():
        result = contract_cols(out_ref[...], matrix_ref[...])
        size = part_refs[0].shape[0]
        for i, part_ref in enumerate(part_refs):
            part_ref[...] = result[i * size : (i + 1) * size].astype(part_ref.dtype)


def gate_up_gradient(table, pieces, down, gate, up, matrix, parts):
    count, width = gate.shape
    tile = tile_of(width, 256)
    steps = width // tile
    out_width = matrix.shape[0]
    out_tile = tile_of(out_width, 512)
    first = lambda i: jnp.minimum(i, steps - 1)
    later = lambda i: jnp.maximum(i - steps, 0)
    part = pl.BlockSpec((count, tile), lambda i, table: (0, first(i)))
    grads, *products = row_call(
        lambda *refs: gate_grad_kernel(len(pieces), steps, *refs),
        "gate_up_grad",
        table,
        (steps + out_width // out_tile,),
        [piece.array for piece in pieces] + [down, gate, up, matrix],
        [piece.spec() for piece in pieces]
        + [
            pl.BlockSpec((tile, down.shape[1]), lambda i, table: (first(i), 0)),
            part,
            part,
            pl.BlockSpec((out_tile, 2 * width), lambda i, table: (later(i), 0)),
        ],
        [jax.ShapeDtypeStruct((count, 2 * width), jnp.bfloat16)]
        + [jax.ShapeDtypeStruct((count // parts, out_width), jnp.bfloat16)] * parts,
        [pl.BlockSpec((count, 2 * width), lambda i, table: (0, 0))]
        + [pl.BlockSpec((count // parts, out_tile), lambda i, table: (0, later(i)))] * parts,
    )
    return grads, products if parts > 1 else products[0]


def rows_kernel(count, weighed, *refs):
    out_ref = refs[2 * count + 1 + weighed]
    result = sum(contract_rows(refs[1 + i][...], refs[1 + count + i][...]) for i in range(count))
    out_ref[...] = result.astype(out_ref.dtype)
    if weighed:
        by_column = jnp.transpose(result * refs[2 * count + 1][...].astype(jnp.float32))
        refs[-1][...] = jnp.sum(by_column, axis=0, keepdims=True)


def weight_gradient(table, lefts, rights, weights=None):
    width, columns = lefts[0].array.shape[1], rights[0].columns
    tile = tile_of(width, 256)
    weighed = weights is not None
    block_spec = pl.BlockSpec((tile, columns), lambda i, table: (i, 0))
    result = row_call(
        lambda *refs: rows_kernel(len(lefts), weighed, *refs),
        "weight_grad",
        table,
        (width // tile,),
        [piece.array for piece in lefts + rights] + ([weights] if weighed else []),
        [piece.spec(tile) for piece in lefts]
        + [piece.spec() for piece in rights]
        + ([block_spec] if weighed else []),
        [jax.ShapeDtypeStruct((width, columns), jnp.bfloat16)]
        + ([jax.ShapeDtypeStruct((1, width), jnp.float32)] if weighed else []),
        [block_spec] + ([pl.BlockSpec((1, tile), lambda i, table: (0, i))] if weighed else []),
    )
    return result if weighed else result[0]


def split_groups(groups, half, side=0, sides=1):
    return [
        Piece(array, half, i, side=side, sides=sides)
        for array in groups
        for i in range(array.shape[0] // half)
    ]


def arrived_sum(split, low_refs, high_refs):
    low = sum(ref[...].astype(jnp.float32) for ref in low_refs)
    high = sum(ref[...].astype(jnp.float32) for ref in high_refs)
    return jnp.where(pl.program_id(0) < split, low, high)


def half_specs(tile, split, width):
    return (
        pl.BlockSpec((tile, width), lambda i: (jnp.minimum(i, split - 1), 0)),
        pl.BlockSpec((tile, width), lambda i: (jnp.maximum(i - split, 0), 0)),
    )


def put_half(split, low_ref, high_ref, value):
    @pl.when(pl.program_id(0) < split)
    def _():
        low_ref[...] = value

    @pl.when(pl.program_id(0) >= split)
    def _():
        high_ref[...] = value


def row_kernel_call(kernel, name, whole, lows, highs, gain, outs):
    rows, width = whole[0].shape
    tile = min(rows // 2, 128)
    split = rows // 2 // tile
    spec = pl.BlockSpec((tile, width), lambda i: (i, 0))
    low_spec, high_spec = half_specs(tile, split, width)
    row_spec = pl.BlockSpec((1, width), lambda i: (0, 0))
    shapes, specs = [], []
    for out in outs:
        if out == "halves":
            shapes += [jax.ShapeDtypeStruct((rows // 2, width), jnp.bfloat16)] * 2
            specs += [low_spec, high_spec]
        elif out == "row":
            shapes.append(jax.ShapeDtypeStruct((1, width), jnp.float32))
            specs.append(row_spec)
        else:
            shapes.append(jax.ShapeDtypeStruct((rows, width), out))
            specs.append(spec)
    return pl.pallas_call(
        lambda *refs: kernel(split, len(lows), *refs),
        grid=(2 * split,),
        in_specs=[spec] * len(whole)
        + [low_spec] * len(lows)
        + [high_spec] * len(highs)
        + [row_spec],
        out_specs=specs,
        out_shape=shapes,
        compiler_params=kernel_params(),
        cost_estimate=SMALL_COST,
        name=name,
    )(*whole, *lows, *highs, gain)


def add_norm_kernel(split, count, base_ref, own_ref, *refs):
    gain_ref, sum_ref, low_ref, high_ref = refs[2 * count :]
    values = base_ref[...].astype(jnp.float32) + own_ref[...].astype(jnp.float32)
    values = values + arrived_sum(split, refs[:count], refs[count : 2 * count])
    sum_ref[...] = values
    put_half(split, low_ref, high_ref, rms_gain(values, gain_ref[...]).astype(jnp.bfloat16))


def add_and_norm(base, own, lows, highs, gain):
    outs = (jnp.float32, "halves")
    return row_kernel_call(add_norm_kernel, "add_norm", [base, own], lows, highs, gain, outs)


def add_kernel(split, count, base_ref, own_ref, *refs):
    values = base_ref[...].astype(jnp.float32) + own_ref[...].astype(jnp.float32)
    values = values + arrived_sum(split, refs[:count], refs[count : 2 * count])
    refs[-1][...] = values.astype(jnp.bfloat16)


def norm_gradient_kernel(split, count, base_ref, value_ref, own_ref, *refs):
    gain_ref, outs = refs[2 * count], refs[2 * count + 1 :]
    grad = own_ref[...].astype(jnp.float32)
    grad = grad + arrived_sum(split, refs[:count], refs[count : 2 * count])
    values = value_ref[...].astype(jnp.float32)
    scale = lax.rsqrt(jnp.mean(values * values, axis=1, keepdims=True) + norm_eps)
    unit = values * scale
    inner = grad * gain_ref[...]
    result = base_ref[...].astype(jnp.float32) + scale * (
        inner - unit * jnp.mean(inner * unit, axis=1, keepdims=True)
    )
    if len(outs) == 1:
        outs[0][...] = result.astype(jnp.bfloat16)
        return
    low_ref, high_ref, whole_ref, gain_out = outs
    whole_ref[...] = result.astype(jnp.bfloat16)
    put_half(split, low_ref, high_ref, result.astype(jnp.bfloat16))

    @pl.when(pl.program_id(0) == 0)
    def _():
        gain_out[...] = jnp.zeros_like(gain_out)

    gain_out[...] += jnp.sum(grad * unit, axis=0, keepdims=True)


def norm_gradient(base, values, own, lows, highs, gain, outs):
    return row_kernel_call(
        norm_gradient_kernel, "norm_gradient", [base, values, own], lows, highs, gain, outs
    )


def project_kernel(count, *refs):
    rows = stacked(refs[1 : 1 + count])
    matrix_ref, gain_ref, cos_ref, sin_ref = refs[1 + count : 5 + count]
    query_ref, key_ref, value_ref, query_raw, key_raw = refs[-5:]
    width = HEAD_WIDTH
    mixed = product(rows, matrix_ref[...])
    cos, sin = cos_ref[...], sin_ref[...]
    for part in range(QUERY_PER_KEY + 1):
        values = mixed[:, part * width : (part + 1) * width]
        is_key = part == QUERY_PER_KEY
        gain = gain_ref[1:2, :] if is_key else gain_ref[0:1, :]
        scale = lax.rsqrt(jnp.mean(values * values, axis=1, keepdims=True) + norm_eps)
        scaled = values * scale * gain
        turned = scaled * cos + pltpu.roll(scaled, width // 2, 1) * sin
        if is_key:
            key_ref[...] = turned.astype(jnp.bfloat16)
            key_raw[...] = values
        else:
            query_ref[:, part * width : (part + 1) * width] = turned.astype(jnp.bfloat16)
            query_raw[:, part * width : (part + 1) * width] = values
    value_ref[...] = mixed[:, (QUERY_PER_KEY + 1) * width :].astype(jnp.bfloat16)


def project(blocks, matrix, gains, cos, sin, place, total_rows, before):
    count, depth = sum(block.shape[0] for block in blocks), matrix.shape[0]
    block = (QUERY_PER_KEY + 2) * HEAD_WIDTH
    heads = matrix.shape[1] // block
    wide = QUERY_PER_KEY * HEAD_WIDTH
    per_table = cos.shape[0] // count
    table_spec = pl.BlockSpec(
        (count, HEAD_WIDTH), lambda h, at: (lax.rem(at[0], per_table), 0)
    )
    widths = (wide, HEAD_WIDTH, HEAD_WIDTH, wide, HEAD_WIDTH)
    kinds = (jnp.bfloat16,) * 3 + (jnp.float32,) * 2
    kept = () if before is None else tuple(before)
    return pl.pallas_call(
        lambda *refs: project_kernel(len(blocks), *refs),
        grid_spec=pltpu.PrefetchScalarGridSpec(
            num_scalar_prefetch=1,
            grid=(heads,),
            in_specs=[
                pl.BlockSpec((rows.shape[0], depth), lambda h, at: (0, 0)) for rows in blocks
            ]
            + [
                pl.BlockSpec((depth, block), lambda h, at: (0, h)),
                pl.BlockSpec((2, HEAD_WIDTH), lambda h, at: (0, 0)),
                table_spec,
                table_spec,
            ]
            + [pl.BlockSpec(memory_space=pltpu.HBM)] * len(kept),
            out_specs=[pl.BlockSpec((count, w), lambda h, at: (at[0], h)) for w in widths],
        ),
        out_shape=[
            jax.ShapeDtypeStruct((total_rows, heads * w), kind) for w, kind in zip(widths, kinds)
        ],
        input_output_aliases={5 + len(blocks) + i: i for i in range(len(kept))},
        compiler_params=kernel_params(56),
        cost_estimate=SMALL_COST,
        name="project",
    )(place.reshape(1), *blocks, matrix, gains, cos, sin, *kept)


def causal(keys, queries):
    rows = lax.broadcasted_iota(jnp.int32, (keys, queries), 0)
    return rows <= lax.broadcasted_iota(jnp.int32, (keys, queries), 1)


def add_after(whole, part, low):
    if low == 0:
        return whole + part
    return jnp.concatenate([whole[:, :low], whole[:, low:] + part], axis=1)


def walk(visit, step, block, carry, pieces):
    carry = lax.fori_loop(
        0,
        step,
        lambda j, c: visit(pl.multiple_of(j * block, block), c, block, 0, False),
        carry,
    )
    start = pl.multiple_of(step * block, block)
    count = block // pieces
    for low in range(0, block, count):
        carry = visit(start + low, carry, count, low, True)
    return carry


def attend_kernel(scale, query_ref, key_ref, value_ref, out_ref, log_ref):
    block = query_ref.shape[0]
    width = key_ref.shape[1]
    group = query_ref.shape[1] // width
    step = pl.program_id(2)
    queries = [query_ref[:, g * width : (g + 1) * width] for g in range(group)]

    def visit(start, carry, count, low, masked):
        keys = key_ref[pl.ds(start, count), :]
        values = value_ref[pl.ds(start, count), :]
        new = []
        for g in range(group):
            total, acc = carry[g]
            weights = jnp.exp2(contract_cols(keys, queries[g][low:]) * (scale * log2_e))
            if masked:
                weights = jnp.where(causal(count, block - low), weights, 0.0)
            total = add_after(total, jnp.sum(weights, axis=0, keepdims=True), low)
            acc = add_after(acc, contract_rows(values, weights.astype(jnp.bfloat16)), low)
            new.append((total, acc))
        return tuple(new)

    carry = tuple(
        (jnp.zeros((1, block), jnp.float32), jnp.zeros((width, block), jnp.float32))
        for _ in range(group)
    )
    carry = walk(visit, step, block, carry, 1)
    for g in range(group):
        total, acc = carry[g]
        out_ref[:, g * width : (g + 1) * width] = jnp.transpose(acc / total).astype(jnp.bfloat16)
        log_ref[0, 0, g : g + 1, :] = jnp.log2(total)


def attention_forward(query, key, value, block):
    rows = query.shape[0]
    heads = key.shape[1] // HEAD_WIDTH
    steps = SEQUENCE_TOKENS // block
    wide = QUERY_PER_KEY * HEAD_WIDTH
    sequences = rows // SEQUENCE_TOKENS
    query_spec = pl.BlockSpec((block, wide), lambda h, s, i: (s * steps + i, h))
    key_spec = pl.BlockSpec((SEQUENCE_TOKENS, HEAD_WIDTH), lambda h, s, i: (s, h))
    return pl.pallas_call(
        lambda *refs: attend_kernel(HEAD_WIDTH ** (-0.5), *refs),
        grid=(heads, sequences, steps),
        in_specs=[query_spec, key_spec, key_spec],
        out_specs=[
            query_spec,
            pl.BlockSpec(
                (1, 1, QUERY_PER_KEY, block), lambda h, s, i: (h, s * steps + i, 0, 0)
            ),
        ],
        out_shape=[
            jax.ShapeDtypeStruct(query.shape, jnp.bfloat16),
            jax.ShapeDtypeStruct((heads, rows // block, QUERY_PER_KEY, block), jnp.float32),
        ],
        compiler_params=kernel_params(56),
        cost_estimate=SMALL_COST,
        name="attend",
    )(query, key, value)


def norm_back(values, grad, gain, cos, sin):
    width = values.shape[1]
    turned = grad * cos + pltpu.roll(grad * sin, width // 2, 1)
    scale = lax.rsqrt(jnp.mean(values * values, axis=1, keepdims=True) + norm_eps)
    unit = values * scale
    inner = turned * gain
    back = scale * (inner - unit * jnp.mean(inner * unit, axis=1, keepdims=True))
    return back.astype(jnp.bfloat16), jnp.sum(turned * unit, axis=0, keepdims=True)


def attend_back_kernel(
    scale,
    table_ref,
    query_ref,
    key_ref,
    value_ref,
    grad_ref,
    context_ref,
    log_ref,
    query_raw,
    key_raw,
    gain_ref,
    cos_ref,
    sin_ref,
    *refs,
):
    mixed_out, gain_out, key_sum, value_sum = refs[-4:]
    block = query_ref.shape[0]
    width = key_ref.shape[1]
    group = query_ref.shape[1] // width
    sequence, step = pl.program_id(0), pl.program_id(1)
    @pl.when(step == 0)
    def _():
        key_sum[...] = jnp.zeros_like(key_sum)
        value_sum[...] = jnp.zeros_like(value_sum)

    @pl.when((step == 0) & (sequence == 0))
    def _():
        gain_out[...] = jnp.zeros_like(gain_out)

    queries, grads, logs, dots = [], [], [], []
    for g in range(group):
        cols = slice(g * width, (g + 1) * width)
        queries.append(query_ref[:, cols])
        grads.append(grad_ref[:, cols])
        logs.append(log_ref[0, 0, g : g + 1, :])
        both = grads[g].astype(jnp.float32) * context_ref[:, cols].astype(jnp.float32)
        dots.append(jnp.sum(jnp.transpose(both), axis=0, keepdims=True))

    def visit(start, carry, count, low, masked):
        rows = pl.ds(start, count)
        keys = key_ref[rows, :]
        values = value_ref[rows, :]
        new = []
        key_part = value_part = None
        for g in range(group):
            seen, sought = queries[g][low:], grads[g][low:]
            weights = jnp.exp2(contract_cols(keys, seen) * (scale * log2_e) - logs[g][:, low:])
            if masked:
                weights = jnp.where(causal(count, block - low), weights, 0.0)
            slope = contract_cols(values, sought)
            score = (weights * (slope - dots[g][:, low:])).astype(jnp.bfloat16)
            value_g = product(weights.astype(jnp.bfloat16), sought)
            key_g = product(score, seen)
            key_part = key_g if key_part is None else key_part + key_g
            value_part = value_g if value_part is None else value_part + value_g
            new.append(add_after(carry[g], contract_rows(keys, score), low))
        key_sum[rows, :] += key_part
        value_sum[rows, :] += value_part
        return tuple(new)

    carry = tuple(jnp.zeros((width, block), jnp.float32) for _ in range(group))
    carry = walk(visit, step, block, carry, 2)
    rows = pl.ds(pl.multiple_of(step * block, block), block)
    cos, sin = cos_ref[rows, :], sin_ref[rows, :]
    for g in range(group):
        cols = slice(g * width, (g + 1) * width)
        back, gain = norm_back(
            query_raw[:, cols], jnp.transpose(carry[g]) * scale, gain_ref[0:1, :], cos, sin
        )
        mixed_out[rows, cols] = back
        gain_out[0:1, :] += gain

    @pl.when(step == pl.num_programs(1) - 1)
    def _():
        def finish(j, _):
            rows = pl.ds(pl.multiple_of(j * block, block), block)
            back, gain = norm_back(
                key_raw[rows, :],
                key_sum[rows, :] * scale,
                gain_ref[1:2, :],
                cos_ref[rows, :],
                sin_ref[rows, :],
            )
            mixed_out[rows, group * width : (group + 1) * width] = back
            mixed_out[rows, (group + 1) * width :] = value_sum[rows, :].astype(jnp.bfloat16)
            gain_out[1:2, :] += gain
            return 0

        lax.fori_loop(0, pl.num_programs(1), finish, 0)


def attention_backward(
    slots, query, key, value, grad, context, logs, query_raw, key_raw, gains, cos, sin, head, before
):
    rows = query.shape[0]
    block = logs.shape[-1]
    steps = SEQUENCE_TOKENS // block
    wide = QUERY_PER_KEY * HEAD_WIDTH
    heads = key.shape[1] // HEAD_WIDTH
    sequences = rows // SEQUENCE_TOKENS
    mixed = (QUERY_PER_KEY + 2) * HEAD_WIDTH
    query_spec = pl.BlockSpec((block, wide), lambda s, i, slots: (s * steps + i, head))
    key_spec = pl.BlockSpec((SEQUENCE_TOKENS, HEAD_WIDTH), lambda s, i, slots: (s, head))
    table_spec = pl.BlockSpec((SEQUENCE_TOKENS, HEAD_WIDTH), lambda s, i, slots: (0, 0))
    gain_spec = pl.BlockSpec((2, HEAD_WIDTH), lambda s, i, slots: (0, 0))
    kept = () if before is None else (before,)
    return pl.pallas_call(
        lambda *refs: attend_back_kernel(HEAD_WIDTH ** (-0.5), *refs),
        grid_spec=pltpu.PrefetchScalarGridSpec(
            num_scalar_prefetch=1,
            grid=(sequences, steps),
            in_specs=[
            query_spec,
            key_spec,
            key_spec,
            pl.BlockSpec((block, wide), lambda s, i, slots: (slots[s * steps + i], head)),
            query_spec,
            pl.BlockSpec(
                (1, 1, QUERY_PER_KEY, block), lambda s, i, slots: (head, s * steps + i, 0, 0)
            ),
            query_spec,
            key_spec,
            gain_spec,
            table_spec,
            table_spec,
        ]
        + [pl.BlockSpec(memory_space=pltpu.HBM)] * len(kept),
        out_specs=[
            pl.BlockSpec((SEQUENCE_TOKENS, mixed), lambda s, i, slots: (s, head)),
            gain_spec,
        ],
        scratch_shapes=[pltpu.VMEM((SEQUENCE_TOKENS, HEAD_WIDTH), jnp.float32)] * 2,
        ),
        out_shape=[
            jax.ShapeDtypeStruct((rows, heads * mixed), jnp.bfloat16),
            jax.ShapeDtypeStruct((2, HEAD_WIDTH), jnp.float32),
        ],
        input_output_aliases={12: 0} if kept else {},
        compiler_params=kernel_params(56),
        cost_estimate=SMALL_COST,
        name="attend_back",
    )(slots, query, key, value, grad, context, logs, query_raw, key_raw, gains, cos, sin, *kept)


def local(
    inputs,
    input_projection_weight,
    input_first_moment,
    input_second_moment,
    out_weight,
    out_mean,
    out_square,
    swiglu_weight,
    swiglu_mean,
    swiglu_square,
    down_weight,
    down_mean,
    down_square,
    norm_gains,
    norm_mean,
    norm_square,
    qknorm_gains,
    qknorm_mean,
    qknorm_square,
    cotangent,
):
    size = lax.axis_size("tensor")
    rows = inputs.shape[0]
    half = rows // 2
    group_rows = rows * size
    last = size // 2
    dp_rows = input_projection_weight.shape[0]
    local_kv = input_projection_weight.shape[1]
    local_ff = swiglu_weight.shape[2]
    me = ring_place(lax.axis_index("tensor"), size)
    places = [ring_place((me + d + size) % size, size) for d in ring_offsets(size)]
    group_places = [places[:1]]
    for step in range(1, last):
        group_places.append(places[2 * step - 1 : 2 * step + 1])
    group_places.append(places[-1:])
    halves = [2 * place + i for place in places for i in range(2)]
    table = jnp.stack(places + halves).astype(jnp.int32)
    away = (ring_place(jnp.arange(size, dtype=jnp.int32), size) - me + size) % size
    slots = jnp.where(
        away == 0,
        size - 2,
        jnp.where(
            away == last,
            size - 1,
            jnp.where(away < last, 2 * away - 2, 2 * (size - away) - 1),
        ),
    ).astype(jnp.int32)
    order = Order()
    turn, mark = order.turn, order.mark
    tie = lax.optimization_barrier

    def ordered(array, group):
        entries = [0] if group == 0 else [2 * group - 1, 2 * group]
        if group == last:
            entries = [size - 1]
        return [Piece(array, rows, entry=entry) for entry in entries]

    def ordered_finely(array):
        return [Piece(array, half, entry=size + i) for i in range(2 * size)]

    def flat(groups):
        return pieces_of([block for group in groups for block in group])

    def parts_of(group):
        return 1 if group == 0 else 2 if group == last else 4

    def marked(part):
        return mark(*part) if isinstance(part, (list, tuple)) else mark(part)

    in_low = input_projection_weight.astype(jnp.bfloat16).reshape(dp_rows, -1)
    out_low = out_weight.astype(jnp.bfloat16)
    swiglu_low = swiglu_weight.astype(jnp.bfloat16).reshape(dp_rows, 2 * local_ff)
    down_low = down_weight.astype(jnp.bfloat16)
    in_matrix = lax.all_gather(in_low, "dp", axis=0, tiled=True)
    out_full = lax.all_gather(out_low, "dp", axis=1, tiled=True)
    swiglu_matrix = lax.all_gather(swiglu_low, "dp", axis=0, tiled=True)
    down_full = lax.all_gather(down_low, "dp", axis=1, tiled=True)

    normed_f = rms_gain(inputs.astype(jnp.float32), norm_gains[0])
    cos, sin = rotary_tables(SEQUENCE_TOKENS, HEAD_WIDTH)
    projected = []

    def project_group(group, blocks):
        calls = [blocks] if group in (0, last) else [blocks[:2], blocks[2:]]
        for place, call in zip(group_places[group], calls):
            call[0] = turn(call[0])
            projected[:] = mark(
                *project(
                    call, in_matrix, qknorm_gains, cos, sin, place, group_rows, projected or None
                )
            )

    normed = normed_f.astype(jnp.bfloat16)
    normed_groups = ring_gather(
        (normed[:half], normed[half:]), size, project_group, order, hold=(in_matrix,)
    )
    query, key, value, query_raw, key_raw = projected
    cotangent_sent = tie((cotangent, *normed_groups[-1]))[0]

    context, logs = mark(*attention_forward(query, key, value, rows))
    cot_groups, cot_carried = ring_near(
        (cotangent_sent[:half], cotangent_sent[half:]), size, lambda group, blocks: None, Order()
    )

    def out_group(group):
        return marked(
            block_product(
                table, ordered(turn(context), group), out_full, False, parts_of(group)
            )
        )

    own, lows, highs = ring_scatter(
        size, out_group, order, first=[half for group in cot_groups[1:] for half in group]
    )
    lows, highs = tie((lows, highs, swiglu_matrix))[:2]
    hidden, *two_halves = mark(*add_and_norm(inputs, own, lows, highs, norm_gains[1:2]))

    gate_groups = []
    grads = [None] * (last + 1)

    def gate_group(group, blocks):
        blocks[0] = turn(blocks[0])
        gate_groups.append(mark(*gate_up_product(table, pieces_of(blocks), swiglu_matrix)))

    two_groups, two_carried = ring_near(two_halves, size, gate_group, order)
    two_groups = ring_far(two_groups, two_carried, size, gate_group, order)
    cot_carried = tie((*cot_carried, *gate_groups[last - 1]))[:2]
    cot_groups = ring_far(cot_groups, cot_carried, size, lambda group, blocks: None, order)
    activated = [parts[0] for parts in gate_groups]
    two_parts = [None] * (last + 1)

    def two_part(group):
        cots = [turn(cot_groups[group][0])] + cot_groups[group][1:]
        grads[group], part = gate_up_gradient(
            table,
            pieces_of(cots),
            down_full,
            *gate_groups[group][1:],
            swiglu_matrix,
            parts_of(group),
        )
        two_parts[group] = marked(part)

    for group in range(1, last):
        two_part(group)
    lefts = split_groups([turn(activated[0])] + activated[1:], half)
    down_part = mark(weight_gradient(table, lefts, flat(cot_groups)))
    down_grad = lax.psum_scatter(down_part, "dp", scatter_dimension=1, tiled=True)
    two_part(last)
    more = []

    def own_part():
        two_part(0)

    def swiglu_gradient():
        twos = flat(two_groups)
        twos[0].array = turn(twos[0].array)
        side = len(more)
        more.append(mark(weight_gradient(table, twos, split_groups(grads, half, side, 2))))

    if last == 1:
        own_part()
    own, lows, highs = ring_scatter(
        size, lambda group: two_parts[group], order, between=own_part, after=swiglu_gradient
    )
    swiglu_part, lows, highs = tie((more[0], lows, highs))
    gate_weight_grad = lax.psum_scatter(swiglu_part, "dp", scatter_dimension=0, tiled=True)
    *attended_halves, hidden_grad, mlp_gain_grad = mark(
        *norm_gradient(
            cotangent, hidden, own, lows, highs, norm_gains[1:2], ("halves", jnp.bfloat16, "row")
        )
    )

    context_grad, down_parts, new_down, head_grads = [None], [None] * (last + 1), [], []

    def context_group(group, blocks):
        blocks[0] = turn(blocks[0])
        index = size - 2 if group == 0 else size - 1 if group == last else group - 1
        context_grad[0] = mark(
            block_product(
                table, pieces_of(blocks), out_full, True, into=(group_rows, index, context_grad[0])
            )
        )
        if group == 0:
            for other in range(last, -1, -1):
                down_parts[other] = marked(
                    block_product(
                        table, [Piece(turn(activated[other]))], down_full, False, parts_of(other)
                    )
                )
            new_down[:] = mark(
                turn(down_grad).astype(jnp.float32),
                *adamw(
                    down_weight,
                    turn(down_grad).astype(jnp.float32),
                    down_mean,
                    down_square,
                    FF ** (-0.5),
                ),
            )
        if group == last - 1:
            swiglu_gradient()

    attended_groups = ring_gather(attended_halves, size, context_group, order)
    swiglu_part = tie((more[1], *attended_groups[last]))[0]
    up_weight_grad = lax.psum_scatter(swiglu_part, "dp", scatter_dimension=0, tiled=True)

    def head_backward(head):
        head_grads.append(
            mark(
                *attention_backward(
                    slots, turn(query), key, value, context_grad[0], context, logs, query_raw,
                    key_raw, qknorm_gains, cos, sin, head,
                    head_grads[-1][0] if head_grads else None,
                )
            )
        )

    out_part = mark(
        weight_gradient(table, ordered_finely(turn(context)), flat(attended_groups))
    )
    if last == 1:
        head_backward(0)

    def other_heads():
        for head in range(1, local_kv):
            head_backward(head)

    own, lows, highs = ring_scatter(
        size,
        lambda group: down_parts[group],
        order,
        hold=attended_groups[-1],
        between=lambda: head_backward(0),
        after=other_heads,
    )
    sent, outputs = (own, lows, highs), []
    mixed_grad = head_grads[-1][0]
    qknorm_part = sum(pair[1] for pair in head_grads)
    in_parts = []

    def normed_group(group):
        return marked(
            block_product(
                table, ordered(turn(mixed_grad), group), in_matrix, True, parts_of(group)
            )
        )

    def in_gradient():
        normeds = flat(normed_groups)
        normeds[0].array = turn(normeds[0].array)
        in_parts[:] = mark(
            *weight_gradient(table, normeds, ordered_finely(mixed_grad), in_matrix)
        )

    def add_outputs():
        own, lows, highs = sent
        whole = [hidden, turn(own)]
        (result,) = row_kernel_call(
            add_kernel, "add", whole, lows, highs, norm_gains[0:1], (jnp.bfloat16,)
        )
        outputs.append(mark(result))

    got = []
    came = []
    own, lows, highs = ring_scatter(
        size,
        normed_group,
        order,
        between=in_gradient,
        after=add_outputs,
        got=got,
        came=came,
        eager=False,
    )
    if not in_parts:
        in_gradient()
    rows_of_gains = jnp.concatenate([in_parts[1] / norm_gains[0:1], mlp_gain_grad], axis=0)
    gain_sums = jnp.concatenate([rows_of_gains, qknorm_part], axis=1)
    (outputs,) = outputs
    out_part, gate_weight_grad = tie((out_part, gate_weight_grad, sent, mixed_grad))[:2]
    out_grad = lax.psum_scatter(out_part, "dp", scatter_dimension=1, tiled=True)
    in_part, up_weight_grad = tie((in_parts[0], up_weight_grad, *came))[:2]
    in_grad = lax.psum_scatter(in_part, "dp", scatter_dimension=0, tiled=True)
    out_grad, gate_weight_grad = tie((out_grad, gate_weight_grad, *got))[:2]
    out_grad = out_grad.astype(jnp.float32)
    out_new, out_second = adamw(
        out_weight, out_grad, out_mean, out_square, (HQ * HEAD_WIDTH / 8.0) ** (-0.5)
    )
    swiglu_grad, swiglu_new, swiglu_second = adamw_parts(
        swiglu_weight,
        (gate_weight_grad, up_weight_grad),
        swiglu_mean,
        swiglu_square,
        MODEL_WIDTH ** (-0.5),
    )
    down_grad, down_new, down_second = new_down
    (
        lows,
        highs,
        own,
        outputs,
        out_grad,
        out_new,
        out_second,
        swiglu_grad,
        swiglu_new,
        swiglu_second,
    ) = tie(
        (
            lows,
            highs,
            own,
            outputs,
            out_grad,
            out_new,
            out_second,
            swiglu_grad,
            swiglu_new,
            swiglu_second,
        )
    )
    (input_grad,) = norm_gradient(
        hidden_grad, inputs, own, lows, highs, norm_gains[0:1], (jnp.bfloat16,)
    )
    in_grad, in_new, in_second = adamw_parts(
        input_projection_weight,
        (in_grad,),
        input_first_moment,
        input_second_moment,
        MODEL_WIDTH ** (-0.5),
    )
    gain_sums = sum_over(tie((gain_sums, *lows, *highs))[0], "tensor", (input_grad,))
    gain_sums = sum_over(gain_sums, "dp", (in_new,))
    norm_grad, qknorm_grad = gain_sums[:, :MODEL_WIDTH], gain_sums[:, MODEL_WIDTH:]
    norm_new, norm_second = adamw(norm_gains, norm_grad, norm_mean, norm_square, gain_rate)
    qknorm_new, qknorm_second = adamw(
        qknorm_gains, qknorm_grad, qknorm_mean, qknorm_square, gain_rate
    )
    return (
        outputs,
        input_grad,
        in_grad,
        in_new,
        in_second,
        out_grad,
        out_new,
        out_second,
        swiglu_grad,
        swiglu_new,
        swiglu_second,
        down_grad,
        down_new,
        down_second,
        norm_grad,
        norm_new,
        norm_second,
        qknorm_grad,
        qknorm_new,
        qknorm_second,
    )


def solution(mesh):
    return jax.shard_map(
        local,
        mesh=mesh,
        in_specs=(
            P(("dp", "tensor"), None),
            P("dp", "tensor", None),
            P("dp", "tensor", None),
            P("dp", "tensor", None),
            P("tensor", "dp"),
            P("tensor", "dp"),
            P("tensor", "dp"),
            P("dp", None, "tensor"),
            P("dp", None, "tensor"),
            P("dp", None, "tensor"),
            P("tensor", "dp"),
            P("tensor", "dp"),
            P("tensor", "dp"),
            P(),
            P(),
            P(),
            P(),
            P(),
            P(),
            P(("dp", "tensor"), None),
        ),
        out_specs=(
            P(("dp", "tensor"), None),
            P(("dp", "tensor"), None),
            P("dp", "tensor", None),
            P("dp", "tensor", None),
            P("dp", "tensor", None),
            P("tensor", "dp"),
            P("tensor", "dp"),
            P("tensor", "dp"),
            P("dp", None, "tensor"),
            P("dp", None, "tensor"),
            P("dp", None, "tensor"),
            P("tensor", "dp"),
            P("tensor", "dp"),
            P("tensor", "dp"),
            P(),
            P(),
            P(),
            P(),
            P(),
            P(),
        ),
        check_vma=False,
    )
```

```python
import jax
import jax.numpy as jnp
from jax import lax
from jax.experimental import pallas as pl
from jax.experimental.pallas import tpu as pltpu
from jax.sharding import PartitionSpec as P

MODEL_WIDTH = 2048
HQ = 16
HEAD_WIDTH = 128
FF = 6144
QUERY_PER_KEY = 2
SEQUENCE_TOKENS = 2048


norm_eps = 1e-06
rope_base = 1000000.0
beta_one = 0.5
beta_two = 0.55
step_count = 5.0
adam_eps = 1e-08
decay_rate = 0.1
gain_rate = 0.3
masked_score = -1e30
log2_e = 1.4426950408889634


def rms_gain(values, gain_row):
    return (
        values * lax.rsqrt(jnp.mean(values * values, axis=-1, keepdims=True) + norm_eps) * gain_row
    )


def rotary_tables(length, width):
    frequency = rope_base ** (
        -2.0 * jnp.arange(width // 2, dtype=jnp.int32).astype(jnp.float32) / width
    )
    angles = jnp.arange(length, dtype=jnp.int32).astype(jnp.float32)[:, None] * frequency[None, :]
    cos, sin = jnp.cos(angles), jnp.sin(angles)
    return jnp.concatenate([cos, cos], axis=1), jnp.concatenate([-sin, sin], axis=1)


def contract_rows(left, right):
    return lax.dot_general(
        left, right, (((0,), (0,)), ((), ())), preferred_element_type=jnp.float32
    )


def contract_cols(left, right):
    return lax.dot_general(
        left, right, (((1,), (1,)), ((), ())), preferred_element_type=jnp.float32
    )


def product(left, right):
    return jnp.dot(left, right, preferred_element_type=jnp.float32)


def adamw(weight, gradient, mean_old, square_old, rate):
    mean_new = beta_one * mean_old + (1.0 - beta_one) * gradient
    square_new = beta_two * square_old + (1.0 - beta_two) * gradient * gradient
    mean_hat = mean_new / (1.0 - beta_one**step_count)
    square_hat = square_new / (1.0 - beta_two**step_count)
    weight_new = weight - rate * (
        mean_hat / (jnp.sqrt(square_hat) + adam_eps) + decay_rate * weight
    )
    return (weight_new, square_new)


def adam_kernel(rate, weight_ref, mean_ref, square_ref, *refs):
    *grad_refs, grad_out, new_out, second_out = refs
    width = weight_ref.shape[2]
    for part in range(weight_ref.shape[1]):
        start = part * width
        for grad_ref in grad_refs:
            if start < grad_ref.shape[1]:
                break
            start -= grad_ref.shape[1]
        grad = grad_ref[:, start : start + width].astype(jnp.float32)
        new, second = adamw(
            weight_ref[:, part, :], grad, mean_ref[:, part, :], square_ref[:, part, :], rate
        )
        grad_out[:, part, :] = grad
        new_out[:, part, :] = new
        second_out[:, part, :] = second


def adamw_parts(weight, grads, mean_old, square_old, rate):
    rows, parts, width = weight.shape
    tile = min(rows, 64)
    spec = pl.BlockSpec((tile, parts, width), lambda i: (i, 0, 0))
    return pl.pallas_call(
        lambda *refs: adam_kernel(rate, *refs),
        grid=(rows // tile,),
        in_specs=[spec] * 3
        + [pl.BlockSpec((tile, grad.shape[1]), lambda i: (i, 0)) for grad in grads],
        out_specs=[spec] * 3,
        out_shape=[jax.ShapeDtypeStruct(weight.shape, jnp.float32)] * 3,
        compiler_params=kernel_params(),
        cost_estimate=SMALL_COST,
        name="adamw",
    )(weight, mean_old, square_old, *grads)


def ring_place(index, size):
    return jnp.where(index < size // 2, index, size // 2 + size - 1 - index)


def ring_pairs(size):
    half = size // 2
    order = list(range(half)) + list(range(size - 1, half - 1, -1))
    ahead = [(order[r], order[(r + 1) % size]) for r in range(size)]
    return ahead, [(b, a) for a, b in ahead]


def ring_offsets(size):
    offsets = [0]
    for step in range(1, size // 2):
        offsets += [step, -step]
    return offsets + [size // 2]


class Order:
    def __init__(self):
        self.last = ()

    def turn(self, *values):
        tied = lax.optimization_barrier(values + self.last)[: len(values)]
        return tied[0] if len(values) == 1 else tied

    def mark(self, *values):
        self.last = values
        return values[0] if len(values) == 1 else values


def ring_near(blocks, size, work, order, hold=()):
    ahead, back = ring_pairs(size)
    tie = lax.optimization_barrier
    groups = [list(blocks)]
    left, right = list(blocks), list(blocks)
    work(0, list(blocks))
    for step in range(1, size // 2):
        left_low = lax.ppermute(left[0], "tensor", ahead)
        right_high = lax.ppermute(right[1], "tensor", back)
        left_high = lax.ppermute(left[1], "tensor", ahead)
        right_low = lax.ppermute(right[0], "tensor", back)
        held = tuple(hold) if step == size // 2 - 1 else ()
        left_low, right_high = tie((left_low, right_high) + held + order.last)[:2]
        left, right = [left_low, left_high], [right_low, right_high]
        pair = tie((*right, *left) + order.last)[:4]
        groups.append(list(pair))
        work(step, list(pair))
    return groups, (left[0], right[1])


def ring_far(groups, carried, size, work, order):
    ahead, back = ring_pairs(size)
    low = lax.ppermute(carried[0], "tensor", ahead)
    high = lax.ppermute(carried[1], "tensor", back)
    groups.append(list(lax.optimization_barrier((low, high) + order.last)[:2]))
    work(size // 2, list(groups[-1]))
    return groups


def ring_gather(blocks, size, work, order, hold=()):
    groups, carried = ring_near(blocks, size, work, order, hold)
    return ring_far(groups, carried, size, work, order)


def relay_kernel(count, *refs):
    for i in range(count):
        refs[2 * count + i][...] = (
            refs[i][...].astype(jnp.float32) + refs[count + i][...].astype(jnp.float32)
        ).astype(jnp.bfloat16)


def relay(terms, got):
    rows, width = terms[0].shape
    tile = min(rows, 128)
    spec = pl.BlockSpec((tile, width), lambda i: (i, 0))
    count = len(terms)
    return pl.pallas_call(
        lambda *refs: relay_kernel(count, *refs),
        grid=(rows // tile,),
        in_specs=[spec] * (2 * count),
        out_specs=[spec] * count,
        out_shape=[jax.ShapeDtypeStruct((rows, width), jnp.bfloat16)] * count,
        compiler_params=kernel_params(),
        cost_estimate=SMALL_COST,
        name="relay",
    )(*terms, *got)


def ring_scatter(
    size, part, order, hold=(), first=(), between=None, after=None, got=None, came=None,
    eager=True,
):
    ahead, back = ring_pairs(size)
    send = lambda value, pairs: lax.ppermute(value, "tensor", pairs)
    low, high = part(size // 2)
    if hold:
        low, high = lax.optimization_barrier((low, high) + tuple(hold))[:2]
    from_left, from_right = [send(low, ahead), None], [None, send(high, back)]
    for step in range(size // 2 - 1, 0, -1):
        right_low, right_high, left_low, left_high = part(step)
        full = from_left[1] is not None
        if not full:
            if eager:
                early = send(right_high, ahead), send(left_low, back)
            if between is not None:
                between()
        arrived = [from_left[0], from_right[1]] + ([from_left[1], from_right[0]] if full else [])
        waited = (*first, *early) if eager and not full else tuple(first)
        if came is not None and not full:
            came[:] = arrived
        tied = order.turn(*arrived, *waited)
        arrived = tied[: len(arrived)]
        if eager and not full:
            early = tied[len(tied) - 2 :]
        terms = [right_low, left_high] + ([right_high, left_low] if full else [])
        passed = order.mark(*relay(terms, arrived))
        if got is not None:
            got[:] = passed
        if full:
            early = send(passed[2], ahead), send(passed[3], back)
        elif not eager:
            right_high, left_low = order.turn(right_high, left_low)
            early = send(right_high, ahead), send(left_low, back)
        from_left = [send(passed[0], ahead), early[0]]
        from_right = [early[1], send(passed[1], back)]
    if after is not None:
        after()
    own = part(0)
    if size == 2:
        return own, [from_left[0]], [from_right[1]]
    return own, [from_left[0], from_right[0]], [from_left[1], from_right[1]]


def sum_over(values, axis, beside=()):
    size = lax.axis_size(axis)
    if size & (size - 1):
        return lax.psum(values, axis)
    reach, beside = 1, list(beside)
    while reach < size:
        ways = 4 if size >= 4 * reach else 2
        values = values + sum(
            lax.ppermute(values, axis, [(i, i ^ (way * reach)) for i in range(size)])
            for way in range(1, ways)
        )
        if beside:
            values = lax.optimization_barrier((values, beside.pop(0)))[0]
        reach *= ways
    return values


def tile_of(width, most):
    return next(t for t in (most, 512, 256, 128) if t <= most and width % t == 0)


def kernel_params(mebibytes=56):
    return pltpu.CompilerParams(vmem_limit_bytes=mebibytes * 1024 * 1024)


SMALL_COST = pl.CostEstimate(flops=1_000_000, bytes_accessed=1_000_000, transcendentals=0)


class Piece:
    def __init__(self, array, count=None, index=0, entry=None, side=0, sides=1):
        self.array, self.count = array, count or array.shape[0]
        self.index, self.entry = index, entry
        self.side, self.columns = side, array.shape[1] // sides

    def row(self, table):
        return self.index if self.entry is None else table[self.entry]

    def spec(self, width=None):
        if width is None:
            return pl.BlockSpec(
                (self.count, self.columns),
                lambda i, table: (self.row(table), self.side),
                pipeline_mode=pl.Buffered(1),
            )
        return pl.BlockSpec((self.count, width), lambda i, table: (self.row(table), i))


def pieces_of(blocks):
    return [Piece(block) for block in blocks]


def stacked(refs):
    values = [ref[...] for ref in refs]
    return values[0] if len(values) == 1 else jnp.concatenate(values, axis=0)


def row_call(
    kernel, name, table, grid, operands, specs, outs, out_specs, aliases=None, mebibytes=56
):
    return pl.pallas_call(
        kernel,
        grid_spec=pltpu.PrefetchScalarGridSpec(
            num_scalar_prefetch=1, grid=grid, in_specs=specs, out_specs=out_specs
        ),
        out_shape=outs,
        input_output_aliases=aliases or {},
        compiler_params=kernel_params(mebibytes),
        cost_estimate=SMALL_COST,
        name=name,
    )(table, *operands)


def product_kernel(count, crossed, *refs):
    rows = stacked(refs[1 : 1 + count])
    matrix = refs[1 + count][...]
    result = contract_cols(rows, matrix) if crossed else product(rows, matrix)
    size = refs[-1].shape[0]
    outs = refs[-(rows.shape[0] // size) :]
    for i, out_ref in enumerate(outs):
        out_ref[...] = result[i * size : (i + 1) * size].astype(out_ref.dtype)


def block_product(table, pieces, matrix, crossed, parts=1, into=None):
    width = matrix.shape[0] if crossed else matrix.shape[1]
    tile = tile_of(width, 512)
    count = sum(piece.count for piece in pieces)
    if crossed:
        matrix_spec = pl.BlockSpec((tile, matrix.shape[1]), lambda i, table: (i, 0))
    else:
        matrix_spec = pl.BlockSpec((matrix.shape[0], tile), lambda i, table: (0, i))
    operands = [piece.array for piece in pieces] + [matrix]
    specs = [piece.spec() for piece in pieces] + [matrix_spec]
    aliases = {}
    index, all_rows = 0, count
    if into is not None:
        all_rows, index, so_far = into
        if so_far is not None:
            operands.append(so_far)
            specs.append(pl.BlockSpec(memory_space=pltpu.HBM))
            aliases = {len(operands): 0}
    if parts > 1:
        count = all_rows = count // parts
    out_spec = pl.BlockSpec((count, tile), lambda i, table: (index, i))
    out = jax.ShapeDtypeStruct((all_rows, width), jnp.bfloat16)
    result = row_call(
        lambda *refs: product_kernel(len(pieces), crossed, *refs),
        "block_product",
        table,
        (width // tile,),
        operands,
        specs,
        [out] * parts,
        [out_spec] * parts,
        aliases,
        56 if matrix.size > 4 * 1024 * 1024 else 32,
    )
    return result if parts > 1 else result[0]


def gate_kernel(count, *refs):
    rows = stacked(refs[1 : 1 + count])
    gate_ref, up_ref, activated_ref, gate_out, up_out = refs[1 + count :]
    gate = product(rows, gate_ref[...])
    up = product(rows, up_ref[...])
    activated_ref[...] = (gate * jax.nn.sigmoid(gate) * up).astype(jnp.bfloat16)
    gate_out[...] = gate.astype(gate_out.dtype)
    up_out[...] = up.astype(up_out.dtype)


def gate_up_product(table, pieces, matrix):
    depth, width = matrix.shape[0], matrix.shape[1] // 2
    count = sum(piece.count for piece in pieces)
    tile = tile_of(width, 256)
    steps = width // tile
    return row_call(
        lambda *refs: gate_kernel(len(pieces), *refs),
        "gate_up",
        table,
        (steps,),
        [piece.array for piece in pieces] + [matrix, matrix],
        [piece.spec() for piece in pieces]
        + [
            pl.BlockSpec((depth, tile), lambda i, table: (0, i)),
            pl.BlockSpec((depth, tile), lambda i, table: (0, steps + i)),
        ],
        [jax.ShapeDtypeStruct((count, width), jnp.bfloat16)] * 3,
        [pl.BlockSpec((count, tile), lambda i, table: (0, i))] * 3,
    )


def gate_grad_kernel(count, steps, *refs):
    down_ref, gate_ref, up_ref, matrix_ref, out_ref = refs[1 + count : 6 + count]
    part_refs = refs[6 + count :]
    step = pl.program_id(0)
    tile = gate_ref.shape[1]
    width = out_ref.shape[1] // 2

    @pl.when(step < steps)
    def _():
        grad = contract_cols(stacked(refs[1 : 1 + count]), down_ref[...])
        gate = gate_ref[...].astype(jnp.float32)
        up = up_ref[...].astype(jnp.float32)
        sigmoid_gate = jax.nn.sigmoid(gate)
        scaled = grad * sigmoid_gate
        start = pl.multiple_of(step * tile, tile)
        out_ref[:, pl.ds(start, tile)] = (
            scaled * up * (1.0 + gate * (1.0 - sigmoid_gate))
        ).astype(jnp.bfloat16)
        out_ref[:, pl.ds(pl.multiple_of(width + step * tile, tile), tile)] = (
            scaled * gate
        ).astype(jnp.bfloat16)

    @pl.when(step >= steps)
    def _():
        result = contract_cols(out_ref[...], matrix_ref[...])
        size = part_refs[0].shape[0]
        for i, part_ref in enumerate(part_refs):
            part_ref[...] = result[i * size : (i + 1) * size].astype(part_ref.dtype)


def gate_up_gradient(table, pieces, down, gate, up, matrix, parts):
    count, width = gate.shape
    tile = tile_of(width, 256)
    steps = width // tile
    out_width = matrix.shape[0]
    out_tile = tile_of(out_width, 512)
    first = lambda i: jnp.minimum(i, steps - 1)
    later = lambda i: jnp.maximum(i - steps, 0)
    part = pl.BlockSpec((count, tile), lambda i, table: (0, first(i)))
    grads, *products = row_call(
        lambda *refs: gate_grad_kernel(len(pieces), steps, *refs),
        "gate_up_grad",
        table,
        (steps + out_width // out_tile,),
        [piece.array for piece in pieces] + [down, gate, up, matrix],
        [piece.spec() for piece in pieces]
        + [
            pl.BlockSpec((tile, down.shape[1]), lambda i, table: (first(i), 0)),
            part,
            part,
            pl.BlockSpec((out_tile, 2 * width), lambda i, table: (later(i), 0)),
        ],
        [jax.ShapeDtypeStruct((count, 2 * width), jnp.bfloat16)]
        + [jax.ShapeDtypeStruct((count // parts, out_width), jnp.bfloat16)] * parts,
        [pl.BlockSpec((count, 2 * width), lambda i, table: (0, 0))]
        + [pl.BlockSpec((count // parts, out_tile), lambda i, table: (0, later(i)))] * parts,
    )
    return grads, products if parts > 1 else products[0]


def rows_kernel(count, weighed, *refs):
    out_ref = refs[2 * count + 1 + weighed]
    result = sum(contract_rows(refs[1 + i][...], refs[1 + count + i][...]) for i in range(count))
    out_ref[...] = result.astype(out_ref.dtype)
    if weighed:
        by_column = jnp.transpose(result * refs[2 * count + 1][...].astype(jnp.float32))
        refs[-1][...] = jnp.sum(by_column, axis=0, keepdims=True)


def weight_gradient(table, lefts, rights, weights=None):
    width, columns = lefts[0].array.shape[1], rights[0].columns
    tile = tile_of(width, 256)
    weighed = weights is not None
    block_spec = pl.BlockSpec((tile, columns), lambda i, table: (i, 0))
    result = row_call(
        lambda *refs: rows_kernel(len(lefts), weighed, *refs),
        "weight_grad",
        table,
        (width // tile,),
        [piece.array for piece in lefts + rights] + ([weights] if weighed else []),
        [piece.spec(tile) for piece in lefts]
        + [piece.spec() for piece in rights]
        + ([block_spec] if weighed else []),
        [jax.ShapeDtypeStruct((width, columns), jnp.bfloat16)]
        + ([jax.ShapeDtypeStruct((1, width), jnp.float32)] if weighed else []),
        [block_spec] + ([pl.BlockSpec((1, tile), lambda i, table: (0, i))] if weighed else []),
    )
    return result if weighed else result[0]


def split_groups(groups, half, side=0, sides=1):
    return [
        Piece(array, half, i, side=side, sides=sides)
        for array in groups
        for i in range(array.shape[0] // half)
    ]


def arrived_sum(split, low_refs, high_refs):
    low = sum(ref[...].astype(jnp.float32) for ref in low_refs)
    high = sum(ref[...].astype(jnp.float32) for ref in high_refs)
    return jnp.where(pl.program_id(0) < split, low, high)


def half_specs(tile, split, width):
    return (
        pl.BlockSpec((tile, width), lambda i: (jnp.minimum(i, split - 1), 0)),
        pl.BlockSpec((tile, width), lambda i: (jnp.maximum(i - split, 0), 0)),
    )


def put_half(split, low_ref, high_ref, value):
    @pl.when(pl.program_id(0) < split)
    def _():
        low_ref[...] = value

    @pl.when(pl.program_id(0) >= split)
    def _():
        high_ref[...] = value


def row_kernel_call(kernel, name, whole, lows, highs, gain, outs):
    rows, width = whole[0].shape
    tile = min(rows // 2, 128)
    split = rows // 2 // tile
    spec = pl.BlockSpec((tile, width), lambda i: (i, 0))
    low_spec, high_spec = half_specs(tile, split, width)
    row_spec = pl.BlockSpec((1, width), lambda i: (0, 0))
    shapes, specs = [], []
    for out in outs:
        if out == "halves":
            shapes += [jax.ShapeDtypeStruct((rows // 2, width), jnp.bfloat16)] * 2
            specs += [low_spec, high_spec]
        elif out == "row":
            shapes.append(jax.ShapeDtypeStruct((1, width), jnp.float32))
            specs.append(row_spec)
        else:
            shapes.append(jax.ShapeDtypeStruct((rows, width), out))
            specs.append(spec)
    return pl.pallas_call(
        lambda *refs: kernel(split, len(lows), *refs),
        grid=(2 * split,),
        in_specs=[spec] * len(whole)
        + [low_spec] * len(lows)
        + [high_spec] * len(highs)
        + [row_spec],
        out_specs=specs,
        out_shape=shapes,
        compiler_params=kernel_params(),
        cost_estimate=SMALL_COST,
        name=name,
    )(*whole, *lows, *highs, gain)


def add_norm_kernel(split, count, base_ref, own_ref, *refs):
    gain_ref, sum_ref, low_ref, high_ref = refs[2 * count :]
    values = base_ref[...].astype(jnp.float32) + own_ref[...].astype(jnp.float32)
    values = values + arrived_sum(split, refs[:count], refs[count : 2 * count])
    sum_ref[...] = values.astype(sum_ref.dtype)
    put_half(split, low_ref, high_ref, rms_gain(values, gain_ref[...]).astype(jnp.bfloat16))


def add_and_norm(base, own, lows, highs, gain):
    outs = (jnp.bfloat16, "halves")
    return row_kernel_call(add_norm_kernel, "add_norm", [base, own], lows, highs, gain, outs)


def add_kernel(split, count, base_ref, own_ref, *refs):
    values = base_ref[...].astype(jnp.float32) + own_ref[...].astype(jnp.float32)
    values = values + arrived_sum(split, refs[:count], refs[count : 2 * count])
    refs[-1][...] = values.astype(jnp.bfloat16)


def norm_gradient_kernel(split, count, base_ref, value_ref, own_ref, *refs):
    gain_ref, outs = refs[2 * count], refs[2 * count + 1 :]
    grad = own_ref[...].astype(jnp.float32)
    grad = grad + arrived_sum(split, refs[:count], refs[count : 2 * count])
    values = value_ref[...].astype(jnp.float32)
    scale = lax.rsqrt(jnp.mean(values * values, axis=1, keepdims=True) + norm_eps)
    unit = values * scale
    inner = grad * gain_ref[...]
    result = base_ref[...].astype(jnp.float32) + scale * (
        inner - unit * jnp.mean(inner * unit, axis=1, keepdims=True)
    )
    if len(outs) == 1:
        outs[0][...] = result.astype(jnp.bfloat16)
        return
    low_ref, high_ref, whole_ref, gain_out = outs
    whole_ref[...] = result.astype(jnp.bfloat16)
    put_half(split, low_ref, high_ref, result.astype(jnp.bfloat16))

    @pl.when(pl.program_id(0) == 0)
    def _():
        gain_out[...] = jnp.zeros_like(gain_out)

    gain_out[...] += jnp.sum(grad * unit, axis=0, keepdims=True)


def norm_gradient(base, values, own, lows, highs, gain, outs):
    return row_kernel_call(
        norm_gradient_kernel, "norm_gradient", [base, values, own], lows, highs, gain, outs
    )


def project_kernel(count, *refs):
    rows = stacked(refs[1 : 1 + count])
    matrix_ref, gain_ref, cos_ref, sin_ref = refs[1 + count : 5 + count]
    query_ref, key_ref, value_ref, query_raw, key_raw = refs[-5:]
    width = HEAD_WIDTH
    mixed = product(rows, matrix_ref[...])
    cos, sin = cos_ref[...], sin_ref[...]
    for part in range(QUERY_PER_KEY + 1):
        values = mixed[:, part * width : (part + 1) * width]
        is_key = part == QUERY_PER_KEY
        gain = gain_ref[1:2, :] if is_key else gain_ref[0:1, :]
        scale = lax.rsqrt(jnp.mean(values * values, axis=1, keepdims=True) + norm_eps)
        scaled = values * scale * gain
        turned = scaled * cos + pltpu.roll(scaled, width // 2, 1) * sin
        if is_key:
            key_ref[...] = turned.astype(jnp.bfloat16)
            key_raw[...] = values
        else:
            query_ref[:, part * width : (part + 1) * width] = turned.astype(jnp.bfloat16)
            query_raw[:, part * width : (part + 1) * width] = values
    value_ref[...] = mixed[:, (QUERY_PER_KEY + 1) * width :].astype(jnp.bfloat16)


def project(blocks, matrix, gains, cos, sin, place, total_rows, before):
    count, depth = sum(block.shape[0] for block in blocks), matrix.shape[0]
    block = (QUERY_PER_KEY + 2) * HEAD_WIDTH
    heads = matrix.shape[1] // block
    wide = QUERY_PER_KEY * HEAD_WIDTH
    per_table = cos.shape[0] // count
    table_spec = pl.BlockSpec(
        (count, HEAD_WIDTH), lambda h, at: (lax.rem(at[0], per_table), 0)
    )
    widths = (wide, HEAD_WIDTH, HEAD_WIDTH, wide, HEAD_WIDTH)
    kinds = (jnp.bfloat16,) * 3 + (jnp.float32,) * 2
    kept = () if before is None else tuple(before)
    return pl.pallas_call(
        lambda *refs: project_kernel(len(blocks), *refs),
        grid_spec=pltpu.PrefetchScalarGridSpec(
            num_scalar_prefetch=1,
            grid=(heads,),
            in_specs=[
                pl.BlockSpec((rows.shape[0], depth), lambda h, at: (0, 0)) for rows in blocks
            ]
            + [
                pl.BlockSpec((depth, block), lambda h, at: (0, h)),
                pl.BlockSpec((2, HEAD_WIDTH), lambda h, at: (0, 0)),
                table_spec,
                table_spec,
            ]
            + [pl.BlockSpec(memory_space=pltpu.HBM)] * len(kept),
            out_specs=[pl.BlockSpec((count, w), lambda h, at: (at[0], h)) for w in widths],
        ),
        out_shape=[
            jax.ShapeDtypeStruct((total_rows, heads * w), kind) for w, kind in zip(widths, kinds)
        ],
        input_output_aliases={5 + len(blocks) + i: i for i in range(len(kept))},
        compiler_params=kernel_params(56),
        cost_estimate=SMALL_COST,
        name="project",
    )(place.reshape(1), *blocks, matrix, gains, cos, sin, *kept)


def causal(keys, queries):
    rows = lax.broadcasted_iota(jnp.int32, (keys, queries), 0)
    return rows <= lax.broadcasted_iota(jnp.int32, (keys, queries), 1)


def add_after(whole, part, low):
    if low == 0:
        return whole + part
    return jnp.concatenate([whole[:, :low], whole[:, low:] + part], axis=1)


def walk(visit, step, block, carry, pieces):
    carry = lax.fori_loop(
        0,
        step,
        lambda j, c: visit(pl.multiple_of(j * block, block), c, block, 0, False),
        carry,
    )
    start = pl.multiple_of(step * block, block)
    count = block // pieces
    for low in range(0, block, count):
        carry = visit(start + low, carry, count, low, True)
    return carry


def attend_kernel(scale, query_ref, key_ref, value_ref, out_ref, log_ref):
    block = query_ref.shape[0]
    width = key_ref.shape[1]
    group = query_ref.shape[1] // width
    step = pl.program_id(2)
    queries = [query_ref[:, g * width : (g + 1) * width] for g in range(group)]

    def visit(start, carry, count, low, masked):
        keys = key_ref[pl.ds(start, count), :]
        values = value_ref[pl.ds(start, count), :]
        new = []
        for g in range(group):
            total, acc = carry[g]
            weights = jnp.exp2(contract_cols(keys, queries[g][low:]) * (scale * log2_e))
            if masked:
                weights = jnp.where(causal(count, block - low), weights, 0.0)
            total = add_after(total, jnp.sum(weights, axis=0, keepdims=True), low)
            acc = add_after(acc, contract_rows(values, weights.astype(jnp.bfloat16)), low)
            new.append((total, acc))
        return tuple(new)

    carry = tuple(
        (jnp.zeros((1, block), jnp.float32), jnp.zeros((width, block), jnp.float32))
        for _ in range(group)
    )
    carry = walk(visit, step, block, carry, 1)
    for g in range(group):
        total, acc = carry[g]
        out_ref[:, g * width : (g + 1) * width] = jnp.transpose(acc / total).astype(jnp.bfloat16)
        log_ref[0, 0, g : g + 1, :] = jnp.log2(total)


def attention_forward(query, key, value, block):
    rows = query.shape[0]
    heads = key.shape[1] // HEAD_WIDTH
    steps = SEQUENCE_TOKENS // block
    wide = QUERY_PER_KEY * HEAD_WIDTH
    sequences = rows // SEQUENCE_TOKENS
    query_spec = pl.BlockSpec((block, wide), lambda h, s, i: (s * steps + i, h))
    key_spec = pl.BlockSpec((SEQUENCE_TOKENS, HEAD_WIDTH), lambda h, s, i: (s, h))
    return pl.pallas_call(
        lambda *refs: attend_kernel(HEAD_WIDTH ** (-0.5), *refs),
        grid=(heads, sequences, steps),
        in_specs=[query_spec, key_spec, key_spec],
        out_specs=[
            query_spec,
            pl.BlockSpec(
                (1, 1, QUERY_PER_KEY, block), lambda h, s, i: (h, s * steps + i, 0, 0)
            ),
        ],
        out_shape=[
            jax.ShapeDtypeStruct(query.shape, jnp.bfloat16),
            jax.ShapeDtypeStruct((heads, rows // block, QUERY_PER_KEY, block), jnp.float32),
        ],
        compiler_params=kernel_params(56),
        cost_estimate=SMALL_COST,
        name="attend",
    )(query, key, value)


def norm_back(values, grad, gain, cos, sin):
    width = values.shape[1]
    turned = grad * cos + pltpu.roll(grad * sin, width // 2, 1)
    scale = lax.rsqrt(jnp.mean(values * values, axis=1, keepdims=True) + norm_eps)
    unit = values * scale
    inner = turned * gain
    back = scale * (inner - unit * jnp.mean(inner * unit, axis=1, keepdims=True))
    return back.astype(jnp.bfloat16), jnp.sum(turned * unit, axis=0, keepdims=True)


def attend_back_kernel(
    scale,
    table_ref,
    query_ref,
    key_ref,
    value_ref,
    grad_ref,
    context_ref,
    log_ref,
    query_raw,
    key_raw,
    gain_ref,
    cos_ref,
    sin_ref,
    *refs,
):
    mixed_out, gain_out, key_sum, value_sum = refs[-4:]
    block = query_ref.shape[0]
    width = key_ref.shape[1]
    group = query_ref.shape[1] // width
    sequence, step = pl.program_id(0), pl.program_id(1)
    @pl.when(step == 0)
    def _():
        key_sum[...] = jnp.zeros_like(key_sum)
        value_sum[...] = jnp.zeros_like(value_sum)

    @pl.when((step == 0) & (sequence == 0))
    def _():
        gain_out[...] = jnp.zeros_like(gain_out)

    queries, grads, logs, dots = [], [], [], []
    for g in range(group):
        cols = slice(g * width, (g + 1) * width)
        queries.append(query_ref[:, cols])
        grads.append(grad_ref[:, cols])
        logs.append(log_ref[0, 0, g : g + 1, :])
        both = grads[g].astype(jnp.float32) * context_ref[:, cols].astype(jnp.float32)
        dots.append(jnp.sum(jnp.transpose(both), axis=0, keepdims=True))

    def visit(start, carry, count, low, masked):
        rows = pl.ds(start, count)
        keys = key_ref[rows, :]
        values = value_ref[rows, :]
        new = []
        key_part = value_part = None
        for g in range(group):
            seen, sought = queries[g][low:], grads[g][low:]
            weights = jnp.exp2(contract_cols(keys, seen) * (scale * log2_e) - logs[g][:, low:])
            if masked:
                weights = jnp.where(causal(count, block - low), weights, 0.0)
            slope = contract_cols(values, sought)
            score = (weights * (slope - dots[g][:, low:])).astype(jnp.bfloat16)
            value_g = product(weights.astype(jnp.bfloat16), sought)
            key_g = product(score, seen)
            key_part = key_g if key_part is None else key_part + key_g
            value_part = value_g if value_part is None else value_part + value_g
            new.append(add_after(carry[g], contract_rows(keys, score), low))
        key_sum[rows, :] += key_part
        value_sum[rows, :] += value_part
        return tuple(new)

    carry = tuple(jnp.zeros((width, block), jnp.float32) for _ in range(group))
    carry = walk(visit, step, block, carry, 2)
    rows = pl.ds(pl.multiple_of(step * block, block), block)
    cos, sin = cos_ref[rows, :], sin_ref[rows, :]
    for g in range(group):
        cols = slice(g * width, (g + 1) * width)
        back, gain = norm_back(
            query_raw[:, cols], jnp.transpose(carry[g]) * scale, gain_ref[0:1, :], cos, sin
        )
        mixed_out[rows, cols] = back
        gain_out[0:1, :] += gain

    @pl.when(step == pl.num_programs(1) - 1)
    def _():
        def finish(j, _):
            rows = pl.ds(pl.multiple_of(j * block, block), block)
            back, gain = norm_back(
                key_raw[rows, :],
                key_sum[rows, :] * scale,
                gain_ref[1:2, :],
                cos_ref[rows, :],
                sin_ref[rows, :],
            )
            mixed_out[rows, group * width : (group + 1) * width] = back
            mixed_out[rows, (group + 1) * width :] = value_sum[rows, :].astype(jnp.bfloat16)
            gain_out[1:2, :] += gain
            return 0

        lax.fori_loop(0, pl.num_programs(1), finish, 0)


def attention_backward(
    slots, query, key, value, grad, context, logs, query_raw, key_raw, gains, cos, sin, head, before
):
    rows = query.shape[0]
    block = logs.shape[-1]
    steps = SEQUENCE_TOKENS // block
    wide = QUERY_PER_KEY * HEAD_WIDTH
    heads = key.shape[1] // HEAD_WIDTH
    sequences = rows // SEQUENCE_TOKENS
    mixed = (QUERY_PER_KEY + 2) * HEAD_WIDTH
    query_spec = pl.BlockSpec((block, wide), lambda s, i, slots: (s * steps + i, head))
    key_spec = pl.BlockSpec((SEQUENCE_TOKENS, HEAD_WIDTH), lambda s, i, slots: (s, head))
    table_spec = pl.BlockSpec((SEQUENCE_TOKENS, HEAD_WIDTH), lambda s, i, slots: (0, 0))
    gain_spec = pl.BlockSpec((2, HEAD_WIDTH), lambda s, i, slots: (0, 0))
    kept = () if before is None else (before,)
    return pl.pallas_call(
        lambda *refs: attend_back_kernel(HEAD_WIDTH ** (-0.5), *refs),
        grid_spec=pltpu.PrefetchScalarGridSpec(
            num_scalar_prefetch=1,
            grid=(sequences, steps),
            in_specs=[
            query_spec,
            key_spec,
            key_spec,
            pl.BlockSpec((block, wide), lambda s, i, slots: (slots[s * steps + i], head)),
            query_spec,
            pl.BlockSpec(
                (1, 1, QUERY_PER_KEY, block), lambda s, i, slots: (head, s * steps + i, 0, 0)
            ),
            query_spec,
            key_spec,
            gain_spec,
            table_spec,
            table_spec,
        ]
        + [pl.BlockSpec(memory_space=pltpu.HBM)] * len(kept),
        out_specs=[
            pl.BlockSpec((SEQUENCE_TOKENS, mixed), lambda s, i, slots: (s, head)),
            gain_spec,
        ],
        scratch_shapes=[pltpu.VMEM((SEQUENCE_TOKENS, HEAD_WIDTH), jnp.float32)] * 2,
        ),
        out_shape=[
            jax.ShapeDtypeStruct((rows, heads * mixed), jnp.bfloat16),
            jax.ShapeDtypeStruct((2, HEAD_WIDTH), jnp.float32),
        ],
        input_output_aliases={12: 0} if kept else {},
        compiler_params=kernel_params(56),
        cost_estimate=SMALL_COST,
        name="attend_back",
    )(slots, query, key, value, grad, context, logs, query_raw, key_raw, gains, cos, sin, *kept)


def local(
    inputs,
    input_projection_weight,
    input_first_moment,
    input_second_moment,
    out_weight,
    out_mean,
    out_square,
    swiglu_weight,
    swiglu_mean,
    swiglu_square,
    down_weight,
    down_mean,
    down_square,
    norm_gains,
    norm_mean,
    norm_square,
    qknorm_gains,
    qknorm_mean,
    qknorm_square,
    cotangent,
):
    size = lax.axis_size("tensor")
    rows = inputs.shape[0]
    half = rows // 2
    group_rows = rows * size
    last = size // 2
    dp_rows = input_projection_weight.shape[0]
    local_kv = input_projection_weight.shape[1]
    local_ff = swiglu_weight.shape[2]
    me = ring_place(lax.axis_index("tensor"), size)
    places = [ring_place((me + d + size) % size, size) for d in ring_offsets(size)]
    group_places = [places[:1]]
    for step in range(1, last):
        group_places.append(places[2 * step - 1 : 2 * step + 1])
    group_places.append(places[-1:])
    halves = [2 * place + i for place in places for i in range(2)]
    table = jnp.stack(places + halves).astype(jnp.int32)
    away = (ring_place(jnp.arange(size, dtype=jnp.int32), size) - me + size) % size
    slots = jnp.where(
        away == 0,
        size - 2,
        jnp.where(
            away == last,
            size - 1,
            jnp.where(away < last, 2 * away - 2, 2 * (size - away) - 1),
        ),
    ).astype(jnp.int32)
    order = Order()
    turn, mark = order.turn, order.mark
    tie = lax.optimization_barrier

    def ordered(array, group):
        entries = [0] if group == 0 else [2 * group - 1, 2 * group]
        if group == last:
            entries = [size - 1]
        return [Piece(array, rows, entry=entry) for entry in entries]

    def ordered_finely(array):
        return [Piece(array, half, entry=size + i) for i in range(2 * size)]

    def flat(groups):
        return pieces_of([block for group in groups for block in group])

    def parts_of(group):
        return 1 if group == 0 else 2 if group == last else 4

    def marked(part):
        return mark(*part) if isinstance(part, (list, tuple)) else mark(part)

    in_low = input_projection_weight.astype(jnp.bfloat16).reshape(dp_rows, -1)
    out_low = out_weight.astype(jnp.bfloat16)
    swiglu_low = swiglu_weight.astype(jnp.bfloat16).reshape(dp_rows, 2 * local_ff)
    down_low = down_weight.astype(jnp.bfloat16)
    in_matrix = lax.all_gather(in_low, "dp", axis=0, tiled=True)
    out_full = lax.all_gather(out_low, "dp", axis=1, tiled=True)
    swiglu_matrix = lax.all_gather(swiglu_low, "dp", axis=0, tiled=True)
    down_full = lax.all_gather(down_low, "dp", axis=1, tiled=True)

    normed_f = rms_gain(inputs.astype(jnp.float32), norm_gains[0])
    cos, sin = rotary_tables(SEQUENCE_TOKENS, HEAD_WIDTH)
    projected = []

    def project_group(group, blocks):
        calls = [blocks] if group in (0, last) else [blocks[:2], blocks[2:]]
        for place, call in zip(group_places[group], calls):
            call[0] = turn(call[0])
            projected[:] = mark(
                *project(
                    call, in_matrix, qknorm_gains, cos, sin, place, group_rows, projected or None
                )
            )

    normed = normed_f.astype(jnp.bfloat16)
    normed_groups = ring_gather(
        (normed[:half], normed[half:]), size, project_group, order, hold=(in_matrix,)
    )
    query, key, value, query_raw, key_raw = projected
    cotangent_sent = tie((cotangent, *normed_groups[-1]))[0]

    context, logs = mark(*attention_forward(query, key, value, rows))
    cot_groups, cot_carried = ring_near(
        (cotangent_sent[:half], cotangent_sent[half:]), size, lambda group, blocks: None, Order()
    )

    def out_group(group):
        return marked(
            block_product(
                table, ordered(turn(context), group), out_full, False, parts_of(group)
            )
        )

    own, lows, highs = ring_scatter(
        size, out_group, order, first=[half for group in cot_groups[1:] for half in group]
    )
    lows, highs = tie((lows, highs, swiglu_matrix))[:2]
    hidden, *two_halves = mark(*add_and_norm(inputs, own, lows, highs, norm_gains[1:2]))

    gate_groups = []
    grads = [None] * (last + 1)

    def gate_group(group, blocks):
        blocks[0] = turn(blocks[0])
        gate_groups.append(mark(*gate_up_product(table, pieces_of(blocks), swiglu_matrix)))

    two_groups, two_carried = ring_near(two_halves, size, gate_group, order)
    two_groups = ring_far(two_groups, two_carried, size, gate_group, order)
    cot_carried = tie((*cot_carried, *gate_groups[last - 1]))[:2]
    cot_groups = ring_far(cot_groups, cot_carried, size, lambda group, blocks: None, order)
    activated = [parts[0] for parts in gate_groups]
    two_parts = [None] * (last + 1)

    def two_part(group):
        cots = [turn(cot_groups[group][0])] + cot_groups[group][1:]
        grads[group], part = gate_up_gradient(
            table,
            pieces_of(cots),
            down_full,
            *gate_groups[group][1:],
            swiglu_matrix,
            parts_of(group),
        )
        two_parts[group] = marked(part)

    for group in range(1, last):
        two_part(group)
    lefts = split_groups([turn(activated[0])] + activated[1:], half)
    down_part = mark(weight_gradient(table, lefts, flat(cot_groups)))
    down_grad = lax.psum_scatter(down_part, "dp", scatter_dimension=1, tiled=True)
    two_part(last)
    more = []

    def own_part():
        two_part(0)

    def swiglu_gradient():
        twos = flat(two_groups)
        twos[0].array = turn(twos[0].array)
        side = len(more)
        more.append(mark(weight_gradient(table, twos, split_groups(grads, half, side, 2))))

    if last == 1:
        own_part()
    own, lows, highs = ring_scatter(
        size, lambda group: two_parts[group], order, between=own_part, after=swiglu_gradient
    )
    swiglu_part, lows, highs = tie((more[0], lows, highs))
    gate_weight_grad = lax.psum_scatter(swiglu_part, "dp", scatter_dimension=0, tiled=True)
    *attended_halves, hidden_grad, mlp_gain_grad = mark(
        *norm_gradient(
            cotangent, hidden, own, lows, highs, norm_gains[1:2], ("halves", jnp.bfloat16, "row")
        )
    )

    context_grad, down_parts, new_down, head_grads = [None], [None] * (last + 1), [], []

    def context_group(group, blocks):
        blocks[0] = turn(blocks[0])
        index = size - 2 if group == 0 else size - 1 if group == last else group - 1
        context_grad[0] = mark(
            block_product(
                table, pieces_of(blocks), out_full, True, into=(group_rows, index, context_grad[0])
            )
        )
        if group == 0:
            for other in range(last, -1, -1):
                down_parts[other] = marked(
                    block_product(
                        table, [Piece(turn(activated[other]))], down_full, False, parts_of(other)
                    )
                )
            new_down[:] = mark(
                turn(down_grad).astype(jnp.float32),
                *adamw(
                    down_weight,
                    turn(down_grad).astype(jnp.float32),
                    down_mean,
                    down_square,
                    FF ** (-0.5),
                ),
            )
        if group == last - 1:
            swiglu_gradient()

    attended_groups = ring_gather(attended_halves, size, context_group, order)
    swiglu_part = tie((more[1], *attended_groups[last]))[0]
    up_weight_grad = lax.psum_scatter(swiglu_part, "dp", scatter_dimension=0, tiled=True)

    def head_backward(head):
        head_grads.append(
            mark(
                *attention_backward(
                    slots, turn(query), key, value, context_grad[0], context, logs, query_raw,
                    key_raw, qknorm_gains, cos, sin, head,
                    head_grads[-1][0] if head_grads else None,
                )
            )
        )

    out_part = mark(
        weight_gradient(table, ordered_finely(turn(context)), flat(attended_groups))
    )
    if last == 1:
        head_backward(0)

    def other_heads():
        for head in range(1, local_kv):
            head_backward(head)

    own, lows, highs = ring_scatter(
        size,
        lambda group: down_parts[group],
        order,
        hold=attended_groups[-1],
        between=lambda: head_backward(0),
        after=other_heads,
    )
    sent, outputs = (own, lows, highs), []
    mixed_grad = head_grads[-1][0]
    qknorm_part = sum(pair[1] for pair in head_grads)
    in_parts = []

    def normed_group(group):
        return marked(
            block_product(
                table, ordered(turn(mixed_grad), group), in_matrix, True, parts_of(group)
            )
        )

    def in_gradient():
        normeds = flat(normed_groups)
        normeds[0].array = turn(normeds[0].array)
        in_parts[:] = mark(
            *weight_gradient(table, normeds, ordered_finely(mixed_grad), in_matrix)
        )

    def add_outputs():
        own, lows, highs = sent
        whole = [hidden, turn(own)]
        (result,) = row_kernel_call(
            add_kernel, "add", whole, lows, highs, norm_gains[0:1], (jnp.bfloat16,)
        )
        outputs.append(mark(result))

    got = []
    came = []
    own, lows, highs = ring_scatter(
        size,
        normed_group,
        order,
        between=in_gradient,
        after=add_outputs,
        got=got,
        came=came,
        eager=False,
    )
    if not in_parts:
        in_gradient()
    rows_of_gains = jnp.concatenate([in_parts[1] / norm_gains[0:1], mlp_gain_grad], axis=0)
    gain_sums = jnp.concatenate([rows_of_gains, qknorm_part], axis=1)
    (outputs,) = outputs
    out_part, gate_weight_grad = tie((out_part, gate_weight_grad, sent, mixed_grad))[:2]
    out_grad = lax.psum_scatter(out_part, "dp", scatter_dimension=1, tiled=True)
    in_part, up_weight_grad = tie((in_parts[0], up_weight_grad, *came))[:2]
    in_grad = lax.psum_scatter(in_part, "dp", scatter_dimension=0, tiled=True)
    out_grad, gate_weight_grad = tie((out_grad, gate_weight_grad, *got))[:2]
    out_grad = out_grad.astype(jnp.float32)
    out_new, out_second = adamw(
        out_weight, out_grad, out_mean, out_square, (HQ * HEAD_WIDTH / 8.0) ** (-0.5)
    )
    swiglu_grad, swiglu_new, swiglu_second = adamw_parts(
        swiglu_weight,
        (gate_weight_grad, up_weight_grad),
        swiglu_mean,
        swiglu_square,
        MODEL_WIDTH ** (-0.5),
    )
    down_grad, down_new, down_second = new_down
    (
        lows,
        highs,
        own,
        outputs,
        out_grad,
        out_new,
        out_second,
        swiglu_grad,
        swiglu_new,
        swiglu_second,
    ) = tie(
        (
            lows,
            highs,
            own,
            outputs,
            out_grad,
            out_new,
            out_second,
            swiglu_grad,
            swiglu_new,
            swiglu_second,
        )
    )
    (input_grad,) = norm_gradient(
        hidden_grad, inputs, own, lows, highs, norm_gains[0:1], (jnp.bfloat16,)
    )
    in_grad, in_new, in_second = adamw_parts(
        input_projection_weight,
        (in_grad,),
        input_first_moment,
        input_second_moment,
        MODEL_WIDTH ** (-0.5),
    )
    gain_sums = sum_over(tie((gain_sums, *lows, *highs))[0], "tensor", (input_grad,))
    gain_sums = sum_over(gain_sums, "dp", (in_new,))
    norm_grad, qknorm_grad = gain_sums[:, :MODEL_WIDTH], gain_sums[:, MODEL_WIDTH:]
    norm_new, norm_second = adamw(norm_gains, norm_grad, norm_mean, norm_square, gain_rate)
    qknorm_new, qknorm_second = adamw(
        qknorm_gains, qknorm_grad, qknorm_mean, qknorm_square, gain_rate
    )
    return (
        outputs,
        input_grad,
        in_grad,
        in_new,
        in_second,
        out_grad,
        out_new,
        out_second,
        swiglu_grad,
        swiglu_new,
        swiglu_second,
        down_grad,
        down_new,
        down_second,
        norm_grad,
        norm_new,
        norm_second,
        qknorm_grad,
        qknorm_new,
        qknorm_second,
    )


def solution(mesh):
    return jax.shard_map(
        local,
        mesh=mesh,
        in_specs=(
            P(("dp", "tensor"), None),
            P("dp", "tensor", None),
            P("dp", "tensor", None),
            P("dp", "tensor", None),
            P("tensor", "dp"),
            P("tensor", "dp"),
            P("tensor", "dp"),
            P("dp", None, "tensor"),
            P("dp", None, "tensor"),
            P("dp", None, "tensor"),
            P("tensor", "dp"),
            P("tensor", "dp"),
            P("tensor", "dp"),
            P(),
            P(),
            P(),
            P(),
            P(),
            P(),
            P(("dp", "tensor"), None),
        ),
        out_specs=(
            P(("dp", "tensor"), None),
            P(("dp", "tensor"), None),
            P("dp", "tensor", None),
            P("dp", "tensor", None),
            P("dp", "tensor", None),
            P("tensor", "dp"),
            P("tensor", "dp"),
            P("tensor", "dp"),
            P("dp", None, "tensor"),
            P("dp", None, "tensor"),
            P("dp", None, "tensor"),
            P("tensor", "dp"),
            P("tensor", "dp"),
            P("tensor", "dp"),
            P(),
            P(),
            P(),
            P(),
            P(),
            P(),
        ),
        check_vma=False,
    )
```
